32 devices in a mesh: dp: 4 (over y, core), seq: 8 (over z, x).
Axes of the slice: x: 2, y: 2, z: 4, core: 2. Of those that a mesh axis runs over, the one named last changes fastest.
Arguments:
- inputs: bfloat16 [4, 16384, 768], P('dp', 'seq'), may hold values from -6 to 6
- w_in: bfloat16 [768, 3352], P('seq'), may hold values from -0.21875 to 0.21875
- w_out: bfloat16 [1536, 768], P('seq'), may hold values from -0.15625 to 0.15625
- norm_gain: float32 [768], replicated, may hold values from 0.5 to 1.5
- conv_weight: float32 [4, 1792], replicated, may hold values from -3 to 3
- conv_bias: float32 [1792], replicated, may hold values from -3 to 3
- dt_bias: float32 [24], replicated, may hold values from -6 to -1
- a_log: float32 [24], replicated, may hold values from -4 to 2
- skip: float32 [24], replicated, may hold values from 0.5 to 1.5
- gate_gain: float32 [1536], replicated, may hold values from 0.5 to 1.5
- cotangent: bfloat16 [4, 16384, 768], P('dp', 'seq'), may hold values from -6 to 6
Outputs:
- mixed: bfloat16 [4, 16384, 768], P('dp', 'seq')
- grad_inputs: float32 [4, 16384, 768], P('dp', 'seq')
- grad_w_in: float32 [768, 3352], P('seq')
- grad_w_out: float32 [1536, 768], P('seq')
- grad_norm_gain: float32 [768], replicated
- grad_conv_weight: float32 [4, 1792], replicated
- grad_conv_bias: float32 [1792], replicated
- grad_dt_bias: float32 [24], replicated
- grad_a_log: float32 [24], replicated
- grad_skip: float32 [24], replicated
- grad_gate_gain: float32 [1536], replicated
The draws below stay inside these ranges and needn't reach their ends.
All inputs are finite; a program needn't handle non-finite values.
Results may differ from the reference program's by a relative error of at most 0.012.
The reference program's roundings to bfloat16 on the way count: a program that leaves them out, or rounds other values in their place, can miss the bound.
Values may be sent and summed in bfloat16 or wider, within the bound.
No kernel may reach another device: no remote copies, remote signals or barrier semaphores. Data moves between devices by JAX's collectives and lax.ppermute only.
A program may use at most 384 MiB of HBM per device.

```python
from functools import partial
import jax
import jax.numpy as jnp
from jax import lax

D = 768
INNER = 1536
HEADS = 24
HEADDIM = 64
STATE = 128
CONV = 4
SPAN = 256
LEN = 16384
BATCH = 4
PROJ = 3352


def levels(stream_key, shape, cuts, low, top_value):
    def one(dim, shards_of):
        heights = jax.random.uniform(jax.random.fold_in(jax.random.fold_in(stream_key, 6), dim), (shards_of,), jnp.float32, low / len(cuts), top_value / len(cuts))
        return jnp.repeat(jnp.exp(heights), shape[dim] // shards_of).reshape((-1,) + (1,) * (len(shape) - dim - 1))

    factor_of = one(*cuts[0])
    for cut in cuts[1:]:
        factor_of = factor_of * one(*cut)
    return factor_of


def noise(stream_key, extent, deviation, most, split=(), kind=jnp.bfloat16):
    factor_of = levels(stream_key, extent, split, -0.22, 0.18) if split else 1.0
    values = jax.random.normal(stream_key, extent, jnp.float32) * deviation * factor_of
    return jnp.minimum(jnp.maximum(values, -most), most).astype(kind)


def setup_inputs(seed: int = 0) -> dict:
    seeds = jax.random.split(jax.random.key(seed), 12)
    return {
        "inputs": noise(seeds[0], (BATCH, LEN, D), 1.0, 6.0, ((0, 4), (1, 8))),
        "w_in": noise(seeds[1], (D, PROJ), D ** -0.5, 0.21875, ((0, 8),)),
        "w_out": noise(seeds[2], (INNER, D), INNER ** -0.5, 0.15625, ((0, 8),)),
        "norm_gain": jnp.clip(1.0 + 0.1 * jax.random.normal(seeds[3], (D,), jnp.float32), 0.5, 1.5),
        "conv_weight": noise(seeds[4], (CONV, INNER + 2 * STATE), CONV ** -0.5, 3.0, (), jnp.float32),
        "conv_bias": noise(seeds[5], (INNER + 2 * STATE,), 0.5, 3.0, (), jnp.float32),
        "dt_bias": jnp.clip(jax.random.uniform(seeds[6], (HEADS,), jnp.float32, -6.0, -1.0), -6.0, -1.0),
        "a_log": jnp.clip(jax.random.uniform(seeds[7], (HEADS,), jnp.float32, -4.0, 2.0), -4.0, 2.0),
        "skip": jnp.clip(jax.random.uniform(seeds[8], (HEADS,), jnp.float32, 0.5, 1.5), 0.5, 1.5),
        "gate_gain": jnp.clip(1.0 + 0.1 * jax.random.normal(seeds[9], (INNER,), jnp.float32), 0.5, 1.5),
        "cotangent": noise(seeds[10], (BATCH, LEN, D), 1.0, 6.0, ((0, 4), (1, 8))),
    }


EPS = 1e-05
HIGH = lax.Precision.HIGHEST

@jax.custom_vjp
def low(v):
    return lax.optimization_barrier(v.astype(jnp.bfloat16)).astype(jnp.float32)

@jax.custom_vjp
def low_back(v):
    return v

def low_keep(v):
    return (low(v), None)

def low_pass(kept, grad):
    return (grad,)

def back_keep(v):
    return (v, None)

def back_low(kept, grad):
    return (low(grad),)
low.defvjp(low_keep, low_pass)
low_back.defvjp(back_keep, back_low)

def product(left, right):
    return jnp.dot(left, right, precision=HIGH, preferred_element_type=jnp.float32)

def rms_gain(values, gain):
    return values * lax.rsqrt(lax.optimization_barrier(jnp.mean(values * values, axis=-1, keepdims=True)) + EPS) * gain

def causal_conv(signal, taps, offset):
    width = taps.shape[0]
    padded = jnp.concatenate([jnp.zeros((width - 1, signal.shape[1]), signal.dtype), signal], axis=0)
    total = jnp.broadcast_to(offset[None, :], signal.shape)
    for shift_at in range(width):
        total = total + taps[shift_at][None, :] * padded[shift_at:shift_at + signal.shape[0]]
    return total

def span_step(state, block):
    xs, bmat, cmat, dts, rates = block
    steps = dts * rates[None, :]
    count = steps.shape[0]
    lower = (lax.broadcasted_iota(jnp.int32, (count, count), 0) >= lax.broadcasted_iota(jnp.int32, (count, count), 1)).astype(steps.dtype)
    cums = product(lower, steps)
    heads_cum = cums.T
    diff = heads_cum[:, :, None] - heads_cum[:, None, :]
    decay = jnp.exp(jnp.where(lower[None] > 0, diff, 0.0)) * lower[None]
    scores = product(cmat, bmat.T)
    weights = scores[None] * decay * dts.T[:, None, :]
    intra = jnp.einsum('hts,shp->thp', weights, xs, precision=HIGH)
    inter = jnp.einsum('tn,hpn->thp', cmat, state, precision=HIGH) * jnp.exp(cums)[:, :, None]
    tail = jnp.exp(cums[-1][None, :] - cums) * dts
    new_state = state * jnp.exp(cums[-1])[:, None, None] + jnp.einsum('sh,shp,sn->hpn', tail, xs, bmat, precision=HIGH)
    return (new_state, intra + inter)

def scan_heads(xs, bmat, cmat, dts, rates):
    total = xs.shape[0]
    count = total // SPAN
    heads, width = (xs.shape[1], xs.shape[2])
    blocks = (xs.reshape(count, SPAN, heads, width), bmat.reshape(count, SPAN, bmat.shape[1]), cmat.reshape(count, SPAN, cmat.shape[1]), dts.reshape(count, SPAN, heads), jnp.broadcast_to(rates[None, :], (count, heads)))
    start = jnp.zeros((heads, width, bmat.shape[1]), jnp.float32)
    final, outs = lax.scan(jax.checkpoint(span_step), start, blocks)
    return outs.reshape(total, heads, width)

def one_sequence(params, u):
    w_in, w_out, norm_gain, conv_weight, conv_bias, dt_bias, a_log, skip, gate_gain = params
    normed = low(rms_gain(u, norm_gain))
    projected = low_back(low(product(normed, w_in)))
    gates = projected[:, :INNER]
    mixed_in = jax.nn.silu(causal_conv(projected[:, INNER:2 * INNER + 2 * STATE], conv_weight, conv_bias))
    xs = mixed_in[:, :INNER].reshape(LEN, HEADS, HEADDIM)
    bmat = mixed_in[:, INNER:INNER + STATE]
    cmat = mixed_in[:, INNER + STATE:]
    dts = jax.nn.softplus(projected[:, 2 * INNER + 2 * STATE:] + dt_bias[None, :])
    rates = -jnp.exp(a_log)
    scanned = scan_heads(xs, bmat, cmat, dts, rates) + skip[None, :, None] * xs
    scanned = low_back(low(scanned.reshape(LEN, INNER)))
    normalized = low(rms_gain(scanned * jax.nn.silu(gates), gate_gain))
    return u + product(normalized, w_out)

def forward(params, inputs):
    return lax.map(jax.checkpoint(partial(one_sequence, params)), inputs)

def reference(inputs, w_in, w_out, norm_gain, conv_weight, conv_bias, dt_bias, a_log, skip, gate_gain, cotangent):
    params = (w_in.astype(jnp.float32), w_out.astype(jnp.float32), norm_gain, conv_weight, conv_bias, dt_bias, a_log, skip, gate_gain)
    result, pullback = jax.vjp(forward, params, inputs.astype(jnp.float32))
    grads, grad_inputs = pullback(cotangent.astype(jnp.float32))
    return (result.astype(jnp.bfloat16), grad_inputs, grads[0], grads[1], grads[2], grads[3], grads[4], grads[5], grads[6], grads[7], grads[8])
```

```python
import functools

import jax
import jax.numpy as jnp
from jax import lax
from jax.experimental import pallas as pl
from jax.experimental.pallas import tpu as pltpu
from jax.sharding import PartitionSpec as P

HEADS = 24
HEADDIM = 64
STATE = 128
LANES = 128
Q = 128
QUAD = 256
EPS = 1e-05
F32 = jnp.float32
BF16 = jnp.bfloat16
VMEM_LIMIT = 56 * 1024 * 1024


def dot(left, right, dims):
    return lax.dot_general(left, right, (dims, ((), ())), preferred_element_type=F32)


def nn(left, right):
    return dot(left, right, ((1,), (0,)))


def nt(left, right):
    return dot(left, right, ((1,), (1,)))


def tn(left, right):
    return dot(left, right, ((0,), (0,)))


def exact(left, right):
    return lax.dot_general(
        left, right, (((1,), (0,)), ((), ())), precision=lax.Precision.HIGHEST,
        preferred_element_type=F32,
    )


def split2(values):
    high = values.astype(BF16)
    rest = (values - high.astype(F32)).astype(BF16)
    return jnp.concatenate([high, rest], axis=1)


def sigmoid(values):
    return 0.5 + 0.5 * jnp.tanh(0.5 * values)


def softplus(values):
    return jnp.maximum(values, 0.0) + jnp.log1p(jnp.exp(-jnp.abs(values)))


def iotas(rows, cols):
    return (
        lax.broadcasted_iota(jnp.int32, (rows, cols), 0),
        lax.broadcasted_iota(jnp.int32, (rows, cols), 1),
    )


def head_matrices(inner):
    col_head = jnp.arange(inner) // HEADDIM
    expand = (jnp.arange(LANES)[:, None] == col_head[None, :]).astype(BF16)
    return jnp.concatenate([expand, expand], axis=0), expand.T


def block_pair(pair):
    low = lax.broadcasted_iota(jnp.int32, pair.shape, 1) < HEADDIM
    zero = jnp.zeros_like(pair)
    return jnp.concatenate([jnp.where(low, pair, zero), jnp.where(low, zero, pair)], axis=0)


def conv_columns(ext_ref, taps_ref, bias_ref, cols, rows):
    total = bias_ref[0:1, cols] + taps_ref[0:1, cols] * ext_ref[pl.ds(5, rows), cols]
    for k in range(1, 4):
        total = total + taps_ref[k : k + 1, cols] * ext_ref[pl.ds(5 + k, rows), cols]
    return total


def fill_ext(ext_ref, xbc_ref, prev_ref, halo_ref, first):
    rows = xbc_ref.shape[1]
    before = jnp.where(first, halo_ref[0].astype(F32), prev_ref[0].astype(F32))
    ext_ref[0:8, :] = before[8:16]
    ext_ref[pl.ds(8, rows), :] = xbc_ref[0].astype(F32)


def scan_kernel(
    xbc_ref, prev_ref, halo_ref, raw_ref, taps_ref, bias_ref, heads_ref, ex_ref,
    act_ref, y_ref, dt_ref, cum_ref, dev_ref, st_ref, fin_ref,
    ext_ref, state_ref, carry_ref,
):
    c = pl.program_id(1)
    width = xbc_ref.shape[2]
    inner = y_ref.shape[2]

    @pl.when(c == 0)
    def _():
        state_ref[...] = jnp.zeros_like(state_ref)
        carry_ref[...] = jnp.zeros_like(carry_ref)

    fill_ext(ext_ref, xbc_ref, prev_ref, halo_ref, c == 0)
    for start in range(0, width, QUAD):
        cols = slice(start, start + QUAD)
        half = 0.5 * conv_columns(ext_ref, taps_ref, bias_ref, cols, Q)
        act_ref[0, :, cols] = (half + half * jnp.tanh(half)).astype(BF16)

    dts = softplus(raw_ref[0].astype(F32) + heads_ref[0:1, :]) * heads_ref[3:4, :]
    row, col = iotas(Q, Q)
    lower = row >= col
    cum = exact(lower.astype(F32), dts * heads_ref[1:2, :])
    dev = cum + carry_ref[0:1, :]
    carry_ref[...] = jnp.broadcast_to(dev[Q - 1 : Q, :], carry_ref.shape)
    dt_ref[0] = dts
    cum_ref[0] = cum
    dev_ref[0] = dev
    cum_t = cum.T
    dt2 = split2(dts)
    ec2 = split2(jnp.exp(cum))
    tail2 = split2(jnp.exp(cum[Q - 1 : Q, :] - cum))

    bmat = act_ref[0, :, inner : inner + STATE]
    cmat = act_ref[0, :, inner + STATE : inner + 2 * STATE]
    bmat_t = bmat.astype(F32).T.astype(BF16)
    scores = jnp.where(lower, nt(cmat, bmat), 0.0)

    for quad in range(inner // QUAD):
        cols = slice(quad * QUAD, (quad + 1) * QUAD)
        ex = ex_ref[:, cols]
        xdt = act_ref[0, :, cols].astype(F32) * nn(dt2, ex)
        xdt_b = xdt.astype(BF16)
        xtail = (xdt * nn(tail2, ex)).astype(BF16)
        ece = nn(ec2, ex)
        parts = []
        for pair in range(2):
            heads = [quad * 4 + pair * 2, quad * 4 + pair * 2 + 1]
            mats = []
            for h in heads:
                diff = cum[:, h : h + 1] - cum_t[h : h + 1, :]
                mats.append((scores * jnp.exp(jnp.minimum(diff, 0.0))).astype(BF16))
            mat = jnp.concatenate(mats, axis=1)
            parts.append(nn(mat, block_pair(xdt_b[:, pair * LANES : (pair + 1) * LANES])))
        state = state_ref[:, cols]
        state_b = state.astype(BF16)
        st_ref[0, 0, :, cols] = state_b
        y_ref[0, :, cols] = jnp.concatenate(parts, axis=1) + ece * nn(cmat, state_b)
        new = state * ece[Q - 1 : Q, :] + nn(bmat_t, xtail)
        state_ref[:, cols] = new
        fin_ref[0, :, cols] = new


def scan_call(xbc, halo, raw, taps, bias, heads, ex, inner):
    seqs, length, width = xbc.shape
    chunks = length // Q
    whole = lambda s, c: (0, 0)
    row = lambda s, c: (s, c, 0)
    lanes = jax.ShapeDtypeStruct((seqs, length, LANES), F32)
    return pl.pallas_call(
        scan_kernel,
        grid=(seqs, chunks),
        in_specs=[
            pl.BlockSpec((1, Q, width), row),
            pl.BlockSpec((1, 16, width), lambda s, c: (s, jnp.maximum(c * (Q // 16) - 1, 0), 0)),
            pl.BlockSpec((1, 16, width), lambda s, c: (s, 0, 0)),
            pl.BlockSpec((1, Q, LANES), row),
            pl.BlockSpec(taps.shape, whole),
            pl.BlockSpec(bias.shape, whole),
            pl.BlockSpec(heads.shape, whole),
            pl.BlockSpec(ex.shape, whole),
        ],
        out_specs=[
            pl.BlockSpec((1, Q, width), row),
            pl.BlockSpec((1, Q, inner), row),
            pl.BlockSpec((1, Q, LANES), row),
            pl.BlockSpec((1, Q, LANES), row),
            pl.BlockSpec((1, Q, LANES), row),
            pl.BlockSpec((1, 1, STATE, inner), lambda s, c: (s, c, 0, 0)),
            pl.BlockSpec((1, STATE, inner), lambda s, c: (s, 0, 0)),
        ],
        out_shape=[
            jax.ShapeDtypeStruct((seqs, length, width), BF16),
            jax.ShapeDtypeStruct((seqs, length, inner), F32),
            lanes,
            lanes,
            lanes,
            jax.ShapeDtypeStruct((seqs, chunks, STATE, inner), BF16),
            jax.ShapeDtypeStruct((seqs, STATE, inner), F32),
        ],
        scratch_shapes=[
            pltpu.VMEM((Q + 8, width), F32),
            pltpu.VMEM((STATE, inner), F32),
            pltpu.VMEM((8, LANES), F32),
        ],
        compiler_params=pltpu.CompilerParams(vmem_limit_bytes=VMEM_LIMIT),
        name="scan_forward",
    )(xbc, xbc, halo, raw, taps, bias, heads, ex)


def gate_kernel(
    y_ref, act_ref, z_ref, dev_ref, sin_ref, u_ref, c_ref, w_ref, vec_ref, ex_ref, red_ref,
    mixed_ref, dy_ref, dz_ref, norm_ref, rows_ref, q2_ref, sums_ref, ds_ref,
):
    s, i = pl.program_id(0), pl.program_id(1)
    inner = y_ref.shape[2]

    @pl.when(jnp.logical_and(s == 0, i == 0))
    def _():
        sums_ref[...] = jnp.zeros_like(sums_ref)

    @pl.when(i == 0)
    def _():
        ds_ref[...] = jnp.zeros_like(ds_ref)

    cmat = act_ref[0, :, inner + STATE : inner + 2 * STATE]
    ec2 = split2(jnp.exp(dev_ref[0]))
    ece = nn(ec2, ex_ref[...])
    x = act_ref[0, :, :inner].astype(F32)
    y_loc = y_ref[0]
    y_in = ece * nn(cmat, sin_ref[0])
    y = (y_loc + y_in + vec_ref[1:2, :] * x).astype(BF16).astype(F32)
    z = z_ref[0].astype(F32)
    sig = sigmoid(z)
    silu = z * sig
    g = y * silu
    scale = lax.rsqrt(jnp.mean(g * g, axis=1, keepdims=True) + EPS)
    gain = vec_ref[0:1, :]
    gs = g * scale
    normalized = (gs * gain).astype(BF16)
    norm_ref[0] = normalized
    mixed_ref[0] = (u_ref[0].astype(F32) + nn(normalized, w_ref[...])).astype(BF16)
    gn = nt(c_ref[0], w_ref[...])
    sums_ref[0:1, :] += jnp.sum(gn * gs, axis=0, keepdims=True)
    h = gn * gain
    dg = scale * (h - gs * jnp.mean(h * gs, axis=1, keepdims=True))
    dy_b = (dg * silu).astype(BF16)
    dy = dy_b.astype(F32)
    dy_ref[0] = dy_b
    dz_ref[0] = (dg * y * (sig + silu * (1.0 - sig))).astype(BF16)
    sums_ref[1:2, :] += jnp.sum(dy * x, axis=0, keepdims=True)
    rows = dy * y_loc
    high = rows.astype(BF16)
    rest = (rows - high.astype(F32)).astype(BF16)
    rows_ref[0] = nn(high, red_ref[...]) + nn(rest, red_ref[...])
    q2_ref[0] = nn((dy * y_in).astype(BF16), red_ref[...])
    ds_ref[0] += tn(cmat, (dy * ece).astype(BF16))


def gate_call(y, act, z, dev, s_in, u, cot, w_out, vecs, ex, red, rows):
    seqs, length, inner = y.shape
    width = act.shape[2]
    depth = u.shape[2]
    whole = lambda s, c: (0, 0)
    row = lambda s, c: (s, c, 0)
    per_seq = lambda s, c: (s, 0, 0)
    lanes = jax.ShapeDtypeStruct((seqs, length, LANES), F32)
    wide = jax.ShapeDtypeStruct((seqs, length, inner), BF16)
    return pl.pallas_call(
        gate_kernel,
        grid=(seqs, length // rows),
        in_specs=[
            pl.BlockSpec((1, rows, inner), row),
            pl.BlockSpec((1, rows, width), row),
            pl.BlockSpec((1, rows, inner), row),
            pl.BlockSpec((1, rows, LANES), row),
            pl.BlockSpec((1, STATE, inner), per_seq),
            pl.BlockSpec((1, rows, depth), row),
            pl.BlockSpec((1, rows, depth), row),
            pl.BlockSpec(w_out.shape, whole),
            pl.BlockSpec(vecs.shape, whole),
            pl.BlockSpec(ex.shape, whole),
            pl.BlockSpec(red.shape, whole),
        ],
        out_specs=[
            pl.BlockSpec((1, rows, depth), row),
            pl.BlockSpec((1, rows, inner), row),
            pl.BlockSpec((1, rows, inner), row),
            pl.BlockSpec((1, rows, inner), row),
            pl.BlockSpec((1, rows, LANES), row),
            pl.BlockSpec((1, rows, LANES), row),
            pl.BlockSpec((8, inner), whole),
            pl.BlockSpec((1, STATE, inner), per_seq),
        ],
        out_shape=[
            jax.ShapeDtypeStruct((seqs, length, depth), BF16),
            wide,
            wide,
            wide,
            lanes,
            lanes,
            jax.ShapeDtypeStruct((8, inner), F32),
            jax.ShapeDtypeStruct((seqs, STATE, inner), F32),
        ],
        compiler_params=pltpu.CompilerParams(vmem_limit_bytes=VMEM_LIMIT),
        name="gate_and_output",
    )(y, act, z, dev, s_in, u, cot, w_out, vecs, ex, red)


def back_kernel(
    act_ref, dy_ref, dt_ref, cum_ref, dev_ref, st_ref, sin_ref, rows_ref, vec_ref, ex_ref, red_ref,
    g_ref, direct_ref, da_ref,
    ds_ref,
):
    inner = dy_ref.shape[2]

    @pl.when(pl.program_id(1) == 0)
    def _():
        ds_ref[...] = jnp.zeros_like(ds_ref)

    bmat = act_ref[0, :, inner : inner + STATE]
    cmat = act_ref[0, :, inner + STATE : inner + 2 * STATE]
    cmat_t = cmat.astype(F32).T.astype(BF16)
    row, col = iotas(Q, Q)
    upper = row <= col
    scores = jnp.where(upper, nt(bmat, cmat), 0.0)
    cum = cum_ref[0]
    cum_t = cum.T
    dt2 = split2(dt_ref[0])
    ec2 = split2(jnp.exp(cum))
    tail2 = split2(jnp.exp(cum[Q - 1 : Q, :] - cum))
    before2 = split2(jnp.exp(dev_ref[0, 0:8, :] - cum[0:8, :]))

    d_scores = jnp.zeros((Q, Q), F32)
    db = jnp.zeros((Q, STATE), F32)
    dc = jnp.zeros((Q, STATE), F32)
    direct = jnp.zeros((Q, LANES), F32)
    col_sums = jnp.zeros((Q, LANES), F32)
    w_loc = jnp.zeros((Q, LANES), F32)
    const = jnp.zeros((8, LANES), F32)
    for quad in range(inner // QUAD):
        cols = slice(quad * QUAD, (quad + 1) * QUAD)
        ex = ex_ref[:, cols]
        red = red_ref[cols, :]
        dte = nn(dt2, ex)
        tle = nn(tail2, ex)
        ece = nn(ec2, ex)
        x = act_ref[0, :, cols].astype(F32)
        xdt_b = (x * dte).astype(BF16)
        xdt = xdt_b.astype(F32)
        dy_b = dy_ref[0, :, cols]
        dy = dy_b.astype(F32)
        parts = []
        for pair in range(2):
            lanes = slice(pair * LANES, (pair + 1) * LANES)
            stacked = block_pair(dy_b[:, lanes])
            d_mat = nt(xdt_b[:, lanes], stacked)
            mats = []
            for j in range(2):
                h = quad * 4 + pair * 2 + j
                decay = jnp.exp(jnp.minimum(cum_t[h : h + 1, :] - cum[:, h : h + 1], 0.0))
                mats.append((scores * decay).astype(BF16))
                d_scores = d_scores + d_mat[:, j * Q : (j + 1) * Q] * decay
            parts.append(nn(jnp.concatenate(mats, axis=1), stacked))
        ds = ds_ref[:, cols]
        ds_b = ds.astype(BF16)
        st = st_ref[0, 0, :, cols].astype(F32)
        before = nn(before2, ex)[0:1, :]
        state_b = (st + before * sin_ref[0, :, cols].astype(F32)).astype(BF16)
        dx_intra = jnp.concatenate(parts, axis=1)
        dx_inter = tle * nn(bmat, ds_b)
        dxp = dx_intra + dx_inter
        g_ref[0, :, cols] = dte * dxp + vec_ref[1:2, cols] * dy
        direct = direct + nn((x * dxp).astype(BF16), red)
        prod = xdt * dx_intra
        high = prod.astype(BF16)
        col_sums = col_sums + nn(high, red) + nn((prod - high.astype(F32)).astype(BF16), red)
        w_loc = w_loc + nn((xdt * dx_inter).astype(BF16), red)
        db = db + nt((xdt * tle).astype(BF16), ds_b)
        dye = (dy * ece).astype(BF16)
        dc = dc + nt(dye, state_b)
        last = ece[Q - 1 : Q, :]
        both = jnp.sum(st * ds, axis=0, keepdims=True) * last
        both = jnp.broadcast_to(both, (8, QUAD))
        high = both.astype(BF16)
        const = const + nn(high, red) + nn((both - high.astype(F32)).astype(BF16), red)
        ds_ref[:, cols] = ds * last + nn(cmat_t, dye)
    d_scores = jnp.where(upper, d_scores, 0.0)
    g_ref[0, :, inner : inner + STATE] = db + nn(d_scores.astype(BF16), cmat)
    g_ref[0, :, inner + STATE :] = dc + nn(d_scores.T.astype(BF16), bmat)
    direct_ref[0] = direct
    da_ref[0] = (
        exact(upper.astype(F32), rows_ref[0] - col_sums)
        + exact((row > col).astype(F32), w_loc)
        + const[0:1, :]
    )


def back_call(act, dy, dts, cum, dev, states, s_in, rows, vecs, ex, red):
    seqs, length, width = act.shape
    inner = dy.shape[2]
    chunks = length // Q
    whole = lambda s, c: (0, 0)
    row = lambda s, c: (s, chunks - 1 - c, 0)
    lanes = jax.ShapeDtypeStruct((seqs, length, LANES), F32)
    lane_block = pl.BlockSpec((1, Q, LANES), row)
    return pl.pallas_call(
        back_kernel,
        grid=(seqs, chunks),
        in_specs=[
            pl.BlockSpec((1, Q, width), row),
            pl.BlockSpec((1, Q, inner), row),
            lane_block,
            lane_block,
            lane_block,
            pl.BlockSpec((1, 1, STATE, inner), lambda s, c: (s, chunks - 1 - c, 0, 0)),
            pl.BlockSpec((1, STATE, inner), lambda s, c: (s, 0, 0)),
            lane_block,
            pl.BlockSpec(vecs.shape, whole),
            pl.BlockSpec(ex.shape, whole),
            pl.BlockSpec(red.shape, whole),
        ],
        out_specs=[pl.BlockSpec((1, Q, width), row), lane_block, lane_block],
        out_shape=[jax.ShapeDtypeStruct((seqs, length, width), F32), lanes, lanes],
        scratch_shapes=[pltpu.VMEM((STATE, inner), F32)],
        compiler_params=pltpu.CompilerParams(vmem_limit_bytes=VMEM_LIMIT),
        name="scan_backward",
    )(act, dy, dts, cum, dev, states, s_in, rows, vecs, ex, red)


def finish_kernel(
    g_ref, act_ref, xbc_ref, prev_ref, halo_ref, raw_ref, dt_ref, dev_ref, tot_ref, ds_ref, q2_ref,
    direct_ref, da_ref, c4_ref, taps_ref, bias_ref, heads_ref, ex_ref, red_ref,
    gconv_ref, gdt_ref, taps_sum_ref, heads_sum_ref,
    ext_ref, carry_ref,
):
    s, c = pl.program_id(0), pl.program_id(1)
    width = xbc_ref.shape[2]
    inner = ds_ref.shape[2]
    rows = xbc_ref.shape[1]

    @pl.when(jnp.logical_and(s == 0, c == 0))
    def _():
        taps_sum_ref[...] = jnp.zeros_like(taps_sum_ref)
        heads_sum_ref[...] = jnp.zeros_like(heads_sum_ref)

    @pl.when(c == 0)
    def _():
        carry_ref[...] = jnp.zeros_like(carry_ref)

    fill_ext(ext_ref, xbc_ref, prev_ref, halo_ref, c == 0)

    def conv_back(grad, cols):
        conv = conv_columns(ext_ref, taps_ref, bias_ref, cols, rows)
        sig = sigmoid(conv)
        out = grad * (sig + conv * sig * (1.0 - sig))
        gconv_ref[0, :, cols] = out
        for k in range(4):
            taps_sum_ref[k : k + 1, cols] += jnp.sum(
                out * ext_ref[pl.ds(5 + k, rows), cols], axis=0, keepdims=True
            )
        taps_sum_ref[4:5, cols] += jnp.sum(out, axis=0, keepdims=True)

    bmat = act_ref[0, :, inner : inner + STATE]
    dts = dt_ref[0]
    dt2 = split2(dts)
    tail2 = split2(jnp.exp(tot_ref[0, 0:1, :] - dev_ref[0]))
    db = jnp.zeros((rows, STATE), F32)
    direct = direct_ref[0]
    q3 = jnp.zeros((rows, LANES), F32)
    for quad in range(inner // QUAD):
        cols = slice(quad * QUAD, (quad + 1) * QUAD)
        ex = ex_ref[:, cols]
        red = red_ref[cols, :]
        dte = nn(dt2, ex)
        tle = nn(tail2, ex)
        x = act_ref[0, :, cols].astype(F32)
        xdt = (x * dte).astype(BF16).astype(F32)
        ds_b = ds_ref[0, :, cols]
        dxc = tle * nn(bmat, ds_b)
        direct = direct + nn((x * dxc).astype(BF16), red)
        q3 = q3 + nn((xdt * dxc).astype(BF16), red)
        db = db + nt((xdt * tle).astype(BF16), ds_b)
        conv_back(g_ref[0, :, cols] + dte * dxc, cols)
    db_all = jnp.concatenate([db, jnp.zeros_like(db)], axis=1)
    cols = slice(inner, inner + QUAD)
    conv_back(g_ref[0, :, cols] + db_all, cols)

    step = q3 - q2_ref[0]
    row, col = iotas(rows, rows)
    prefix = exact((row > col).astype(F32), step) + carry_ref[0:1, :]
    carry_ref[...] = carry_ref[...] + jnp.sum(step, axis=0, keepdims=True)
    da = da_ref[0] + c4_ref[0, 0:1, :] + prefix
    rate = heads_ref[1:2, :]
    raw = raw_ref[0].astype(F32) + heads_ref[0:1, :]
    grad = (direct + rate * da) * sigmoid(raw) * heads_ref[3:4, :]
    gdt_ref[0] = grad.astype(BF16)
    heads_sum_ref[0:1, :] += jnp.sum(grad, axis=0, keepdims=True)
    heads_sum_ref[1:2, :] += jnp.sum(da * dts, axis=0, keepdims=True) * rate


def finish_call(
    grad, act, xbc, halo, raw, dts, dev, tot, ds_end, q2, direct, da, c4, taps, bias, heads, ex, red,
    rows,
):
    seqs, length, width = xbc.shape
    inner = ds_end.shape[2]
    whole = lambda s, c: (0, 0)
    row = lambda s, c: (s, c, 0)
    per_seq = lambda s, c: (s, 0, 0)
    lane_block = pl.BlockSpec((1, rows, LANES), row)
    wide_block = pl.BlockSpec((1, rows, width), row)
    return pl.pallas_call(
        finish_kernel,
        grid=(seqs, length // rows),
        in_specs=[
            wide_block,
            wide_block,
            wide_block,
            pl.BlockSpec((1, 16, width), lambda s, c: (s, jnp.maximum(c * (rows // 16) - 1, 0), 0)),
            pl.BlockSpec((1, 16, width), per_seq),
            lane_block,
            lane_block,
            lane_block,
            pl.BlockSpec((1, 8, LANES), per_seq),
            pl.BlockSpec((1, STATE, inner), per_seq),
            lane_block,
            lane_block,
            lane_block,
            pl.BlockSpec((1, 8, LANES), per_seq),
            pl.BlockSpec(taps.shape, whole),
            pl.BlockSpec(bias.shape, whole),
            pl.BlockSpec(heads.shape, whole),
            pl.BlockSpec(ex.shape, whole),
            pl.BlockSpec(red.shape, whole),
        ],
        out_specs=[
            wide_block,
            lane_block,
            pl.BlockSpec((8, width), whole),
            pl.BlockSpec((8, LANES), whole),
        ],
        out_shape=[
            jax.ShapeDtypeStruct((seqs, length, width), F32),
            jax.ShapeDtypeStruct((seqs, length, LANES), BF16),
            jax.ShapeDtypeStruct((8, width), F32),
            jax.ShapeDtypeStruct((8, LANES), F32),
        ],
        scratch_shapes=[pltpu.VMEM((rows + 8, width), F32), pltpu.VMEM((8, LANES), F32)],
        compiler_params=pltpu.CompilerParams(vmem_limit_bytes=VMEM_LIMIT),
        name="conv_backward",
    )(
        grad, act, xbc, xbc, halo, raw, dts, dev, tot, ds_end, q2, direct, da, c4, taps, bias, heads,
        ex, red,
    )


def rms_gain(values, gain):
    return values * lax.rsqrt(jnp.mean(values * values, axis=-1, keepdims=True) + EPS) * gain


def shift_in(value, size, step):
    pairs = [(i, i + step) for i in range(size) if 0 <= i + step < size]
    return lax.ppermute(value, "seq", pairs)


def carry_over(states, totals, size, step):
    seqs, depth, inner = states.shape
    piece = depth // size
    sent = states.astype(BF16).reshape(seqs, size, piece, inner)
    got = lax.all_to_all(sent, "seq", split_axis=1, concat_axis=1, tiled=True).astype(F32)
    decay = jnp.exp(lax.all_gather(totals, "seq", axis=0))
    order = range(size) if step > 0 else range(size - 1, -1, -1)
    held = jnp.zeros((seqs, piece, inner), F32)
    into = [None] * size
    for i in order:
        into[i] = held
        held = held * decay[i][:, None, :] + got[:, i]
    back = jnp.stack(into, axis=1).astype(BF16)
    back = lax.all_to_all(back, "seq", split_axis=1, concat_axis=1, tiled=True)
    return back.reshape(seqs, depth, inner)


def body(
    size, inputs, w_in, w_out, norm_gain, conv_weight, conv_bias, dt_bias, a_log, skip, gate_gain,
    cotangent,
):
    seqs, length, depth = inputs.shape
    inner = gate_gain.shape[0]
    width = conv_weight.shape[1]
    tokens = seqs * length
    rows = min(256, length)

    full_in = lax.all_gather(w_in, "seq", axis=0, tiled=True)
    full_out = lax.all_gather(w_out, "seq", axis=0, tiled=True)
    w_z = full_in[:, :inner]
    w_x = full_in[:, inner : inner + width]
    w_dt = jnp.pad(full_in[:, inner + width :], ((0, 0), (0, LANES - HEADS)))

    def pad_heads(values):
        return jnp.pad(values, (0, LANES - HEADS))

    rates = -jnp.exp(a_log)
    heads = jnp.stack([pad_heads(dt_bias), pad_heads(rates), pad_heads(skip), pad_heads(jnp.ones_like(skip))])
    heads = jnp.pad(heads, ((0, 4), (0, 0)))
    taps = jnp.pad(conv_weight, ((0, 4), (0, 0)))
    bias = jnp.pad(conv_bias[None, :], ((0, 7), (0, 0)))
    vecs = jnp.pad(jnp.stack([gate_gain, jnp.repeat(skip, HEADDIM)]), ((0, 6), (0, 0)))
    ex, red = head_matrices(inner)

    edge = shift_in(inputs[:, length - 16 :], size, 1).astype(F32)
    halo = jnp.dot(rms_gain(edge, norm_gain).astype(BF16).reshape(seqs * 16, depth), w_x,
                   preferred_element_type=F32).astype(BF16).reshape(seqs, 16, width)
    u = inputs.reshape(tokens, depth)
    u32 = u.astype(F32)
    scale = lax.rsqrt(jnp.mean(u32 * u32, axis=-1, keepdims=True) + EPS)
    normed = (u32 * scale * norm_gain).astype(BF16)

    def project(matrix):
        out = jnp.dot(normed, matrix, preferred_element_type=F32).astype(BF16)
        return out.reshape(seqs, length, matrix.shape[1])

    xbc, raw, z = project(w_x), project(w_dt), project(w_z)

    act, y, dts, cum, dev, states, final = scan_call(xbc, halo, raw, taps, bias, heads, ex, inner)
    total = dev[:, length - 1, :]
    total_cols = jnp.repeat(total[:, :HEADS], HEADDIM, axis=1)
    s_in = carry_over(final, total_cols, size, 1)

    mixed, dy, dz, normalized, row_sums, q2, gate_sums, ds_loc = gate_call(
        y, act, z, dev, s_in, inputs, cotangent, full_out, vecs, ex, red, rows
    )
    cot = cotangent.reshape(tokens, depth)
    grad_out_full = lax.dot_general(
        normalized.reshape(tokens, inner), cot, (((0,), (0,)), ((), ())), preferred_element_type=F32
    )
    rows_out = lax.psum(lax.psum_scatter(grad_out_full, "seq", scatter_dimension=0, tiled=True), "dp")

    ds_end = carry_over(ds_loc, total_cols, size, -1)
    grad, direct, da = back_call(act, dy, dts, cum, dev, states, s_in, row_sums, vecs, ex, red)

    both = (s_in.astype(F32) * ds_end.astype(F32)).sum(axis=1).reshape(seqs, HEADS, HEADDIM).sum(axis=2)
    both = jnp.pad(both, ((0, 0), (0, LANES - HEADS))) * jnp.exp(total)
    c4 = jnp.broadcast_to((both + q2.sum(axis=1))[:, None, :], (seqs, 8, LANES))
    tot = jnp.broadcast_to(total[:, None, :], (seqs, 8, LANES))
    gconv, gdt, taps_sum, heads_sum = finish_call(
        grad, act, xbc, halo, raw, dts, dev, tot, ds_end, q2, direct, da, c4, taps, bias, heads, ex,
        red, rows,
    )

    after = shift_in(gconv[:, :8], size, -1)
    ext = jnp.concatenate([gconv, after], axis=1)
    gx = sum(conv_weight[k][None, None, :] * ext[:, 3 - k : 3 - k + length] for k in range(4))
    gx = gx.astype(BF16).reshape(tokens, width)
    dz = dz.reshape(tokens, inner)
    gdt = gdt.reshape(tokens, LANES)

    def weight_grad(columns):
        return lax.dot_general(normed, columns, (((0,), (0,)), ((), ())), preferred_element_type=F32)

    grad_in_full = jnp.concatenate(
        [weight_grad(dz), weight_grad(gx), weight_grad(gdt)[:, :HEADS]], axis=1
    )
    rows_in = lax.psum(lax.psum_scatter(grad_in_full, "seq", scatter_dimension=0, tiled=True), "dp")

    grad_normed = sum(
        lax.dot_general(columns, matrix, (((1,), (1,)), ((), ())), preferred_element_type=F32)
        for columns, matrix in ((dz, w_z), (gx, w_x), (gdt, w_dt))
    )
    us = u32 * scale
    h = grad_normed * norm_gain
    grad_norm_gain = jnp.sum(grad_normed * us, axis=0)
    grad_u = scale * (h - us * jnp.mean(h * us, axis=-1, keepdims=True))
    grad_inputs = (cot.astype(F32) + grad_u).reshape(seqs, length, depth)

    sums = lax.psum(
        (
            grad_norm_gain,
            taps_sum[:4],
            taps_sum[4],
            heads_sum[0, :HEADS],
            heads_sum[1, :HEADS],
            gate_sums[1].reshape(HEADS, HEADDIM).sum(axis=1),
            gate_sums[0],
        ),
        ("dp", "seq"),
    )
    return (mixed, grad_inputs, rows_in, rows_out, *sums)


def solution(mesh):
    placed = (
        P("dp", "seq", None),
        P("seq", None),
        P("seq", None),
        P(),
        P(),
        P(),
        P(),
        P(),
        P(),
        P(),
        P("dp", "seq", None),
    )
    return jax.shard_map(
        functools.partial(body, mesh.shape["seq"]),
        mesh=mesh,
        in_specs=placed,
        out_specs=(
            P("dp", "seq", None),
            P("dp", "seq", None),
            P("seq", None),
            P("seq", None),
            P(),
            P(),
            P(),
            P(),
            P(),
            P(),
            P(),
        ),
        check_vma=False,
    )
```

```python
import functools

import jax
import jax.numpy as jnp
from jax import lax
from jax.experimental import pallas as pl
from jax.experimental.pallas import tpu as pltpu
from jax.sharding import PartitionSpec as P

HEADS = 24
HEADDIM = 64
STATE = 128
LANES = 128
Q = 128
QUAD = 256
EPS = 1e-05
F32 = jnp.float32
BF16 = jnp.bfloat16
VMEM_LIMIT = 56 * 1024 * 1024


def cost(tokens, per_token_ns):
    seconds = tokens * per_token_ns * 1e-9
    return pl.CostEstimate(
        flops=int(seconds * 1e15), bytes_accessed=int(seconds * 3e12), transcendentals=0
    )


def dot(left, right, dims):
    return lax.dot_general(left, right, (dims, ((), ())), preferred_element_type=F32)


def nn(left, right):
    return dot(left, right, ((1,), (0,)))


def nt(left, right):
    return dot(left, right, ((1,), (1,)))


def tn(left, right):
    return dot(left, right, ((0,), (0,)))


def exact(left, right):
    return lax.dot_general(
        left, right, (((1,), (0,)), ((), ())), precision=lax.Precision.HIGHEST,
        preferred_element_type=F32,
    )


def split2(values):
    high = values.astype(BF16)
    rest = (values - high.astype(F32)).astype(BF16)
    return jnp.concatenate([high, rest], axis=1)


def sigmoid(values):
    return 0.5 + 0.5 * jnp.tanh(0.5 * values)


def softplus(values):
    return jnp.maximum(values, 0.0) + jnp.log1p(jnp.exp(-jnp.abs(values)))


def iotas(rows, cols):
    return (
        lax.broadcasted_iota(jnp.int32, (rows, cols), 0),
        lax.broadcasted_iota(jnp.int32, (rows, cols), 1),
    )


def head_matrices(inner):
    col_head = jnp.arange(inner) // HEADDIM
    expand = (jnp.arange(LANES)[:, None] == col_head[None, :]).astype(BF16)
    return jnp.concatenate([expand, expand], axis=0), expand.T


def block_pair(pair):
    low = lax.broadcasted_iota(jnp.int32, pair.shape, 1) < HEADDIM
    zero = jnp.zeros_like(pair)
    return jnp.concatenate([jnp.where(low, pair, zero), jnp.where(low, zero, pair)], axis=0)


def conv_columns(ext_ref, taps_ref, bias_ref, cols, rows):
    total = bias_ref[0:1, cols] + taps_ref[0:1, cols] * ext_ref[pl.ds(5, rows), cols]
    for k in range(1, 4):
        total = total + taps_ref[k : k + 1, cols] * ext_ref[pl.ds(5 + k, rows), cols]
    return total


def fill_ext(ext_ref, xbc_ref, prev_ref, halo_ref, first):
    rows = xbc_ref.shape[1]
    before = jnp.where(first, halo_ref[0].astype(F32), prev_ref[0].astype(F32))
    ext_ref[0:8, :] = before[8:16]
    ext_ref[pl.ds(8, rows), :] = xbc_ref[0].astype(F32)


def scan_kernel(
    xbc_ref, prev_ref, halo_ref, raw_ref, taps_ref, bias_ref, heads_ref, ex_ref,
    act_ref, y_ref, dt_ref, cum_ref, dev_ref, st_ref, fin_ref,
    ext_ref, state_ref, carry_ref,
):
    c = pl.program_id(1)
    width = xbc_ref.shape[2]
    inner = y_ref.shape[2]

    @pl.when(c == 0)
    def _():
        state_ref[...] = jnp.zeros_like(state_ref)
        carry_ref[...] = jnp.zeros_like(carry_ref)

    fill_ext(ext_ref, xbc_ref, prev_ref, halo_ref, c == 0)
    for start in range(0, width, QUAD):
        cols = slice(start, start + QUAD)
        half = 0.5 * conv_columns(ext_ref, taps_ref, bias_ref, cols, Q)
        act_ref[0, :, cols] = (half + half * jnp.tanh(half)).astype(BF16)

    dts = softplus(raw_ref[0].astype(F32) + heads_ref[0:1, :]) * heads_ref[3:4, :]
    row, col = iotas(Q, Q)
    lower = row >= col
    cum = exact(lower.astype(F32), dts * heads_ref[1:2, :])
    dev = cum + carry_ref[0:1, :]
    carry_ref[...] = jnp.broadcast_to(dev[Q - 1 : Q, :], carry_ref.shape)
    dt_ref[0] = dts
    cum_ref[0] = cum
    dev_ref[0] = dev
    cum_t = cum.T
    dt2 = split2(dts)
    ec2 = split2(jnp.exp(cum))
    tail2 = split2(jnp.exp(cum[Q - 1 : Q, :] - cum))

    bmat = act_ref[0, :, inner : inner + STATE]
    cmat = act_ref[0, :, inner + STATE : inner + 2 * STATE]
    bmat_t = bmat.astype(F32).T.astype(BF16)
    scores = jnp.where(lower, nt(cmat, bmat), 0.0)

    for quad in range(inner // QUAD):
        cols = slice(quad * QUAD, (quad + 1) * QUAD)
        ex = ex_ref[:, cols]
        xdt = act_ref[0, :, cols].astype(F32) * nn(dt2, ex)
        xdt_b = xdt.astype(BF16)
        xtail = (xdt * nn(tail2, ex)).astype(BF16)
        ece = nn(ec2, ex)
        parts = []
        for pair in range(2):
            heads = [quad * 4 + pair * 2, quad * 4 + pair * 2 + 1]
            mats = []
            for h in heads:
                diff = cum[:, h : h + 1] - cum_t[h : h + 1, :]
                mats.append((scores * jnp.exp(jnp.minimum(diff, 0.0))).astype(BF16))
            mat = jnp.concatenate(mats, axis=1)
            parts.append(nn(mat, block_pair(xdt_b[:, pair * LANES : (pair + 1) * LANES])))
        state = state_ref[:, cols]
        state_b = state.astype(BF16)
        st_ref[0, 0, :, cols] = state_b
        y_ref[0, :, cols] = jnp.concatenate(parts, axis=1) + ece * nn(cmat, state_b)
        new = state * ece[Q - 1 : Q, :] + nn(bmat_t, xtail)
        state_ref[:, cols] = new
        fin_ref[0, :, cols] = new


def scan_call(xbc, halo, raw, taps, bias, heads, ex, inner):
    seqs, length, width = xbc.shape
    chunks = length // Q
    whole = lambda s, c: (0, 0)
    row = lambda s, c: (s, c, 0)
    lanes = jax.ShapeDtypeStruct((seqs, length, LANES), F32)
    return pl.pallas_call(
        scan_kernel,
        grid=(seqs, chunks),
        in_specs=[
            pl.BlockSpec((1, Q, width), row),
            pl.BlockSpec((1, 16, width), lambda s, c: (s, jnp.maximum(c * (Q // 16) - 1, 0), 0)),
            pl.BlockSpec((1, 16, width), lambda s, c: (s, 0, 0)),
            pl.BlockSpec((1, Q, LANES), row),
            pl.BlockSpec(taps.shape, whole),
            pl.BlockSpec(bias.shape, whole),
            pl.BlockSpec(heads.shape, whole),
            pl.BlockSpec(ex.shape, whole),
        ],
        out_specs=[
            pl.BlockSpec((1, Q, width), row),
            pl.BlockSpec((1, Q, inner), row),
            pl.BlockSpec((1, Q, LANES), row),
            pl.BlockSpec((1, Q, LANES), row),
            pl.BlockSpec((1, Q, LANES), row),
            pl.BlockSpec((1, 1, STATE, inner), lambda s, c: (s, c, 0, 0)),
            pl.BlockSpec((1, STATE, inner), lambda s, c: (s, 0, 0)),
        ],
        out_shape=[
            jax.ShapeDtypeStruct((seqs, length, width), BF16),
            jax.ShapeDtypeStruct((seqs, length, inner), F32),
            lanes,
            lanes,
            lanes,
            jax.ShapeDtypeStruct((seqs, chunks, STATE, inner), BF16),
            jax.ShapeDtypeStruct((seqs, STATE, inner), F32),
        ],
        scratch_shapes=[
            pltpu.VMEM((Q + 8, width), F32),
            pltpu.VMEM((STATE, inner), F32),
            pltpu.VMEM((8, LANES), F32),
        ],
        compiler_params=pltpu.CompilerParams(vmem_limit_bytes=VMEM_LIMIT),
        cost_estimate=cost(seqs * length, 20),
        name="scan_forward",
    )(xbc, xbc, halo, raw, taps, bias, heads, ex)


def gate_kernel(
    y_ref, act_ref, z_ref, dev_ref, sin_ref, u_ref, c_ref, w_ref, vec_ref, ex_ref, red_ref,
    mixed_ref, dy_ref, dz_ref, norm_ref, rows_ref, q2_ref, sums_ref, ds_ref,
):
    s, i = pl.program_id(0), pl.program_id(1)
    inner = y_ref.shape[2]

    @pl.when(jnp.logical_and(s == 0, i == 0))
    def _():
        sums_ref[...] = jnp.zeros_like(sums_ref)

    @pl.when(i == 0)
    def _():
        ds_ref[...] = jnp.zeros_like(ds_ref)

    cmat = act_ref[0, :, inner + STATE : inner + 2 * STATE]
    ec2 = split2(jnp.exp(dev_ref[0]))
    ece = nn(ec2, ex_ref[...])
    x = act_ref[0, :, :inner].astype(F32)
    y_loc = y_ref[0]
    y_in = ece * nn(cmat, sin_ref[0])
    y = (y_loc + y_in + vec_ref[1:2, :] * x).astype(BF16).astype(F32)
    z = z_ref[0].astype(F32)
    sig = sigmoid(z)
    silu = z * sig
    g = y * silu
    scale = lax.rsqrt(jnp.mean(g * g, axis=1, keepdims=True) + EPS)
    gain = vec_ref[0:1, :]
    gs = g * scale
    normalized = (gs * gain).astype(BF16)
    norm_ref[0] = normalized
    mixed_ref[0] = (u_ref[0].astype(F32) + nn(normalized, w_ref[...])).astype(BF16)
    gn = nt(c_ref[0], w_ref[...])
    sums_ref[0:1, :] += jnp.sum(gn * gs, axis=0, keepdims=True)
    h = gn * gain
    dg = scale * (h - gs * jnp.mean(h * gs, axis=1, keepdims=True))
    dy_b = (dg * silu).astype(BF16)
    dy = dy_b.astype(F32)
    dy_ref[0] = dy_b
    dz_ref[0] = (dg * y * (sig + silu * (1.0 - sig))).astype(BF16)
    sums_ref[1:2, :] += jnp.sum(dy * x, axis=0, keepdims=True)
    rows = dy * y_loc
    high = rows.astype(BF16)
    rest = (rows - high.astype(F32)).astype(BF16)
    rows_ref[0] = nn(high, red_ref[...]) + nn(rest, red_ref[...])
    q2_ref[0] = nn((dy * y_in).astype(BF16), red_ref[...])
    ds_ref[0] += tn(cmat, (dy * ece).astype(BF16))


def gate_call(y, act, z, dev, s_in, u, cot, w_out, vecs, ex, red, rows):
    seqs, length, inner = y.shape
    width = act.shape[2]
    depth = u.shape[2]
    whole = lambda s, c: (0, 0)
    row = lambda s, c: (s, c, 0)
    per_seq = lambda s, c: (s, 0, 0)
    lanes = jax.ShapeDtypeStruct((seqs, length, LANES), F32)
    wide = jax.ShapeDtypeStruct((seqs, length, inner), BF16)
    return pl.pallas_call(
        gate_kernel,
        grid=(seqs, length // rows),
        in_specs=[
            pl.BlockSpec((1, rows, inner), row),
            pl.BlockSpec((1, rows, width), row),
            pl.BlockSpec((1, rows, inner), row),
            pl.BlockSpec((1, rows, LANES), row),
            pl.BlockSpec((1, STATE, inner), per_seq),
            pl.BlockSpec((1, rows, depth), row),
            pl.BlockSpec((1, rows, depth), row),
            pl.BlockSpec(w_out.shape, whole),
            pl.BlockSpec(vecs.shape, whole),
            pl.BlockSpec(ex.shape, whole),
            pl.BlockSpec(red.shape, whole),
        ],
        out_specs=[
            pl.BlockSpec((1, rows, depth), row),
            pl.BlockSpec((1, rows, inner), row),
            pl.BlockSpec((1, rows, inner), row),
            pl.BlockSpec((1, rows, inner), row),
            pl.BlockSpec((1, rows, LANES), row),
            pl.BlockSpec((1, rows, LANES), row),
            pl.BlockSpec((8, inner), whole),
            pl.BlockSpec((1, STATE, inner), per_seq),
        ],
        out_shape=[
            jax.ShapeDtypeStruct((seqs, length, depth), BF16),
            wide,
            wide,
            wide,
            lanes,
            lanes,
            jax.ShapeDtypeStruct((8, inner), F32),
            jax.ShapeDtypeStruct((seqs, STATE, inner), F32),
        ],
        compiler_params=pltpu.CompilerParams(vmem_limit_bytes=VMEM_LIMIT),
        cost_estimate=cost(seqs * length, 22),
        name="gate_and_output",
    )(y, act, z, dev, s_in, u, cot, w_out, vecs, ex, red)


def weights_kernel(norm_ref, c_ref, n_ref, dz_ref, gwo_ref, gwz_ref):
    @pl.when(jnp.logical_and(pl.program_id(0) == 0, pl.program_id(1) == 0))
    def _():
        gwo_ref[...] = jnp.zeros_like(gwo_ref)
        gwz_ref[...] = jnp.zeros_like(gwz_ref)

    gwo_ref[...] += tn(norm_ref[0], c_ref[0])
    gwz_ref[...] += tn(n_ref[0], dz_ref[0])


def weights_call(normalized, cot, normed, dz, rows):
    seqs, length, inner = dz.shape
    depth = cot.shape[2]
    whole = lambda s, c: (0, 0)
    row = lambda s, c: (s, c, 0)
    return pl.pallas_call(
        weights_kernel,
        grid=(seqs, length // rows),
        in_specs=[
            pl.BlockSpec((1, rows, inner), row),
            pl.BlockSpec((1, rows, depth), row),
            pl.BlockSpec((1, rows, depth), row),
            pl.BlockSpec((1, rows, inner), row),
        ],
        out_specs=[pl.BlockSpec((inner, depth), whole), pl.BlockSpec((depth, inner), whole)],
        out_shape=[
            jax.ShapeDtypeStruct((inner, depth), F32),
            jax.ShapeDtypeStruct((depth, inner), F32),
        ],
        compiler_params=pltpu.CompilerParams(vmem_limit_bytes=VMEM_LIMIT),
        cost_estimate=cost(seqs * length, 8),
        name="weight_gradients",
    )(normalized, cot, normed, dz)


def back_kernel(
    act_ref, dy_ref, dt_ref, cum_ref, dev_ref, st_ref, sin_ref, rows_ref, vec_ref, ex_ref, red_ref,
    g_ref, direct_ref, da_ref,
    ds_ref,
):
    inner = dy_ref.shape[2]

    @pl.when(pl.program_id(1) == 0)
    def _():
        ds_ref[...] = jnp.zeros_like(ds_ref)

    bmat = act_ref[0, :, inner : inner + STATE]
    cmat = act_ref[0, :, inner + STATE : inner + 2 * STATE]
    cmat_t = cmat.astype(F32).T.astype(BF16)
    row, col = iotas(Q, Q)
    upper = row <= col
    scores = jnp.where(upper, nt(bmat, cmat), 0.0)
    cum = cum_ref[0]
    cum_t = cum.T
    dt2 = split2(dt_ref[0])
    ec2 = split2(jnp.exp(cum))
    tail2 = split2(jnp.exp(cum[Q - 1 : Q, :] - cum))
    before2 = split2(jnp.exp(dev_ref[0, 0:8, :] - cum[0:8, :]))

    d_scores = jnp.zeros((Q, Q), F32)
    db = jnp.zeros((Q, STATE), F32)
    dc = jnp.zeros((Q, STATE), F32)
    direct = jnp.zeros((Q, LANES), F32)
    col_sums = jnp.zeros((Q, LANES), F32)
    w_loc = jnp.zeros((Q, LANES), F32)
    const = jnp.zeros((8, LANES), F32)
    for quad in range(inner // QUAD):
        cols = slice(quad * QUAD, (quad + 1) * QUAD)
        ex = ex_ref[:, cols]
        red = red_ref[cols, :]
        dte = nn(dt2, ex)
        tle = nn(tail2, ex)
        ece = nn(ec2, ex)
        x = act_ref[0, :, cols].astype(F32)
        xdt_b = (x * dte).astype(BF16)
        xdt = xdt_b.astype(F32)
        dy_b = dy_ref[0, :, cols]
        dy = dy_b.astype(F32)
        parts = []
        for pair in range(2):
            lanes = slice(pair * LANES, (pair + 1) * LANES)
            stacked = block_pair(dy_b[:, lanes])
            d_mat = nt(xdt_b[:, lanes], stacked)
            mats = []
            for j in range(2):
                h = quad * 4 + pair * 2 + j
                decay = jnp.exp(jnp.minimum(cum_t[h : h + 1, :] - cum[:, h : h + 1], 0.0))
                mats.append((scores * decay).astype(BF16))
                d_scores = d_scores + d_mat[:, j * Q : (j + 1) * Q] * decay
            parts.append(nn(jnp.concatenate(mats, axis=1), stacked))
        ds = ds_ref[:, cols]
        ds_b = ds.astype(BF16)
        st = st_ref[0, 0, :, cols].astype(F32)
        before = nn(before2, ex)[0:1, :]
        state_b = (st + before * sin_ref[0, :, cols].astype(F32)).astype(BF16)
        dx_intra = jnp.concatenate(parts, axis=1)
        dx_inter = tle * nn(bmat, ds_b)
        dxp = dx_intra + dx_inter
        g_ref[0, :, cols] = dte * dxp + vec_ref[1:2, cols] * dy
        direct = direct + nn((x * dxp).astype(BF16), red)
        prod = xdt * dx_intra
        high = prod.astype(BF16)
        col_sums = col_sums + nn(high, red) + nn((prod - high.astype(F32)).astype(BF16), red)
        w_loc = w_loc + nn((xdt * dx_inter).astype(BF16), red)
        db = db + nt((xdt * tle).astype(BF16), ds_b)
        dye = (dy * ece).astype(BF16)
        dc = dc + nt(dye, state_b)
        last = ece[Q - 1 : Q, :]
        both = jnp.sum(st * ds, axis=0, keepdims=True) * last
        both = jnp.broadcast_to(both, (8, QUAD))
        high = both.astype(BF16)
        const = const + nn(high, red) + nn((both - high.astype(F32)).astype(BF16), red)
        ds_ref[:, cols] = ds * last + nn(cmat_t, dye)
    d_scores = jnp.where(upper, d_scores, 0.0)
    g_ref[0, :, inner : inner + STATE] = db + nn(d_scores.astype(BF16), cmat)
    g_ref[0, :, inner + STATE :] = dc + nn(d_scores.T.astype(BF16), bmat)
    direct_ref[0] = direct
    da_ref[0] = (
        exact(upper.astype(F32), rows_ref[0] - col_sums)
        + exact((row > col).astype(F32), w_loc)
        + const[0:1, :]
    )


def back_call(act, dy, dts, cum, dev, states, s_in, rows, vecs, ex, red):
    seqs, length, width = act.shape
    inner = dy.shape[2]
    chunks = length // Q
    whole = lambda s, c: (0, 0)
    row = lambda s, c: (s, chunks - 1 - c, 0)
    lanes = jax.ShapeDtypeStruct((seqs, length, LANES), F32)
    lane_block = pl.BlockSpec((1, Q, LANES), row)
    return pl.pallas_call(
        back_kernel,
        grid=(seqs, chunks),
        in_specs=[
            pl.BlockSpec((1, Q, width), row),
            pl.BlockSpec((1, Q, inner), row),
            lane_block,
            lane_block,
            lane_block,
            pl.BlockSpec((1, 1, STATE, inner), lambda s, c: (s, chunks - 1 - c, 0, 0)),
            pl.BlockSpec((1, STATE, inner), lambda s, c: (s, 0, 0)),
            lane_block,
            pl.BlockSpec(vecs.shape, whole),
            pl.BlockSpec(ex.shape, whole),
            pl.BlockSpec(red.shape, whole),
        ],
        out_specs=[pl.BlockSpec((1, Q, width), row), lane_block, lane_block],
        out_shape=[jax.ShapeDtypeStruct((seqs, length, width), F32), lanes, lanes],
        scratch_shapes=[pltpu.VMEM((STATE, inner), F32)],
        compiler_params=pltpu.CompilerParams(vmem_limit_bytes=VMEM_LIMIT),
        cost_estimate=cost(seqs * length, 29),
        name="scan_backward",
    )(act, dy, dts, cum, dev, states, s_in, rows, vecs, ex, red)


def finish_kernel(
    g_ref, act_ref, xbc_ref, prev_ref, halo_ref, raw_ref, dt_ref, dev_ref, tot_ref, ds_ref, q2_ref,
    direct_ref, da_ref, c4_ref, taps_ref, bias_ref, heads_ref, ex_ref, red_ref,
    gconv_ref, gdt_ref, taps_sum_ref, heads_sum_ref,
    ext_ref, carry_ref,
):
    s, c = pl.program_id(0), pl.program_id(1)
    width = xbc_ref.shape[2]
    inner = ds_ref.shape[2]
    rows = xbc_ref.shape[1]

    @pl.when(jnp.logical_and(s == 0, c == 0))
    def _():
        taps_sum_ref[...] = jnp.zeros_like(taps_sum_ref)
        heads_sum_ref[...] = jnp.zeros_like(heads_sum_ref)

    @pl.when(c == 0)
    def _():
        carry_ref[...] = jnp.zeros_like(carry_ref)

    fill_ext(ext_ref, xbc_ref, prev_ref, halo_ref, c == 0)

    def conv_back(grad, cols):
        conv = conv_columns(ext_ref, taps_ref, bias_ref, cols, rows)
        sig = sigmoid(conv)
        out = grad * (sig + conv * sig * (1.0 - sig))
        gconv_ref[0, :, cols] = out
        for k in range(4):
            taps_sum_ref[k : k + 1, cols] += jnp.sum(
                out * ext_ref[pl.ds(5 + k, rows), cols], axis=0, keepdims=True
            )
        taps_sum_ref[4:5, cols] += jnp.sum(out, axis=0, keepdims=True)

    bmat = act_ref[0, :, inner : inner + STATE]
    dts = dt_ref[0]
    dt2 = split2(dts)
    tail2 = split2(jnp.exp(tot_ref[0, 0:1, :] - dev_ref[0]))
    db = jnp.zeros((rows, STATE), F32)
    direct = direct_ref[0]
    q3 = jnp.zeros((rows, LANES), F32)
    for quad in range(inner // QUAD):
        cols = slice(quad * QUAD, (quad + 1) * QUAD)
        ex = ex_ref[:, cols]
        red = red_ref[cols, :]
        dte = nn(dt2, ex)
        tle = nn(tail2, ex)
        x = act_ref[0, :, cols].astype(F32)
        xdt = (x * dte).astype(BF16).astype(F32)
        ds_b = ds_ref[0, :, cols]
        dxc = tle * nn(bmat, ds_b)
        direct = direct + nn((x * dxc).astype(BF16), red)
        q3 = q3 + nn((xdt * dxc).astype(BF16), red)
        db = db + nt((xdt * tle).astype(BF16), ds_b)
        conv_back(g_ref[0, :, cols] + dte * dxc, cols)
    db_all = jnp.concatenate([db, jnp.zeros_like(db)], axis=1)
    cols = slice(inner, inner + QUAD)
    conv_back(g_ref[0, :, cols] + db_all, cols)

    step = q3 - q2_ref[0]
    row, col = iotas(rows, rows)
    prefix = exact((row > col).astype(F32), step) + carry_ref[0:1, :]
    carry_ref[...] = carry_ref[...] + jnp.sum(step, axis=0, keepdims=True)
    da = da_ref[0] + c4_ref[0, 0:1, :] + prefix
    rate = heads_ref[1:2, :]
    raw = raw_ref[0].astype(F32) + heads_ref[0:1, :]
    grad = (direct + rate * da) * sigmoid(raw) * heads_ref[3:4, :]
    gdt_ref[0] = grad.astype(BF16)
    heads_sum_ref[0:1, :] += jnp.sum(grad, axis=0, keepdims=True)
    heads_sum_ref[1:2, :] += jnp.sum(da * dts, axis=0, keepdims=True) * rate


def finish_call(
    grad, act, xbc, halo, raw, dts, dev, tot, ds_end, q2, direct, da, c4, taps, bias, heads, ex, red,
    rows,
):
    seqs, length, width = xbc.shape
    inner = ds_end.shape[2]
    whole = lambda s, c: (0, 0)
    row = lambda s, c: (s, c, 0)
    per_seq = lambda s, c: (s, 0, 0)
    lane_block = pl.BlockSpec((1, rows, LANES), row)
    wide_block = pl.BlockSpec((1, rows, width), row)
    return pl.pallas_call(
        finish_kernel,
        grid=(seqs, length // rows),
        in_specs=[
            wide_block,
            wide_block,
            wide_block,
            pl.BlockSpec((1, 16, width), lambda s, c: (s, jnp.maximum(c * (rows // 16) - 1, 0), 0)),
            pl.BlockSpec((1, 16, width), per_seq),
            lane_block,
            lane_block,
            lane_block,
            pl.BlockSpec((1, 8, LANES), per_seq),
            pl.BlockSpec((1, STATE, inner), per_seq),
            lane_block,
            lane_block,
            lane_block,
            pl.BlockSpec((1, 8, LANES), per_seq),
            pl.BlockSpec(taps.shape, whole),
            pl.BlockSpec(bias.shape, whole),
            pl.BlockSpec(heads.shape, whole),
            pl.BlockSpec(ex.shape, whole),
            pl.BlockSpec(red.shape, whole),
        ],
        out_specs=[
            wide_block,
            lane_block,
            pl.BlockSpec((8, width), whole),
            pl.BlockSpec((8, LANES), whole),
        ],
        out_shape=[
            jax.ShapeDtypeStruct((seqs, length, width), F32),
            jax.ShapeDtypeStruct((seqs, length, LANES), BF16),
            jax.ShapeDtypeStruct((8, width), F32),
            jax.ShapeDtypeStruct((8, LANES), F32),
        ],
        scratch_shapes=[pltpu.VMEM((rows + 8, width), F32), pltpu.VMEM((8, LANES), F32)],
        compiler_params=pltpu.CompilerParams(vmem_limit_bytes=VMEM_LIMIT),
        cost_estimate=cost(seqs * length, 21),
        name="conv_backward",
    )(
        grad, act, xbc, xbc, halo, raw, dts, dev, tot, ds_end, q2, direct, da, c4, taps, bias, heads,
        ex, red,
    )


def taps_back_kernel(
    g_ref, next_ref, after_ref, gdt_ref, normed_ref, taps_ref,
    gx_ref, gw_ref,
    ext_ref,
):
    s, c = pl.program_id(0), pl.program_id(1)
    rows, width = g_ref.shape[1], g_ref.shape[2]

    @pl.when(jnp.logical_and(s == 0, c == 0))
    def _():
        gw_ref[...] = jnp.zeros_like(gw_ref)

    ext_ref[0:rows, :] = g_ref[0]
    ext_ref[rows : rows + 8, :] = jnp.where(c == pl.num_programs(1) - 1, after_ref[0], next_ref[0])
    for start in range(0, width, QUAD):
        cols = slice(start, start + QUAD)
        total = taps_ref[3:4, cols] * ext_ref[pl.ds(0, rows), cols]
        for k in range(3):
            total = total + taps_ref[k : k + 1, cols] * ext_ref[pl.ds(3 - k, rows), cols]
        gx_ref[0, :, cols] = total.astype(BF16)
    gx_ref[0, :, width:] = gdt_ref[0]
    gw_ref[...] += tn(normed_ref[0], gx_ref[0])


def taps_back_call(gconv, after, gdt, normed, taps, rows):
    seqs, length, width = gconv.shape
    depth = normed.shape[2]
    whole = lambda s, c: (0, 0)
    row = lambda s, c: (s, c, 0)
    last = length // 8 - 1
    return pl.pallas_call(
        taps_back_kernel,
        grid=(seqs, length // rows),
        in_specs=[
            pl.BlockSpec((1, rows, width), row),
            pl.BlockSpec(
                (1, 8, width), lambda s, c: (s, jnp.minimum((c + 1) * (rows // 8), last), 0)
            ),
            pl.BlockSpec((1, 8, width), lambda s, c: (s, 0, 0)),
            pl.BlockSpec((1, rows, LANES), row),
            pl.BlockSpec((1, rows, depth), row),
            pl.BlockSpec(taps.shape, whole),
        ],
        out_specs=[
            pl.BlockSpec((1, rows, width + LANES), row),
            pl.BlockSpec((depth, width + LANES), whole),
        ],
        out_shape=[
            jax.ShapeDtypeStruct((seqs, length, width + LANES), BF16),
            jax.ShapeDtypeStruct((depth, width + LANES), F32),
        ],
        scratch_shapes=[pltpu.VMEM((rows + 8, width), F32)],
        compiler_params=pltpu.CompilerParams(vmem_limit_bytes=VMEM_LIMIT),
        cost_estimate=cost(seqs * length, 9),
        name="taps_backward",
    )(gconv, gconv, after, gdt, normed, taps)


def input_kernel(dz_ref, gx_ref, wz_ref, wx_ref, u_ref, c_ref, gain_ref, out_ref, sum_ref):
    @pl.when(jnp.logical_and(pl.program_id(0) == 0, pl.program_id(1) == 0))
    def _():
        sum_ref[...] = jnp.zeros_like(sum_ref)

    grad = nt(dz_ref[0], wz_ref[...]) + nt(gx_ref[0], wx_ref[...])
    u = u_ref[0].astype(F32)
    scale = lax.rsqrt(jnp.mean(u * u, axis=1, keepdims=True) + EPS)
    us = u * scale
    sum_ref[0:1, :] += jnp.sum(grad * us, axis=0, keepdims=True)
    h = grad * gain_ref[0:1, :]
    back = scale * (h - us * jnp.mean(h * us, axis=1, keepdims=True))
    out_ref[0] = c_ref[0].astype(F32) + back


def input_call(dz, gx, w_z, w_x, u, cot, gain, rows):
    seqs, length, depth = u.shape
    whole = lambda s, c: (0, 0)
    row = lambda s, c: (s, c, 0)
    return pl.pallas_call(
        input_kernel,
        grid=(seqs, length // rows),
        in_specs=[
            pl.BlockSpec((1, rows, dz.shape[2]), row),
            pl.BlockSpec((1, rows, gx.shape[2]), row),
            pl.BlockSpec(w_z.shape, whole),
            pl.BlockSpec(w_x.shape, whole),
            pl.BlockSpec((1, rows, depth), row),
            pl.BlockSpec((1, rows, depth), row),
            pl.BlockSpec(gain.shape, whole),
        ],
        out_specs=[pl.BlockSpec((1, rows, depth), row), pl.BlockSpec((8, depth), whole)],
        out_shape=[
            jax.ShapeDtypeStruct((seqs, length, depth), F32),
            jax.ShapeDtypeStruct((8, depth), F32),
        ],
        compiler_params=pltpu.CompilerParams(vmem_limit_bytes=VMEM_LIMIT),
        cost_estimate=cost(seqs * length, 9),
        name="input_gradient",
    )(dz, gx, w_z, w_x, u, cot, gain)


def to_all(value, size, axes):
    copies = jnp.broadcast_to(value[None], (size,) + value.shape)
    return lax.all_to_all(copies, axes, split_axis=0, concat_axis=0, tiled=True)


def other_core(value, sizes):
    return lax.ppermute(value, "dp", [(i, i ^ 1) for i in range(sizes["dp"])])


def both_cores(value, sizes, axis):
    other = other_core(value, sizes)
    first = lax.axis_index("dp") % 2 == 0
    return jnp.where(first, jnp.stack([value, other], axis), jnp.stack([other, value], axis))


def core_half(shard):
    half = shard.shape[0] // 2
    return lax.dynamic_slice_in_dim(shard, (lax.axis_index("dp") % 2) * half, half, 0)


def gather_rows(shard, sizes):
    got = to_all(core_half(shard), sizes["seq"], "seq").reshape(sizes["seq"], -1, shard.shape[1])
    return both_cores(got, sizes, 1).reshape(sizes["seq"] * shard.shape[0], shard.shape[1])


def gather_later(shards, sizes):
    columns = max(shard.shape[1] for shard in shards)
    halves = [core_half(shard).reshape(-1, columns) for shard in shards]
    got = lax.all_gather(jnp.concatenate(halves, axis=0), "seq", axis=0)
    other = other_core(got, sizes)
    first = lax.axis_index("dp") % 2 == 0
    outs, at = [], 0
    for shard, half in zip(shards, halves):
        rows = slice(at, at + half.shape[0])
        at += half.shape[0]
        mine, away = got[:, rows], other[:, rows]
        pair = jnp.where(first, jnp.stack([mine, away], 1), jnp.stack([away, mine], 1))
        outs.append(pair.reshape(sizes["seq"] * shard.shape[0], shard.shape[1]))
    return outs


def scatter_rows(grads, sizes):
    size = sizes["seq"]
    core = lax.axis_index("dp") % 2
    columns = max(grad.shape[1] for grad in grads)
    halves = []
    for grad in grads:
        parts = grad.reshape(size, 2, -1, grad.shape[1])
        mine = lax.dynamic_index_in_dim(parts, core, 1, keepdims=False)
        away = lax.dynamic_index_in_dim(parts, 1 - core, 1, keepdims=False).astype(BF16)
        half = (mine + other_core(away, sizes).astype(F32)).astype(BF16)
        halves.append(half.reshape(size, -1, columns))
    return lax.all_to_all(
        jnp.concatenate(halves, axis=1), "seq", split_axis=0, concat_axis=0, tiled=True
    )


def add_rows(got, shapes, sizes):
    total = got.astype(F32).sum(axis=0)
    step = 2
    while step < sizes["dp"]:
        total = total + lax.ppermute(total, "dp", [(i, i ^ step) for i in range(sizes["dp"])])
        step *= 2
    pair = both_cores(total, sizes, 0)
    outs, at = [], 0
    for rows, columns in shapes:
        count = rows * columns // (2 * sizes["seq"] * total.shape[1])
        outs.append(pair[:, at : at + count].reshape(rows // sizes["seq"], columns))
        at += count
    return outs


def sum_small(values, sizes):
    flat = jnp.concatenate([value.reshape(-1) for value in values])
    count = flat.shape[0]
    flat = jnp.pad(flat, (0, -count % 1024)).reshape(-1, LANES)
    for axis in ("dp", "seq"):
        step = 1
        while step < sizes[axis]:
            flat = flat + lax.ppermute(flat, axis, [(i, i ^ step) for i in range(sizes[axis])])
            step *= 2
    flat = flat.reshape(-1)
    out, at = [], 0
    for value in values:
        out.append(flat[at : at + value.size].reshape(value.shape))
        at += value.size
    return out


def shift_in(value, size, step):
    pairs = [(i, i + step) for i in range(size) if 0 <= i + step < size]
    return lax.ppermute(value, "seq", pairs)


def carry_over(states, decay, size, step, beside):
    seqs, depth, inner = states.shape
    piece = depth // size
    sent = states.astype(BF16).reshape(seqs, size, piece, inner)
    got = lax.all_to_all(sent, "seq", split_axis=1, concat_axis=1, tiled=True)
    got, beside = lax.optimization_barrier((got, beside))
    got = got.astype(F32)
    order = range(size) if step > 0 else range(size - 1, -1, -1)
    held = jnp.zeros((seqs, piece, inner), F32)
    into = [None] * size
    for i in order:
        into[i] = held
        held = held * decay[i][:, None, :] + got[:, i]
    back = jnp.stack(into, axis=1).astype(BF16)
    back = lax.all_to_all(back, "seq", split_axis=1, concat_axis=1, tiled=True)
    return back.reshape(seqs, depth, inner), beside


def rms_gain(values, gain):
    return values * lax.rsqrt(jnp.mean(values * values, axis=-1, keepdims=True) + EPS) * gain


def body(
    sizes, inputs, w_in, w_out, norm_gain, conv_weight, conv_bias, dt_bias, a_log, skip, gate_gain,
    cotangent,
):
    size = sizes["seq"]
    seqs, length, depth = inputs.shape
    inner = gate_gain.shape[0]
    width = conv_weight.shape[1]
    tokens = seqs * length
    rows = min(256, length)

    w_x = gather_rows(jnp.pad(w_in[:, inner:], ((0, 0), (0, LANES - HEADS))), sizes)
    w_z, full_out = gather_later([w_in[:, :inner], w_out], sizes)

    def pad_heads(values):
        return jnp.pad(values, (0, LANES - HEADS))

    rates = -jnp.exp(a_log)
    heads = jnp.stack([pad_heads(dt_bias), pad_heads(rates), pad_heads(skip), pad_heads(jnp.ones_like(skip))])
    heads = jnp.pad(heads, ((0, 4), (0, 0)))
    taps = jnp.pad(conv_weight, ((0, 4), (0, 0)))
    bias = jnp.pad(conv_bias[None, :], ((0, 7), (0, 0)))
    vecs = jnp.pad(jnp.stack([gate_gain, jnp.repeat(skip, HEADDIM)]), ((0, 6), (0, 0)))
    ex, red = head_matrices(inner)

    edge = shift_in(inputs[:, length - 16 :], size, 1).astype(F32)
    edge = rms_gain(edge, norm_gain).astype(BF16).reshape(seqs * 16, depth)
    normed = rms_gain(inputs.astype(F32), norm_gain).astype(BF16)
    flat = normed.reshape(tokens, depth)

    def project(left, matrix):
        return jnp.dot(left, matrix, preferred_element_type=F32).astype(BF16)

    halo = project(edge, w_x)[:, :width].reshape(seqs, 16, width)
    xbc = project(flat, w_x[:, :width]).reshape(seqs, length, width)
    raw = project(flat, w_x[:, width:]).reshape(seqs, length, LANES)

    total = (softplus(raw.astype(F32) + heads[0]) * heads[3]).sum(axis=1) * heads[1]
    decay = jnp.exp(to_all(total, size, "seq").reshape(size, seqs, LANES)[:, :, :HEADS])
    decay = jnp.repeat(decay, HEADDIM, axis=2)
    act, y, dts, cum, dev, states, final = scan_call(xbc, halo, raw, taps, bias, heads, ex, inner)
    final, decay = lax.optimization_barrier((final, decay))
    z = project(flat, w_z).reshape(seqs, length, inner)
    s_in, z = carry_over(final, decay, size, 1, z)

    mixed, dy, dz, normalized, row_sums, q2, gate_sums, ds_loc = gate_call(
        y, act, z, dev, s_in, inputs, cotangent, full_out, vecs, ex, red, rows
    )
    grad_out, grad_z = weights_call(normalized, cotangent, normed, dz, min(512, length))
    ds_end, weight_grads = carry_over(ds_loc, decay, size, -1, (grad_out, grad_z))
    got_zo = scatter_rows(weight_grads, sizes)

    grad, direct, da = back_call(act, dy, dts, cum, dev, states, s_in, row_sums, vecs, ex, red)

    both = (s_in.astype(F32) * ds_end.astype(F32)).sum(axis=1).reshape(seqs, HEADS, HEADDIM).sum(axis=2)
    both = jnp.pad(both, ((0, 0), (0, LANES - HEADS))) * jnp.exp(total)
    c4 = jnp.broadcast_to((both + q2.sum(axis=1))[:, None, :], (seqs, 8, LANES))
    tot = jnp.broadcast_to(total[:, None, :], (seqs, 8, LANES))
    gconv, gdt, taps_sum, heads_sum = finish_call(
        grad, act, xbc, halo, raw, dts, dev, tot, ds_end, q2, direct, da, c4, taps, bias, heads, ex,
        red, rows,
    )
    gconv, got_zo = lax.optimization_barrier((gconv, got_zo))
    after = shift_in(gconv[:, :8], size, -1)
    rows_out, rows_z = add_rows(got_zo, [grad_out.shape, grad_z.shape], sizes)
    gx, grad_x = taps_back_call(gconv, after, gdt, normed, taps, rows)
    (rows_x,) = add_rows(scatter_rows([grad_x], sizes), [grad_x.shape], sizes)
    gain = jnp.pad(norm_gain[None, :], ((0, 7), (0, 0)))
    grad_inputs, gain_sum = input_call(dz, gx, w_z, w_x, inputs, cotangent, gain, rows)
    sums = sum_small(
        (
            gain_sum[0],
            taps_sum[:4],
            taps_sum[4],
            heads_sum[0, :HEADS],
            heads_sum[1, :HEADS],
            gate_sums[1].reshape(HEADS, HEADDIM).sum(axis=1),
            gate_sums[0],
        ),
        sizes,
    )


    rows_in = jnp.concatenate([rows_z, rows_x[:, : width + HEADS]], axis=1)
    return (mixed, grad_inputs, rows_in, rows_out, *sums)


def solution(mesh):
    placed = (
        P("dp", "seq", None),
        P("seq", None),
        P("seq", None),
        P(),
        P(),
        P(),
        P(),
        P(),
        P(),
        P(),
        P("dp", "seq", None),
    )
    return jax.shard_map(
        functools.partial(body, dict(mesh.shape)),
        mesh=mesh,
        in_specs=placed,
        out_specs=(
            P("dp", "seq", None),
            P("dp", "seq", None),
            P("seq", None),
            P("seq", None),
            P(),
            P(),
            P(),
            P(),
            P(),
            P(),
            P(),
        ),
        check_vma=False,
    )
```

```python
import functools

import jax
import jax.numpy as jnp
from jax import lax
from jax.experimental import pallas as pl
from jax.experimental.pallas import tpu as pltpu
from jax.sharding import PartitionSpec as P

HEADS = 24
HEADDIM = 64
STATE = 128
LANES = 128
Q = 128
SUB = 2
QUAD = 256
EPS = 1e-05
F32 = jnp.float32
BF16 = jnp.bfloat16
VMEM_LIMIT = 56 * 1024 * 1024


def cost(tokens, per_token_ns):
    seconds = tokens * per_token_ns * 1e-9
    return pl.CostEstimate(
        flops=int(seconds * 1e15), bytes_accessed=int(seconds * 3e12), transcendentals=0
    )


def dot(left, right, dims):
    return lax.dot_general(left, right, (dims, ((), ())), preferred_element_type=F32)


def nn(left, right):
    return dot(left, right, ((1,), (0,)))


def nt(left, right):
    return dot(left, right, ((1,), (1,)))


def tn(left, right):
    return dot(left, right, ((0,), (0,)))


def exact(left, right):
    return lax.dot_general(
        left, right, (((1,), (0,)), ((), ())), precision=lax.Precision.HIGHEST,
        preferred_element_type=F32,
    )


def split2(values):
    high = values.astype(BF16)
    rest = (values - high.astype(F32)).astype(BF16)
    return jnp.concatenate([high, rest], axis=1)


def sigmoid(values):
    return 0.5 + 0.5 * jnp.tanh(0.5 * values)


def softplus(values):
    return jnp.maximum(values, 0.0) + jnp.log1p(jnp.exp(-jnp.abs(values)))


def iotas(rows, cols):
    return (
        lax.broadcasted_iota(jnp.int32, (rows, cols), 0),
        lax.broadcasted_iota(jnp.int32, (rows, cols), 1),
    )


def head_matrices(inner):
    col_head = jnp.arange(inner) // HEADDIM
    expand = (jnp.arange(LANES)[:, None] == col_head[None, :]).astype(BF16)
    return jnp.concatenate([expand, expand], axis=0), expand.T


def block_pair(pair):
    low = lax.broadcasted_iota(jnp.int32, pair.shape, 1) < HEADDIM
    zero = jnp.zeros_like(pair)
    return jnp.concatenate([jnp.where(low, pair, zero), jnp.where(low, zero, pair)], axis=0)


def shifted(ext_ref, start, rows):
    block = start // LANES
    return [ext_ref[block, pl.ds(5 + k, rows), :] for k in range(4)]


def conv_columns(views, taps_ref, bias_ref, cols):
    total = bias_ref[0:1, cols] + taps_ref[0:1, cols] * views[0]
    for k in range(1, 4):
        total = total + taps_ref[k : k + 1, cols] * views[k]
    return total


def fill_ext(ext_ref, xbc_ref, prev_ref, halo_ref, first):
    rows = xbc_ref.shape[1]
    for block in range(ext_ref.shape[0]):
        cols = slice(block * LANES, (block + 1) * LANES)
        before = jnp.where(
            first, halo_ref[0, :, cols].astype(F32), prev_ref[0, :, cols].astype(F32)
        )
        ext_ref[block, 0:8, :] = before[8:16]
        ext_ref[block, pl.ds(8, rows), :] = xbc_ref[0, :, cols].astype(F32)


def scan_kernel(
    xbc_ref, prev_ref, halo_ref, raw_ref, taps_ref, bias_ref, heads_ref, ex_ref,
    act_ref, y_ref, dt_ref, cum_ref, dev_ref, st_ref, fin_ref,
    ext_ref, state_ref, carry_ref,
):
    c = pl.program_id(1)
    rows, width = xbc_ref.shape[1], xbc_ref.shape[2]
    inner = y_ref.shape[2]

    @pl.when(c == 0)
    def _():
        state_ref[...] = jnp.zeros_like(state_ref)
        carry_ref[...] = jnp.zeros_like(carry_ref)

    fill_ext(ext_ref, xbc_ref, prev_ref, halo_ref, c == 0)
    for start in range(0, width, LANES):
        cols = slice(start, start + LANES)
        half = 0.5 * conv_columns(shifted(ext_ref, start, rows), taps_ref, bias_ref, cols)
        act_ref[0, :, cols] = (half + half * jnp.tanh(half)).astype(BF16)

    row, col = iotas(Q, Q)
    lower = row >= col
    before = carry_ref[0:1, :]
    held = []
    for sub in range(rows // Q):
        at = slice(sub * Q, (sub + 1) * Q)
        dts = softplus(raw_ref[0, at].astype(F32) + heads_ref[0:1, :]) * heads_ref[3:4, :]
        cum = exact(lower.astype(F32), dts * heads_ref[1:2, :])
        dt_ref[0, at] = dts
        cum_ref[0, at] = cum
        dev_ref[0, at] = cum + before
        before = before + cum[Q - 1 : Q, :]
        bmat = act_ref[0, at, inner : inner + STATE]
        cmat = act_ref[0, at, inner + STATE : inner + 2 * STATE]
        held.append((
            at, cum, cum.T, split2(dts), split2(jnp.exp(cum)),
            split2(jnp.exp(cum[Q - 1 : Q, :] - cum)), cmat, bmat.astype(F32).T.astype(BF16),
            jnp.where(lower, nt(cmat, bmat), 0.0),
        ))
    carry_ref[...] = jnp.broadcast_to(before, carry_ref.shape)

    for quad in range(inner // QUAD):
        cols = slice(quad * QUAD, (quad + 1) * QUAD)
        ex = ex_ref[:, cols]
        state = state_ref[:, cols]
        for sub, (at, cum, cum_t, dt2, ec2, tail2, cmat, bmat_t, scores) in enumerate(held):
            xdt = act_ref[0, at, cols].astype(F32) * nn(dt2, ex)
            xdt_b = xdt.astype(BF16)
            xtail = (xdt * nn(tail2, ex)).astype(BF16)
            ece = nn(ec2, ex)
            parts = []
            for pair in range(2):
                mats = []
                for h in (quad * 4 + pair * 2, quad * 4 + pair * 2 + 1):
                    diff = cum[:, h : h + 1] - cum_t[h : h + 1, :]
                    mats.append((scores * jnp.exp(jnp.minimum(diff, 0.0))).astype(BF16))
                mat = jnp.concatenate(mats, axis=1)
                parts.append(nn(mat, block_pair(xdt_b[:, pair * LANES : (pair + 1) * LANES])))
            state_b = state.astype(BF16)
            st_ref[0, sub, :, cols] = state_b
            y_ref[0, at, cols] = jnp.concatenate(parts, axis=1) + ece * nn(cmat, state_b)
            state = state * ece[Q - 1 : Q, :] + nn(bmat_t, xtail)
        state_ref[:, cols] = state
        fin_ref[0, :, cols] = state


def scan_call(xbc, halo, raw, taps, bias, heads, ex, inner):
    seqs, length, width = xbc.shape
    chunks = length // Q
    rows = SUB * Q
    whole = lambda s, c: (0, 0)
    row = lambda s, c: (s, c, 0)
    lanes = jax.ShapeDtypeStruct((seqs, length, LANES), F32)
    return pl.pallas_call(
        scan_kernel,
        grid=(seqs, length // rows),
        in_specs=[
            pl.BlockSpec((1, rows, width), row),
            pl.BlockSpec((1, 16, width), lambda s, c: (s, jnp.maximum(c * (rows // 16) - 1, 0), 0)),
            pl.BlockSpec((1, 16, width), lambda s, c: (s, 0, 0)),
            pl.BlockSpec((1, rows, LANES), row),
            pl.BlockSpec(taps.shape, whole),
            pl.BlockSpec(bias.shape, whole),
            pl.BlockSpec(heads.shape, whole),
            pl.BlockSpec(ex.shape, whole),
        ],
        out_specs=[
            pl.BlockSpec((1, rows, width), row),
            pl.BlockSpec((1, rows, inner), row),
            pl.BlockSpec((1, rows, LANES), row),
            pl.BlockSpec((1, rows, LANES), row),
            pl.BlockSpec((1, rows, LANES), row),
            pl.BlockSpec((1, SUB, STATE, inner), lambda s, c: (s, c, 0, 0)),
            pl.BlockSpec((1, STATE, inner), lambda s, c: (s, 0, 0)),
        ],
        out_shape=[
            jax.ShapeDtypeStruct((seqs, length, width), BF16),
            jax.ShapeDtypeStruct((seqs, length, inner), F32),
            lanes,
            lanes,
            lanes,
            jax.ShapeDtypeStruct((seqs, chunks, STATE, inner), BF16),
            jax.ShapeDtypeStruct((seqs, STATE, inner), F32),
        ],
        scratch_shapes=[
            pltpu.VMEM((width // LANES, rows + 8, LANES), F32),
            pltpu.VMEM((STATE, inner), F32),
            pltpu.VMEM((8, LANES), F32),
        ],
        compiler_params=pltpu.CompilerParams(vmem_limit_bytes=VMEM_LIMIT),
        cost_estimate=cost(seqs * length, 20),
        name="scan_forward",
    )(xbc, xbc, halo, raw, taps, bias, heads, ex)


def gate_kernel(
    y_ref, act_ref, z_ref, dev_ref, sin_ref, u_ref, c_ref, w_ref, vec_ref, ex_ref, red_ref,
    mixed_ref, dy_ref, dz_ref, norm_ref, rows_ref, q2_ref, sums_ref, ds_ref,
):
    s, i = pl.program_id(0), pl.program_id(1)
    inner = y_ref.shape[2]

    @pl.when(jnp.logical_and(s == 0, i == 0))
    def _():
        sums_ref[...] = jnp.zeros_like(sums_ref)

    @pl.when(i == 0)
    def _():
        ds_ref[...] = jnp.zeros_like(ds_ref)

    cmat = act_ref[0, :, inner + STATE : inner + 2 * STATE]
    ec2 = split2(jnp.exp(dev_ref[0]))
    ece = nn(ec2, ex_ref[...])
    x = act_ref[0, :, :inner].astype(F32)
    y_loc = y_ref[0]
    y_in = ece * nn(cmat, sin_ref[0])
    y = (y_loc + y_in + vec_ref[1:2, :] * x).astype(BF16).astype(F32)
    z = z_ref[0].astype(F32)
    sig = sigmoid(z)
    silu = z * sig
    g = y * silu
    scale = lax.rsqrt(jnp.mean(g * g, axis=1, keepdims=True) + EPS)
    gain = vec_ref[0:1, :]
    gs = g * scale
    normalized = (gs * gain).astype(BF16)
    norm_ref[0] = normalized
    mixed_ref[0] = (u_ref[0].astype(F32) + nn(normalized, w_ref[...])).astype(BF16)
    gn = nt(c_ref[0], w_ref[...])
    sums_ref[0:1, :] += jnp.sum(gn * gs, axis=0, keepdims=True)
    h = gn * gain
    dg = scale * (h - gs * jnp.mean(h * gs, axis=1, keepdims=True))
    dy_b = (dg * silu).astype(BF16)
    dy = dy_b.astype(F32)
    dy_ref[0] = dy_b
    dz_ref[0] = (dg * y * (sig + silu * (1.0 - sig))).astype(BF16)
    sums_ref[1:2, :] += jnp.sum(dy * x, axis=0, keepdims=True)
    rows = dy * y_loc
    high = rows.astype(BF16)
    rest = (rows - high.astype(F32)).astype(BF16)
    rows_ref[0] = nn(high, red_ref[...]) + nn(rest, red_ref[...])
    q2_ref[0] = nn((dy * y_in).astype(BF16), red_ref[...])
    ds_ref[0] += tn(cmat, (dy * ece).astype(BF16))


def gate_call(y, act, z, dev, s_in, u, cot, w_out, vecs, ex, red, rows):
    seqs, length, inner = y.shape
    width = act.shape[2]
    depth = u.shape[2]
    whole = lambda s, c: (0, 0)
    row = lambda s, c: (s, c, 0)
    per_seq = lambda s, c: (s, 0, 0)
    lanes = jax.ShapeDtypeStruct((seqs, length, LANES), F32)
    wide = jax.ShapeDtypeStruct((seqs, length, inner), BF16)
    return pl.pallas_call(
        gate_kernel,
        grid=(seqs, length // rows),
        in_specs=[
            pl.BlockSpec((1, rows, inner), row),
            pl.BlockSpec((1, rows, width), row),
            pl.BlockSpec((1, rows, inner), row),
            pl.BlockSpec((1, rows, LANES), row),
            pl.BlockSpec((1, STATE, inner), per_seq),
            pl.BlockSpec((1, rows, depth), row),
            pl.BlockSpec((1, rows, depth), row),
            pl.BlockSpec(w_out.shape, whole),
            pl.BlockSpec(vecs.shape, whole),
            pl.BlockSpec(ex.shape, whole),
            pl.BlockSpec(red.shape, whole),
        ],
        out_specs=[
            pl.BlockSpec((1, rows, depth), row),
            pl.BlockSpec((1, rows, inner), row),
            pl.BlockSpec((1, rows, inner), row),
            pl.BlockSpec((1, rows, inner), row),
            pl.BlockSpec((1, rows, LANES), row),
            pl.BlockSpec((1, rows, LANES), row),
            pl.BlockSpec((8, inner), whole),
            pl.BlockSpec((1, STATE, inner), per_seq),
        ],
        out_shape=[
            jax.ShapeDtypeStruct((seqs, length, depth), BF16),
            wide,
            wide,
            wide,
            lanes,
            lanes,
            jax.ShapeDtypeStruct((8, inner), F32),
            jax.ShapeDtypeStruct((seqs, STATE, inner), F32),
        ],
        compiler_params=pltpu.CompilerParams(vmem_limit_bytes=VMEM_LIMIT),
        cost_estimate=cost(seqs * length, 22),
        name="gate_and_output",
    )(y, act, z, dev, s_in, u, cot, w_out, vecs, ex, red)


def weights_kernel(norm_ref, c_ref, n_ref, dz_ref, gwo_ref, gwz_ref):
    @pl.when(jnp.logical_and(pl.program_id(0) == 0, pl.program_id(1) == 0))
    def _():
        gwo_ref[...] = jnp.zeros_like(gwo_ref)
        gwz_ref[...] = jnp.zeros_like(gwz_ref)

    gwo_ref[...] += tn(norm_ref[0], c_ref[0])
    gwz_ref[...] += tn(n_ref[0], dz_ref[0])


def weights_call(normalized, cot, normed, dz, rows):
    seqs, length, inner = dz.shape
    depth = cot.shape[2]
    whole = lambda s, c: (0, 0)
    row = lambda s, c: (s, c, 0)
    return pl.pallas_call(
        weights_kernel,
        grid=(seqs, length // rows),
        in_specs=[
            pl.BlockSpec((1, rows, inner), row),
            pl.BlockSpec((1, rows, depth), row),
            pl.BlockSpec((1, rows, depth), row),
            pl.BlockSpec((1, rows, inner), row),
        ],
        out_specs=[pl.BlockSpec((inner, depth), whole), pl.BlockSpec((depth, inner), whole)],
        out_shape=[
            jax.ShapeDtypeStruct((inner, depth), F32),
            jax.ShapeDtypeStruct((depth, inner), F32),
        ],
        compiler_params=pltpu.CompilerParams(vmem_limit_bytes=VMEM_LIMIT),
        cost_estimate=cost(seqs * length, 8),
        name="weight_gradients",
    )(normalized, cot, normed, dz)


def back_kernel(
    act_ref, dy_ref, dt_ref, cum_ref, dev_ref, st_ref, sin_ref, rows_ref, vec_ref, ex_ref, red_ref,
    g_ref, direct_ref, da_ref,
    ds_ref,
):
    inner = dy_ref.shape[2]

    @pl.when(pl.program_id(1) == 0)
    def _():
        ds_ref[...] = jnp.zeros_like(ds_ref)

    row, col = iotas(Q, Q)
    upper = row <= col
    subs = range(dy_ref.shape[1] // Q)
    held, sums = [], []
    for sub in subs:
        at = slice(sub * Q, (sub + 1) * Q)
        bmat = act_ref[0, at, inner : inner + STATE]
        cmat = act_ref[0, at, inner + STATE : inner + 2 * STATE]
        cum = cum_ref[0, at]
        held.append((
            at, bmat, cmat.astype(F32).T.astype(BF16), jnp.where(upper, nt(bmat, cmat), 0.0), cum,
            cum.T, split2(dt_ref[0, at]), split2(jnp.exp(cum)),
            split2(jnp.exp(cum[Q - 1 : Q, :] - cum)),
            split2(jnp.exp(dev_ref[0, sub * Q : sub * Q + 8, :] - cum[0:8, :])),
        ))
        square = jnp.zeros((Q, LANES), F32)
        sums.append([square] * 6 + [jnp.zeros((8, LANES), F32)])

    for quad in range(inner // QUAD):
        cols = slice(quad * QUAD, (quad + 1) * QUAD)
        ex = ex_ref[:, cols]
        red = red_ref[cols, :]
        ds = ds_ref[:, cols]
        for sub in reversed(subs):
            at, bmat, cmat_t, scores, cum, cum_t, dt2, ec2, tail2, before2 = held[sub]
            d_scores, db, dc, direct, col_sums, w_loc, const = sums[sub]
            dte = nn(dt2, ex)
            tle = nn(tail2, ex)
            ece = nn(ec2, ex)
            x = act_ref[0, at, cols].astype(F32)
            xdt_b = (x * dte).astype(BF16)
            xdt = xdt_b.astype(F32)
            dy_b = dy_ref[0, at, cols]
            dy = dy_b.astype(F32)
            parts = []
            for pair in range(2):
                lanes = slice(pair * LANES, (pair + 1) * LANES)
                stacked = block_pair(dy_b[:, lanes])
                d_mat = nt(xdt_b[:, lanes], stacked)
                mats = []
                for j in range(2):
                    h = quad * 4 + pair * 2 + j
                    decay = jnp.exp(jnp.minimum(cum_t[h : h + 1, :] - cum[:, h : h + 1], 0.0))
                    mats.append((scores * decay).astype(BF16))
                    d_scores = d_scores + d_mat[:, j * Q : (j + 1) * Q] * decay
                parts.append(nn(jnp.concatenate(mats, axis=1), stacked))
            ds_b = ds.astype(BF16)
            st = st_ref[0, sub, :, cols].astype(F32)
            before = nn(before2, ex)[0:1, :]
            state_b = (st + before * sin_ref[0, :, cols].astype(F32)).astype(BF16)
            dx_intra = jnp.concatenate(parts, axis=1)
            dx_inter = tle * nn(bmat, ds_b)
            dxp = dx_intra + dx_inter
            g_ref[0, at, cols] = dte * dxp + vec_ref[1:2, cols] * dy
            direct = direct + nn((x * dxp).astype(BF16), red)
            prod = xdt * dx_intra
            high = prod.astype(BF16)
            col_sums = col_sums + nn(high, red) + nn((prod - high.astype(F32)).astype(BF16), red)
            w_loc = w_loc + nn((xdt * dx_inter).astype(BF16), red)
            db = db + nt((xdt * tle).astype(BF16), ds_b)
            dye = (dy * ece).astype(BF16)
            dc = dc + nt(dye, state_b)
            last = ece[Q - 1 : Q, :]
            both = jnp.sum(st * ds, axis=0, keepdims=True) * last
            both = jnp.broadcast_to(both, (8, QUAD))
            high = both.astype(BF16)
            const = const + nn(high, red) + nn((both - high.astype(F32)).astype(BF16), red)
            ds = ds * last + nn(cmat_t, dye)
            sums[sub] = [d_scores, db, dc, direct, col_sums, w_loc, const]
        ds_ref[:, cols] = ds
    for sub in subs:
        at, bmat = held[sub][:2]
        cmat = act_ref[0, at, inner + STATE : inner + 2 * STATE]
        d_scores, db, dc, direct, col_sums, w_loc, const = sums[sub]
        d_scores = jnp.where(upper, d_scores, 0.0)
        g_ref[0, at, inner : inner + STATE] = db + nn(d_scores.astype(BF16), cmat)
        g_ref[0, at, inner + STATE :] = dc + nn(d_scores.T.astype(BF16), bmat)
        direct_ref[0, at] = direct
        da_ref[0, at] = (
            exact(upper.astype(F32), rows_ref[0, at] - col_sums)
            + exact((row > col).astype(F32), w_loc)
            + const[0:1, :]
        )


def back_call(act, dy, dts, cum, dev, states, s_in, rows, vecs, ex, red):
    seqs, length, width = act.shape
    inner = dy.shape[2]
    step = SUB * Q
    steps = length // step
    whole = lambda s, c: (0, 0)
    row = lambda s, c: (s, steps - 1 - c, 0)
    lanes = jax.ShapeDtypeStruct((seqs, length, LANES), F32)
    lane_block = pl.BlockSpec((1, step, LANES), row)
    return pl.pallas_call(
        back_kernel,
        grid=(seqs, steps),
        in_specs=[
            pl.BlockSpec((1, step, width), row),
            pl.BlockSpec((1, step, inner), row),
            lane_block,
            lane_block,
            lane_block,
            pl.BlockSpec((1, SUB, STATE, inner), lambda s, c: (s, steps - 1 - c, 0, 0)),
            pl.BlockSpec((1, STATE, inner), lambda s, c: (s, 0, 0)),
            lane_block,
            pl.BlockSpec(vecs.shape, whole),
            pl.BlockSpec(ex.shape, whole),
            pl.BlockSpec(red.shape, whole),
        ],
        out_specs=[pl.BlockSpec((1, step, width), row), lane_block, lane_block],
        out_shape=[jax.ShapeDtypeStruct((seqs, length, width), F32), lanes, lanes],
        scratch_shapes=[pltpu.VMEM((STATE, inner), F32)],
        compiler_params=pltpu.CompilerParams(vmem_limit_bytes=VMEM_LIMIT),
        cost_estimate=cost(seqs * length, 29),
        name="scan_backward",
    )(act, dy, dts, cum, dev, states, s_in, rows, vecs, ex, red)


def finish_kernel(
    g_ref, act_ref, xbc_ref, prev_ref, halo_ref, raw_ref, dt_ref, dev_ref, tot_ref, ds_ref, q2_ref,
    direct_ref, da_ref, c4_ref, taps_ref, bias_ref, heads_ref, ex_ref, red_ref,
    gconv_ref, gdt_ref, taps_sum_ref, heads_sum_ref,
    ext_ref, carry_ref,
):
    s, c = pl.program_id(0), pl.program_id(1)
    width = xbc_ref.shape[2]
    inner = ds_ref.shape[2]
    rows = xbc_ref.shape[1]

    @pl.when(jnp.logical_and(s == 0, c == 0))
    def _():
        taps_sum_ref[...] = jnp.zeros_like(taps_sum_ref)
        heads_sum_ref[...] = jnp.zeros_like(heads_sum_ref)

    @pl.when(c == 0)
    def _():
        carry_ref[...] = jnp.zeros_like(carry_ref)

    fill_ext(ext_ref, xbc_ref, prev_ref, halo_ref, c == 0)

    def conv_back(grads, quad_cols):
        for j in range(QUAD // LANES):
            start = quad_cols.start + j * LANES
            cols = slice(start, start + LANES)
            views = shifted(ext_ref, start, rows)
            conv = conv_columns(views, taps_ref, bias_ref, cols)
            sig = sigmoid(conv)
            out = grads[:, j * LANES : (j + 1) * LANES] * (sig + conv * sig * (1.0 - sig))
            gconv_ref[0, :, cols] = out
            for k in range(4):
                taps_sum_ref[k : k + 1, cols] += jnp.sum(out * views[k], axis=0, keepdims=True)
            taps_sum_ref[4:5, cols] += jnp.sum(out, axis=0, keepdims=True)

    bmat = act_ref[0, :, inner : inner + STATE]
    dts = dt_ref[0]
    dt2 = split2(dts)
    tail2 = split2(jnp.exp(tot_ref[0, 0:1, :] - dev_ref[0]))
    db = jnp.zeros((rows, STATE), F32)
    direct = direct_ref[0]
    q3 = jnp.zeros((rows, LANES), F32)
    for quad in range(inner // QUAD):
        cols = slice(quad * QUAD, (quad + 1) * QUAD)
        ex = ex_ref[:, cols]
        red = red_ref[cols, :]
        dte = nn(dt2, ex)
        tle = nn(tail2, ex)
        x = act_ref[0, :, cols].astype(F32)
        xdt = (x * dte).astype(BF16).astype(F32)
        ds_b = ds_ref[0, :, cols]
        dxc = tle * nn(bmat, ds_b)
        direct = direct + nn((x * dxc).astype(BF16), red)
        q3 = q3 + nn((xdt * dxc).astype(BF16), red)
        db = db + nt((xdt * tle).astype(BF16), ds_b)
        conv_back(g_ref[0, :, cols] + dte * dxc, cols)
    db_all = jnp.concatenate([db, jnp.zeros_like(db)], axis=1)
    cols = slice(inner, inner + QUAD)
    conv_back(g_ref[0, :, cols] + db_all, cols)

    step = q3 - q2_ref[0]
    row, col = iotas(rows, rows)
    prefix = exact((row > col).astype(F32), step) + carry_ref[0:1, :]
    carry_ref[...] = carry_ref[...] + jnp.sum(step, axis=0, keepdims=True)
    da = da_ref[0] + c4_ref[0, 0:1, :] + prefix
    rate = heads_ref[1:2, :]
    raw = raw_ref[0].astype(F32) + heads_ref[0:1, :]
    grad = (direct + rate * da) * sigmoid(raw) * heads_ref[3:4, :]
    gdt_ref[0] = grad.astype(BF16)
    heads_sum_ref[0:1, :] += jnp.sum(grad, axis=0, keepdims=True)
    heads_sum_ref[1:2, :] += jnp.sum(da * dts, axis=0, keepdims=True) * rate


def finish_call(
    grad, act, xbc, halo, raw, dts, dev, tot, ds_end, q2, direct, da, c4, taps, bias, heads, ex, red,
    rows,
):
    seqs, length, width = xbc.shape
    inner = ds_end.shape[2]
    whole = lambda s, c: (0, 0)
    row = lambda s, c: (s, c, 0)
    per_seq = lambda s, c: (s, 0, 0)
    lane_block = pl.BlockSpec((1, rows, LANES), row)
    wide_block = pl.BlockSpec((1, rows, width), row)
    return pl.pallas_call(
        finish_kernel,
        grid=(seqs, length // rows),
        in_specs=[
            wide_block,
            wide_block,
            wide_block,
            pl.BlockSpec((1, 16, width), lambda s, c: (s, jnp.maximum(c * (rows // 16) - 1, 0), 0)),
            pl.BlockSpec((1, 16, width), per_seq),
            lane_block,
            lane_block,
            lane_block,
            pl.BlockSpec((1, 8, LANES), per_seq),
            pl.BlockSpec((1, STATE, inner), per_seq),
            lane_block,
            lane_block,
            lane_block,
            pl.BlockSpec((1, 8, LANES), per_seq),
            pl.BlockSpec(taps.shape, whole),
            pl.BlockSpec(bias.shape, whole),
            pl.BlockSpec(heads.shape, whole),
            pl.BlockSpec(ex.shape, whole),
            pl.BlockSpec(red.shape, whole),
        ],
        out_specs=[
            wide_block,
            lane_block,
            pl.BlockSpec((8, width), whole),
            pl.BlockSpec((8, LANES), whole),
        ],
        out_shape=[
            jax.ShapeDtypeStruct((seqs, length, width), F32),
            jax.ShapeDtypeStruct((seqs, length, LANES), BF16),
            jax.ShapeDtypeStruct((8, width), F32),
            jax.ShapeDtypeStruct((8, LANES), F32),
        ],
        scratch_shapes=[
            pltpu.VMEM((width // LANES, rows + 8, LANES), F32),
            pltpu.VMEM((8, LANES), F32),
        ],
        compiler_params=pltpu.CompilerParams(vmem_limit_bytes=VMEM_LIMIT),
        cost_estimate=cost(seqs * length, 21),
        name="conv_backward",
    )(
        grad, act, xbc, xbc, halo, raw, dts, dev, tot, ds_end, q2, direct, da, c4, taps, bias, heads,
        ex, red,
    )


def taps_back_kernel(
    g_ref, next_ref, after_ref, gdt_ref, normed_ref, taps_ref,
    gx_ref, gw_ref,
    ext_ref,
):
    s, c = pl.program_id(0), pl.program_id(1)
    rows, width = g_ref.shape[1], g_ref.shape[2]

    @pl.when(jnp.logical_and(s == 0, c == 0))
    def _():
        gw_ref[...] = jnp.zeros_like(gw_ref)

    last = c == pl.num_programs(1) - 1
    for block in range(width // LANES):
        cols = slice(block * LANES, (block + 1) * LANES)
        ext_ref[block, 0:rows, :] = g_ref[0, :, cols]
        ext_ref[block, rows : rows + 8, :] = jnp.where(
            last, after_ref[0, :, cols], next_ref[0, :, cols]
        )
        total = taps_ref[3:4, cols] * g_ref[0, :, cols]
        for k in range(3):
            total = total + taps_ref[k : k + 1, cols] * ext_ref[block, pl.ds(3 - k, rows), :]
        gx_ref[0, :, cols] = total.astype(BF16)
    gx_ref[0, :, width:] = gdt_ref[0]
    gw_ref[...] += tn(normed_ref[0], gx_ref[0])


def taps_back_call(gconv, after, gdt, normed, taps, rows):
    seqs, length, width = gconv.shape
    depth = normed.shape[2]
    whole = lambda s, c: (0, 0)
    row = lambda s, c: (s, c, 0)
    last = length // 8 - 1
    return pl.pallas_call(
        taps_back_kernel,
        grid=(seqs, length // rows),
        in_specs=[
            pl.BlockSpec((1, rows, width), row),
            pl.BlockSpec(
                (1, 8, width), lambda s, c: (s, jnp.minimum((c + 1) * (rows // 8), last), 0)
            ),
            pl.BlockSpec((1, 8, width), lambda s, c: (s, 0, 0)),
            pl.BlockSpec((1, rows, LANES), row),
            pl.BlockSpec((1, rows, depth), row),
            pl.BlockSpec(taps.shape, whole),
        ],
        out_specs=[
            pl.BlockSpec((1, rows, width + LANES), row),
            pl.BlockSpec((depth, width + LANES), whole),
        ],
        out_shape=[
            jax.ShapeDtypeStruct((seqs, length, width + LANES), BF16),
            jax.ShapeDtypeStruct((depth, width + LANES), F32),
        ],
        scratch_shapes=[pltpu.VMEM((width // LANES, rows + 8, LANES), F32)],
        compiler_params=pltpu.CompilerParams(vmem_limit_bytes=VMEM_LIMIT),
        cost_estimate=cost(seqs * length, 9),
        name="taps_backward",
    )(gconv, gconv, after, gdt, normed, taps)


def input_kernel(dz_ref, gx_ref, wz_ref, wx_ref, u_ref, c_ref, gain_ref, out_ref, sum_ref):
    @pl.when(jnp.logical_and(pl.program_id(0) == 0, pl.program_id(1) == 0))
    def _():
        sum_ref[...] = jnp.zeros_like(sum_ref)

    grad = nt(dz_ref[0], wz_ref[...]) + nt(gx_ref[0], wx_ref[...])
    u = u_ref[0].astype(F32)
    scale = lax.rsqrt(jnp.mean(u * u, axis=1, keepdims=True) + EPS)
    us = u * scale
    sum_ref[0:1, :] += jnp.sum(grad * us, axis=0, keepdims=True)
    h = grad * gain_ref[0:1, :]
    back = scale * (h - us * jnp.mean(h * us, axis=1, keepdims=True))
    out_ref[0] = c_ref[0].astype(F32) + back


def input_call(dz, gx, w_z, w_x, u, cot, gain, rows):
    seqs, length, depth = u.shape
    whole = lambda s, c: (0, 0)
    row = lambda s, c: (s, c, 0)
    return pl.pallas_call(
        input_kernel,
        grid=(seqs, length // rows),
        in_specs=[
            pl.BlockSpec((1, rows, dz.shape[2]), row),
            pl.BlockSpec((1, rows, gx.shape[2]), row),
            pl.BlockSpec(w_z.shape, whole),
            pl.BlockSpec(w_x.shape, whole),
            pl.BlockSpec((1, rows, depth), row),
            pl.BlockSpec((1, rows, depth), row),
            pl.BlockSpec(gain.shape, whole),
        ],
        out_specs=[pl.BlockSpec((1, rows, depth), row), pl.BlockSpec((8, depth), whole)],
        out_shape=[
            jax.ShapeDtypeStruct((seqs, length, depth), F32),
            jax.ShapeDtypeStruct((8, depth), F32),
        ],
        compiler_params=pltpu.CompilerParams(vmem_limit_bytes=VMEM_LIMIT),
        cost_estimate=cost(seqs * length, 9),
        name="input_gradient",
    )(dz, gx, w_z, w_x, u, cot, gain)


def to_all(value, size, axes):
    copies = jnp.broadcast_to(value[None], (size,) + value.shape)
    return lax.all_to_all(copies, axes, split_axis=0, concat_axis=0, tiled=True)


def other_core(value, sizes):
    return lax.ppermute(value, "dp", [(i, i ^ 1) for i in range(sizes["dp"])])


def both_cores(value, sizes, axis):
    other = other_core(value, sizes)
    first = lax.axis_index("dp") % 2 == 0
    return jnp.where(first, jnp.stack([value, other], axis), jnp.stack([other, value], axis))


def core_half(shard):
    half = shard.shape[0] // 2
    return lax.dynamic_slice_in_dim(shard, (lax.axis_index("dp") % 2) * half, half, 0)


def gather_rows(shard, sizes):
    got = to_all(core_half(shard), sizes["seq"], "seq").reshape(sizes["seq"], -1, shard.shape[1])
    return both_cores(got, sizes, 1).reshape(sizes["seq"] * shard.shape[0], shard.shape[1])


def gather_later(shards, sizes):
    columns = max(shard.shape[1] for shard in shards)
    halves = [core_half(shard).reshape(-1, columns) for shard in shards]
    got = lax.all_gather(jnp.concatenate(halves, axis=0), "seq", axis=0)
    other = other_core(got, sizes)
    first = lax.axis_index("dp") % 2 == 0
    outs, at = [], 0
    for shard, half in zip(shards, halves):
        rows = slice(at, at + half.shape[0])
        at += half.shape[0]
        mine, away = got[:, rows], other[:, rows]
        pair = jnp.where(first, jnp.stack([mine, away], 1), jnp.stack([away, mine], 1))
        outs.append(pair.reshape(sizes["seq"] * shard.shape[0], shard.shape[1]))
    return outs


def scatter_rows(grads, sizes):
    size = sizes["seq"]
    core = lax.axis_index("dp") % 2
    columns = max(grad.shape[1] for grad in grads)
    halves = []
    for grad in grads:
        parts = grad.reshape(size, 2, -1, grad.shape[1])
        mine = lax.dynamic_index_in_dim(parts, core, 1, keepdims=False)
        away = lax.dynamic_index_in_dim(parts, 1 - core, 1, keepdims=False).astype(BF16)
        half = (mine + other_core(away, sizes).astype(F32)).astype(BF16)
        halves.append(half.reshape(size, -1, columns))
    return lax.all_to_all(
        jnp.concatenate(halves, axis=1), "seq", split_axis=0, concat_axis=0, tiled=True
    )


def add_up(got, sizes):
    total = got.astype(F32).sum(axis=0)
    step = 2
    while step < sizes["dp"]:
        sent = total.astype(BF16)
        away = lax.ppermute(sent, "dp", [(i, i ^ step) for i in range(sizes["dp"])])
        total = sent.astype(F32) + away.astype(F32)
        step *= 2
    return total


def swap_rows(total, shapes, sizes):
    pair = both_cores(total, sizes, 0)
    outs, at = [], 0
    for rows, columns in shapes:
        count = rows * columns // (2 * sizes["seq"] * total.shape[1])
        outs.append(pair[:, at : at + count].reshape(rows // sizes["seq"], columns))
        at += count
    return outs


def sum_small(values, sizes, beside):
    flat = jnp.concatenate([value.reshape(-1) for value in values])
    count = flat.shape[0]
    flat = jnp.pad(flat, (0, -count % 1024)).reshape(-1, LANES)
    step = 1
    while step < sizes["dp"]:
        flat = flat + lax.ppermute(flat, "dp", [(i, i ^ step) for i in range(sizes["dp"])])
        step *= 2
    flat, beside = lax.optimization_barrier((to_all(flat, sizes["seq"], "seq"), beside))
    flat = flat.reshape(sizes["seq"], -1).sum(axis=0)
    out, at = [], 0
    for value in values:
        out.append(flat[at : at + value.size].reshape(value.shape))
        at += value.size
    return out, beside


def shift_in(value, size, step):
    pairs = [(i, i + step) for i in range(size) if 0 <= i + step < size]
    return lax.ppermute(value, "seq", pairs)


def carry_over(states, decay, size, step, beside):
    seqs, depth, inner = states.shape
    piece = depth // size
    sent = states.astype(BF16).reshape(seqs, size, piece, inner)
    got = lax.all_to_all(sent, "seq", split_axis=1, concat_axis=1, tiled=True)
    got, beside = lax.optimization_barrier((got, beside))
    got = got.astype(F32)
    order = range(size) if step > 0 else range(size - 1, -1, -1)
    held = jnp.zeros((seqs, piece, inner), F32)
    into = [None] * size
    for i in order:
        into[i] = held
        held = held * decay[i][:, None, :] + got[:, i]
    back = jnp.stack(into, axis=1).astype(BF16)
    back = lax.all_to_all(back, "seq", split_axis=1, concat_axis=1, tiled=True)
    return back.reshape(seqs, depth, inner), beside


def rms_gain(values, gain):
    return values * lax.rsqrt(jnp.mean(values * values, axis=-1, keepdims=True) + EPS) * gain


def body(
    sizes, inputs, w_in, w_out, norm_gain, conv_weight, conv_bias, dt_bias, a_log, skip, gate_gain,
    cotangent,
):
    size = sizes["seq"]
    seqs, length, depth = inputs.shape
    inner = gate_gain.shape[0]
    width = conv_weight.shape[1]
    tokens = seqs * length
    rows = min(256, length)

    w_x = gather_rows(jnp.pad(w_in[:, inner:], ((0, 0), (0, LANES - HEADS))), sizes)
    w_z, full_out = gather_later([w_in[:, :inner], w_out], sizes)

    def pad_heads(values):
        return jnp.pad(values, (0, LANES - HEADS))

    rates = -jnp.exp(a_log)
    heads = jnp.stack([pad_heads(dt_bias), pad_heads(rates), pad_heads(skip), pad_heads(jnp.ones_like(skip))])
    heads = jnp.pad(heads, ((0, 4), (0, 0)))
    taps = jnp.pad(conv_weight, ((0, 4), (0, 0)))
    bias = jnp.pad(conv_bias[None, :], ((0, 7), (0, 0)))
    vecs = jnp.pad(jnp.stack([gate_gain, jnp.repeat(skip, HEADDIM)]), ((0, 6), (0, 0)))
    ex, red = head_matrices(inner)

    edge = shift_in(inputs[:, length - 16 :], size, 1).astype(F32)
    edge = rms_gain(edge, norm_gain).astype(BF16).reshape(seqs * 16, depth)
    normed = rms_gain(inputs.astype(F32), norm_gain).astype(BF16)
    flat = normed.reshape(tokens, depth)

    def project(left, matrix):
        return jnp.dot(left, matrix, preferred_element_type=F32).astype(BF16)

    halo = project(edge, w_x)[:, :width].reshape(seqs, 16, width)
    xbc = project(flat, w_x[:, :width]).reshape(seqs, length, width)
    raw = project(flat, w_x[:, width:]).reshape(seqs, length, LANES)

    total = (softplus(raw.astype(F32) + heads[0]) * heads[3]).sum(axis=1) * heads[1]
    decay = jnp.exp(to_all(total, size, "seq").reshape(size, seqs, LANES)[:, :, :HEADS])
    decay = jnp.repeat(decay, HEADDIM, axis=2)
    act, y, dts, cum, dev, states, final = scan_call(xbc, halo, raw, taps, bias, heads, ex, inner)
    final, decay = lax.optimization_barrier((final, decay))
    z = project(flat, w_z).reshape(seqs, length, inner)
    s_in, z = carry_over(final, decay, size, 1, z)

    mixed, dy, dz, normalized, row_sums, q2, gate_sums, ds_loc = gate_call(
        y, act, z, dev, s_in, inputs, cotangent, full_out, vecs, ex, red, rows
    )
    grad_out, grad_z = weights_call(normalized, cotangent, normed, dz, min(512, length))
    ds_end, weight_grads = carry_over(ds_loc, decay, size, -1, (grad_out, grad_z))
    got_zo = scatter_rows(weight_grads, sizes)

    grad, direct, da = back_call(act, dy, dts, cum, dev, states, s_in, row_sums, vecs, ex, red)

    both = (s_in.astype(F32) * ds_end.astype(F32)).sum(axis=1).reshape(seqs, HEADS, HEADDIM).sum(axis=2)
    both = jnp.pad(both, ((0, 0), (0, LANES - HEADS))) * jnp.exp(total)
    c4 = jnp.broadcast_to((both + q2.sum(axis=1))[:, None, :], (seqs, 8, LANES))
    tot = jnp.broadcast_to(total[:, None, :], (seqs, 8, LANES))
    gconv, gdt, taps_sum, heads_sum = finish_call(
        grad, act, xbc, halo, raw, dts, dev, tot, ds_end, q2, direct, da, c4, taps, bias, heads, ex,
        red, rows,
    )
    after = shift_in(gconv[:, :8], size, -1)
    gx, grad_x = taps_back_call(gconv, after, gdt, normed, taps, rows)
    gx, grad_x, got_zo = lax.optimization_barrier((gx, grad_x, got_zo))
    got_x = scatter_rows([grad_x], sizes)
    total_zo = add_up(got_zo, sizes)
    gain = jnp.pad(norm_gain[None, :], ((0, 7), (0, 0)))
    grad_inputs, gain_sum = input_call(dz, gx, w_z, w_x, inputs, cotangent, gain, rows)
    got_x, gain_sum, total_zo = lax.optimization_barrier((got_x, gain_sum, total_zo))
    rows_out, rows_z = swap_rows(total_zo, [grad_out.shape, grad_z.shape], sizes)
    total_x = add_up(got_x, sizes)
    sums, total_x = sum_small(
        (
            gain_sum[0],
            taps_sum[:4],
            taps_sum[4],
            heads_sum[0, :HEADS],
            heads_sum[1, :HEADS],
            gate_sums[1].reshape(HEADS, HEADDIM).sum(axis=1),
            gate_sums[0],
        ),
        sizes,
        total_x,
    )
    (rows_x,) = swap_rows(total_x, [grad_x.shape], sizes)

    rows_in = jnp.concatenate([rows_z, rows_x[:, : width + HEADS]], axis=1)
    return (mixed, grad_inputs, rows_in, rows_out, *sums)


def solution(mesh):
    placed = (
        P("dp", "seq", None),
        P("seq", None),
        P("seq", None),
        P(),
        P(),
        P(),
        P(),
        P(),
        P(),
        P(),
        P("dp", "seq", None),
    )
    return jax.shard_map(
        functools.partial(body, dict(mesh.shape)),
        mesh=mesh,
        in_specs=placed,
        out_specs=(
            P("dp", "seq", None),
            P("dp", "seq", None),
            P("seq", None),
            P("seq", None),
            P(),
            P(),
            P(),
            P(),
            P(),
            P(),
            P(),
        ),
        check_vma=False,
    )
```

```python
import functools

import jax
import jax.numpy as jnp
from jax import lax
from jax.experimental import pallas as pl
from jax.experimental.pallas import tpu as pltpu
from jax.sharding import PartitionSpec as P

HEADS = 24
HEADDIM = 64
STATE = 128
LANES = 128
Q = 128
SUB = 2
QUAD = 256
EPS = 1e-05
F32 = jnp.float32
BF16 = jnp.bfloat16
VMEM_LIMIT = 56 * 1024 * 1024


def cost(tokens, per_token_ns):
    seconds = tokens * per_token_ns * 1e-9
    return pl.CostEstimate(
        flops=int(seconds * 1e15), bytes_accessed=int(seconds * 3e12), transcendentals=0
    )


def dot(left, right, dims):
    return lax.dot_general(left, right, (dims, ((), ())), preferred_element_type=F32)


def nn(left, right):
    return dot(left, right, ((1,), (0,)))


def nt(left, right):
    return dot(left, right, ((1,), (1,)))


def tn(left, right):
    return dot(left, right, ((0,), (0,)))


def exact(left, right):
    return lax.dot_general(
        left, right, (((1,), (0,)), ((), ())), precision=lax.Precision.HIGHEST,
        preferred_element_type=F32,
    )


def split2(values):
    high = values.astype(BF16)
    rest = (values - high.astype(F32)).astype(BF16)
    return jnp.concatenate([high, rest], axis=1)


def sigmoid(values):
    return 0.5 + 0.5 * jnp.tanh(0.5 * values)


def softplus(values):
    return jnp.maximum(values, 0.0) + jnp.log1p(jnp.exp(-jnp.abs(values)))


def iotas(rows, cols):
    return (
        lax.broadcasted_iota(jnp.int32, (rows, cols), 0),
        lax.broadcasted_iota(jnp.int32, (rows, cols), 1),
    )


def head_matrices(inner):
    col_head = jnp.arange(inner) // HEADDIM
    expand = (jnp.arange(LANES)[:, None] == col_head[None, :]).astype(BF16)
    return jnp.concatenate([expand, expand], axis=0), expand.T


def block_pair(pair):
    low = lax.broadcasted_iota(jnp.int32, pair.shape, 1) < HEADDIM
    zero = jnp.zeros_like(pair)
    return jnp.concatenate([jnp.where(low, pair, zero), jnp.where(low, zero, pair)], axis=0)


def shifted(ext_ref, start, rows):
    block = start // LANES
    return [ext_ref[block, pl.ds(5 + k, rows), :] for k in range(4)]


def conv_columns(views, taps_ref, bias_ref, cols):
    total = bias_ref[0:1, cols] + taps_ref[0:1, cols] * views[0]
    for k in range(1, 4):
        total = total + taps_ref[k : k + 1, cols] * views[k]
    return total


def fill_ext(ext_ref, xbc_ref, prev_ref, halo_ref, first):
    rows = xbc_ref.shape[1]
    for block in range(ext_ref.shape[0]):
        cols = slice(block * LANES, (block + 1) * LANES)
        before = jnp.where(
            first, halo_ref[0, :, cols].astype(F32), prev_ref[0, :, cols].astype(F32)
        )
        ext_ref[block, 0:8, :] = before[8:16]
        ext_ref[block, pl.ds(8, rows), :] = xbc_ref[0, :, cols].astype(F32)


def scan_kernel(
    xbc_ref, prev_ref, halo_ref, raw_ref, taps_ref, bias_ref, heads_ref, ex_ref,
    act_ref, y_ref, dt_ref, cum_ref, dev_ref, st_ref, fin_ref,
    ext_ref, state_ref, carry_ref,
):
    c = pl.program_id(1)
    rows, width = xbc_ref.shape[1], xbc_ref.shape[2]
    inner = y_ref.shape[2]

    @pl.when(c == 0)
    def _():
        state_ref[...] = jnp.zeros_like(state_ref)
        carry_ref[...] = jnp.zeros_like(carry_ref)

    fill_ext(ext_ref, xbc_ref, prev_ref, halo_ref, c == 0)
    for start in range(0, width, LANES):
        cols = slice(start, start + LANES)
        half = 0.5 * conv_columns(shifted(ext_ref, start, rows), taps_ref, bias_ref, cols)
        act_ref[0, :, cols] = (half + half * jnp.tanh(half)).astype(BF16)

    row, col = iotas(Q, Q)
    lower = row >= col
    before = carry_ref[0:1, :]
    held, factors = [], []
    for sub in range(rows // Q):
        at = slice(sub * Q, (sub + 1) * Q)
        dts = softplus(raw_ref[0, at].astype(F32) + heads_ref[0:1, :]) * heads_ref[3:4, :]
        cum = exact(lower.astype(F32), dts * heads_ref[1:2, :])
        dt_ref[0, at] = dts
        cum_ref[0, at] = cum
        dev_ref[0, at] = cum + before
        before = before + cum[Q - 1 : Q, :]
        bmat = act_ref[0, at, inner : inner + STATE]
        cmat = act_ref[0, at, inner + STATE : inner + 2 * STATE]
        factors += [dts, jnp.exp(cum), jnp.exp(cum[Q - 1 : Q, :] - cum)]
        held.append((
            at, cum, cum.T, cmat, bmat.astype(F32).T.astype(BF16),
            jnp.where(lower, nt(cmat, bmat), 0.0),
        ))
    factors = jnp.concatenate([split2(factor) for factor in factors], axis=0)
    carry_ref[...] = jnp.broadcast_to(before, carry_ref.shape)

    for quad in range(inner // QUAD):
        cols = slice(quad * QUAD, (quad + 1) * QUAD)
        wide = nn(factors, ex_ref[:, cols])
        state = state_ref[:, cols]
        for sub, (at, cum, cum_t, cmat, bmat_t, scores) in enumerate(held):
            dte, ece, tle = (wide[(3 * sub + k) * Q : (3 * sub + k + 1) * Q] for k in range(3))
            xdt = act_ref[0, at, cols].astype(F32) * dte
            xdt_b = xdt.astype(BF16)
            xtail = (xdt * tle).astype(BF16)
            parts = []
            for pair in range(2):
                mats = []
                for h in (quad * 4 + pair * 2, quad * 4 + pair * 2 + 1):
                    diff = cum[:, h : h + 1] - cum_t[h : h + 1, :]
                    mats.append((scores * jnp.exp(jnp.minimum(diff, 0.0))).astype(BF16))
                mat = jnp.concatenate(mats, axis=1)
                parts.append(nn(mat, block_pair(xdt_b[:, pair * LANES : (pair + 1) * LANES])))
            state_b = state.astype(BF16)
            st_ref[0, sub, :, cols] = state_b
            y_ref[0, at, cols] = jnp.concatenate(parts, axis=1) + ece * nn(cmat, state_b)
            state = state * ece[Q - 1 : Q, :] + nn(bmat_t, xtail)
        state_ref[:, cols] = state
        fin_ref[0, :, cols] = state


def scan_call(xbc, halo, raw, taps, bias, heads, ex, inner):
    seqs, length, width = xbc.shape
    chunks = length // Q
    rows = SUB * Q
    whole = lambda s, c: (0, 0)
    row = lambda s, c: (s, c, 0)
    lanes = jax.ShapeDtypeStruct((seqs, length, LANES), F32)
    return pl.pallas_call(
        scan_kernel,
        grid=(seqs, length // rows),
        in_specs=[
            pl.BlockSpec((1, rows, width), row),
            pl.BlockSpec((1, 16, width), lambda s, c: (s, jnp.maximum(c * (rows // 16) - 1, 0), 0)),
            pl.BlockSpec((1, 16, width), lambda s, c: (s, 0, 0)),
            pl.BlockSpec((1, rows, LANES), row),
            pl.BlockSpec(taps.shape, whole),
            pl.BlockSpec(bias.shape, whole),
            pl.BlockSpec(heads.shape, whole),
            pl.BlockSpec(ex.shape, whole),
        ],
        out_specs=[
            pl.BlockSpec((1, rows, width), row),
            pl.BlockSpec((1, rows, inner), row),
            pl.BlockSpec((1, rows, LANES), row),
            pl.BlockSpec((1, rows, LANES), row),
            pl.BlockSpec((1, rows, LANES), row),
            pl.BlockSpec((1, SUB, STATE, inner), lambda s, c: (s, c, 0, 0)),
            pl.BlockSpec((1, STATE, inner), lambda s, c: (s, 0, 0)),
        ],
        out_shape=[
            jax.ShapeDtypeStruct((seqs, length, width), BF16),
            jax.ShapeDtypeStruct((seqs, length, inner), F32),
            lanes,
            lanes,
            lanes,
            jax.ShapeDtypeStruct((seqs, chunks, STATE, inner), BF16),
            jax.ShapeDtypeStruct((seqs, STATE, inner), F32),
        ],
        scratch_shapes=[
            pltpu.VMEM((width // LANES, rows + 8, LANES), F32),
            pltpu.VMEM((STATE, inner), F32),
            pltpu.VMEM((8, LANES), F32),
        ],
        compiler_params=pltpu.CompilerParams(vmem_limit_bytes=VMEM_LIMIT),
        cost_estimate=cost(seqs * length, 20),
        name="scan_forward",
    )(xbc, xbc, halo, raw, taps, bias, heads, ex)


def gate_kernel(
    y_ref, act_ref, z_ref, dev_ref, sin_ref, u_ref, c_ref, w_ref, vec_ref, ex_ref, red_ref,
    mixed_ref, dy_ref, dz_ref, norm_ref, rows_ref, q2_ref, sums_ref, ds_ref,
):
    s, i = pl.program_id(0), pl.program_id(1)
    inner = y_ref.shape[2]

    @pl.when(jnp.logical_and(s == 0, i == 0))
    def _():
        sums_ref[...] = jnp.zeros_like(sums_ref)

    @pl.when(i == 0)
    def _():
        ds_ref[...] = jnp.zeros_like(ds_ref)

    cmat = act_ref[0, :, inner + STATE : inner + 2 * STATE]
    ec2 = split2(jnp.exp(dev_ref[0]))
    ece = nn(ec2, ex_ref[...])
    x = act_ref[0, :, :inner].astype(F32)
    y_loc = y_ref[0]
    y_in = ece * nn(cmat, sin_ref[0])
    y = (y_loc + y_in + vec_ref[1:2, :] * x).astype(BF16).astype(F32)
    z = z_ref[0].astype(F32)
    sig = sigmoid(z)
    silu = z * sig
    g = y * silu
    scale = lax.rsqrt(jnp.mean(g * g, axis=1, keepdims=True) + EPS)
    gain = vec_ref[0:1, :]
    gs = g * scale
    normalized = (gs * gain).astype(BF16)
    norm_ref[0] = normalized
    mixed_ref[0] = (u_ref[0].astype(F32) + nn(normalized, w_ref[...])).astype(BF16)
    gn = nt(c_ref[0], w_ref[...])
    sums_ref[0:1, :] += jnp.sum(gn * gs, axis=0, keepdims=True)
    h = gn * gain
    dg = scale * (h - gs * jnp.mean(h * gs, axis=1, keepdims=True))
    dy_b = (dg * silu).astype(BF16)
    dy = dy_b.astype(F32)
    dy_ref[0] = dy_b
    dz_ref[0] = (dg * y * (sig + silu * (1.0 - sig))).astype(BF16)
    sums_ref[1:2, :] += jnp.sum(dy * x, axis=0, keepdims=True)
    rows = dy * y_loc
    high = rows.astype(BF16)
    rest = (rows - high.astype(F32)).astype(BF16)
    rows_ref[0] = nn(high, red_ref[...]) + nn(rest, red_ref[...])
    q2_ref[0] = nn((dy * y_in).astype(BF16), red_ref[...])
    ds_ref[0] += tn(cmat, (dy * ece).astype(BF16))


def gate_call(y, act, z, dev, s_in, u, cot, w_out, vecs, ex, red, rows):
    seqs, length, inner = y.shape
    width = act.shape[2]
    depth = u.shape[2]
    whole = lambda s, c: (0, 0)
    row = lambda s, c: (s, c, 0)
    per_seq = lambda s, c: (s, 0, 0)
    lanes = jax.ShapeDtypeStruct((seqs, length, LANES), F32)
    wide = jax.ShapeDtypeStruct((seqs, length, inner), BF16)
    return pl.pallas_call(
        gate_kernel,
        grid=(seqs, length // rows),
        in_specs=[
            pl.BlockSpec((1, rows, inner), row),
            pl.BlockSpec((1, rows, width), row),
            pl.BlockSpec((1, rows, inner), row),
            pl.BlockSpec((1, rows, LANES), row),
            pl.BlockSpec((1, STATE, inner), per_seq),
            pl.BlockSpec((1, rows, depth), row),
            pl.BlockSpec((1, rows, depth), row),
            pl.BlockSpec(w_out.shape, whole),
            pl.BlockSpec(vecs.shape, whole),
            pl.BlockSpec(ex.shape, whole),
            pl.BlockSpec(red.shape, whole),
        ],
        out_specs=[
            pl.BlockSpec((1, rows, depth), row),
            pl.BlockSpec((1, rows, inner), row),
            pl.BlockSpec((1, rows, inner), row),
            pl.BlockSpec((1, rows, inner), row),
            pl.BlockSpec((1, rows, LANES), row),
            pl.BlockSpec((1, rows, LANES), row),
            pl.BlockSpec((8, inner), whole),
            pl.BlockSpec((1, STATE, inner), per_seq),
        ],
        out_shape=[
            jax.ShapeDtypeStruct((seqs, length, depth), BF16),
            wide,
            wide,
            wide,
            lanes,
            lanes,
            jax.ShapeDtypeStruct((8, inner), F32),
            jax.ShapeDtypeStruct((seqs, STATE, inner), F32),
        ],
        compiler_params=pltpu.CompilerParams(vmem_limit_bytes=VMEM_LIMIT),
        cost_estimate=cost(seqs * length, 22),
        name="gate_and_output",
    )(y, act, z, dev, s_in, u, cot, w_out, vecs, ex, red)


def weights_kernel(norm_ref, c_ref, n_ref, dz_ref, gwo_ref, gwz_ref):
    @pl.when(jnp.logical_and(pl.program_id(0) == 0, pl.program_id(1) == 0))
    def _():
        gwo_ref[...] = jnp.zeros_like(gwo_ref)
        gwz_ref[...] = jnp.zeros_like(gwz_ref)

    gwo_ref[...] += tn(norm_ref[0], c_ref[0])
    gwz_ref[...] += tn(n_ref[0], dz_ref[0])


def weights_call(normalized, cot, normed, dz, rows):
    seqs, length, inner = dz.shape
    depth = cot.shape[2]
    whole = lambda s, c: (0, 0)
    row = lambda s, c: (s, c, 0)
    return pl.pallas_call(
        weights_kernel,
        grid=(seqs, length // rows),
        in_specs=[
            pl.BlockSpec((1, rows, inner), row),
            pl.BlockSpec((1, rows, depth), row),
            pl.BlockSpec((1, rows, depth), row),
            pl.BlockSpec((1, rows, inner), row),
        ],
        out_specs=[pl.BlockSpec((inner, depth), whole), pl.BlockSpec((depth, inner), whole)],
        out_shape=[
            jax.ShapeDtypeStruct((inner, depth), F32),
            jax.ShapeDtypeStruct((depth, inner), F32),
        ],
        compiler_params=pltpu.CompilerParams(vmem_limit_bytes=VMEM_LIMIT),
        cost_estimate=cost(seqs * length, 8),
        name="weight_gradients",
    )(normalized, cot, normed, dz)


def back_kernel(
    act_ref, dy_ref, dt_ref, cum_ref, dev_ref, st_ref, sin_ref, rows_ref, vec_ref, ex_ref, red_ref,
    g_ref, direct_ref, da_ref,
    ds_ref,
):
    inner = dy_ref.shape[2]

    @pl.when(pl.program_id(1) == 0)
    def _():
        ds_ref[...] = jnp.zeros_like(ds_ref)

    row, col = iotas(Q, Q)
    upper = row <= col
    subs = range(dy_ref.shape[1] // Q)
    held, sums, factors = [], [], []
    for sub in subs:
        at = slice(sub * Q, (sub + 1) * Q)
        bmat = act_ref[0, at, inner : inner + STATE]
        cmat = act_ref[0, at, inner + STATE : inner + 2 * STATE]
        cum = cum_ref[0, at]
        held.append((
            at, bmat, cmat.astype(F32).T.astype(BF16), jnp.where(upper, nt(bmat, cmat), 0.0), cum,
            cum.T,
        ))
        factors += [
            dt_ref[0, at], jnp.exp(cum), jnp.exp(cum[Q - 1 : Q, :] - cum),
            jnp.exp(dev_ref[0, sub * Q : sub * Q + 16, :] - cum[0:16, :]),
        ]
        square = jnp.zeros((Q, LANES), F32)
        sums.append([square] * 5 + [jnp.zeros((16, LANES), F32)])
    factors = jnp.concatenate([split2(factor) for factor in factors], axis=0)

    for quad in range(inner // QUAD):
        cols = slice(quad * QUAD, (quad + 1) * QUAD)
        wide = nn(factors, ex_ref[:, cols])
        red = red_ref[cols, :]
        ds = ds_ref[:, cols]
        for sub in reversed(subs):
            at, bmat, cmat_t, scores, cum, cum_t = held[sub]
            d_scores, db, dc, col_sums, w_loc, const = sums[sub]
            base = sub * (3 * Q + 16)
            dte, ece, tle = (wide[base + k * Q : base + (k + 1) * Q] for k in range(3))
            before = wide[base + 3 * Q : base + 3 * Q + 1]
            x = act_ref[0, at, cols].astype(F32)
            xdt_b = (x * dte).astype(BF16)
            xdt = xdt_b.astype(F32)
            dy_b = dy_ref[0, at, cols]
            dy = dy_b.astype(F32)
            parts = []
            for pair in range(2):
                lanes = slice(pair * LANES, (pair + 1) * LANES)
                stacked = block_pair(dy_b[:, lanes])
                d_mat = nt(xdt_b[:, lanes], stacked)
                mats = []
                for j in range(2):
                    h = quad * 4 + pair * 2 + j
                    decay = jnp.exp(jnp.minimum(cum_t[h : h + 1, :] - cum[:, h : h + 1], 0.0))
                    mats.append((scores * decay).astype(BF16))
                    d_scores = d_scores + d_mat[:, j * Q : (j + 1) * Q] * decay
                parts.append(nn(jnp.concatenate(mats, axis=1), stacked))
            ds_b = ds.astype(BF16)
            st = st_ref[0, sub, :, cols].astype(F32)
            state_b = (st + before * sin_ref[0, :, cols].astype(F32)).astype(BF16)
            dx_intra = jnp.concatenate(parts, axis=1)
            dx_inter = tle * nn(bmat, ds_b)
            dxp = dx_intra + dx_inter
            g_ref[0, at, cols] = dte * dxp + vec_ref[1:2, cols] * dy
            last = ece[Q - 1 : Q, :]
            both = jnp.sum(st * ds, axis=0, keepdims=True) * last
            stack = []
            for value in (xdt * dx_intra, jnp.broadcast_to(both, (16, QUAD))):
                high = value.astype(BF16)
                stack += [high, (value - high.astype(F32)).astype(BF16)]
            stack.append((xdt * dx_inter).astype(BF16))
            by_head = nn(jnp.concatenate(stack, axis=0), red)
            col_sums = col_sums + by_head[:Q] + by_head[Q : 2 * Q]
            const = const + by_head[2 * Q : 2 * Q + 16] + by_head[2 * Q + 16 : 2 * Q + 32]
            w_loc = w_loc + by_head[2 * Q + 32 :]
            db = db + nt((xdt * tle).astype(BF16), ds_b)
            dye = (dy * ece).astype(BF16)
            dc = dc + nt(dye, state_b)
            ds = ds * last + nn(cmat_t, dye)
            sums[sub] = [d_scores, db, dc, col_sums, w_loc, const]
        ds_ref[:, cols] = ds
    for sub in subs:
        at, bmat = held[sub][:2]
        cmat = act_ref[0, at, inner + STATE : inner + 2 * STATE]
        d_scores, db, dc, col_sums, w_loc, const = sums[sub]
        d_scores = jnp.where(upper, d_scores, 0.0)
        g_ref[0, at, inner : inner + STATE] = db + nn(d_scores.astype(BF16), cmat)
        g_ref[0, at, inner + STATE :] = dc + nn(d_scores.T.astype(BF16), bmat)
        direct_ref[0, at] = col_sums + w_loc
        da_ref[0, at] = (
            exact(upper.astype(F32), rows_ref[0, at] - col_sums)
            + exact((row > col).astype(F32), w_loc)
            + const[0:1, :]
        )


def back_call(act, dy, dts, cum, dev, states, s_in, rows, vecs, ex, red):
    seqs, length, width = act.shape
    inner = dy.shape[2]
    step = SUB * Q
    steps = length // step
    whole = lambda s, c: (0, 0)
    row = lambda s, c: (s, steps - 1 - c, 0)
    lanes = jax.ShapeDtypeStruct((seqs, length, LANES), F32)
    lane_block = pl.BlockSpec((1, step, LANES), row)
    return pl.pallas_call(
        back_kernel,
        grid=(seqs, steps),
        in_specs=[
            pl.BlockSpec((1, step, width), row),
            pl.BlockSpec((1, step, inner), row),
            lane_block,
            lane_block,
            lane_block,
            pl.BlockSpec((1, SUB, STATE, inner), lambda s, c: (s, steps - 1 - c, 0, 0)),
            pl.BlockSpec((1, STATE, inner), lambda s, c: (s, 0, 0)),
            lane_block,
            pl.BlockSpec(vecs.shape, whole),
            pl.BlockSpec(ex.shape, whole),
            pl.BlockSpec(red.shape, whole),
        ],
        out_specs=[pl.BlockSpec((1, step, width), row), lane_block, lane_block],
        out_shape=[jax.ShapeDtypeStruct((seqs, length, width), F32), lanes, lanes],
        scratch_shapes=[pltpu.VMEM((STATE, inner), F32)],
        compiler_params=pltpu.CompilerParams(vmem_limit_bytes=VMEM_LIMIT),
        cost_estimate=cost(seqs * length, 29),
        name="scan_backward",
    )(act, dy, dts, cum, dev, states, s_in, rows, vecs, ex, red)


def finish_kernel(
    g_ref, act_ref, xbc_ref, prev_ref, halo_ref, raw_ref, dt_ref, dev_ref, tot_ref, ds_ref, q2_ref,
    direct_ref, da_ref, c4_ref, taps_ref, bias_ref, heads_ref, ex_ref, red_ref,
    gconv_ref, gdt_ref, taps_sum_ref, heads_sum_ref,
    ext_ref, carry_ref,
):
    s, c = pl.program_id(0), pl.program_id(1)
    width = xbc_ref.shape[2]
    inner = ds_ref.shape[2]
    rows = xbc_ref.shape[1]

    @pl.when(jnp.logical_and(s == 0, c == 0))
    def _():
        taps_sum_ref[...] = jnp.zeros_like(taps_sum_ref)
        heads_sum_ref[...] = jnp.zeros_like(heads_sum_ref)

    @pl.when(c == 0)
    def _():
        carry_ref[...] = jnp.zeros_like(carry_ref)

    fill_ext(ext_ref, xbc_ref, prev_ref, halo_ref, c == 0)

    def conv_back(grads, quad_cols):
        for j in range(QUAD // LANES):
            start = quad_cols.start + j * LANES
            cols = slice(start, start + LANES)
            views = shifted(ext_ref, start, rows)
            conv = conv_columns(views, taps_ref, bias_ref, cols)
            sig = sigmoid(conv)
            out = grads[:, j * LANES : (j + 1) * LANES] * (sig + conv * sig * (1.0 - sig))
            gconv_ref[0, :, cols] = out
            for k in range(4):
                taps_sum_ref[k : k + 1, cols] += jnp.sum(out * views[k], axis=0, keepdims=True)
            taps_sum_ref[4:5, cols] += jnp.sum(out, axis=0, keepdims=True)

    bmat = act_ref[0, :, inner : inner + STATE]
    dts = dt_ref[0]
    tails = jnp.exp(tot_ref[0, 0:1, :] - dev_ref[0])
    factors = jnp.concatenate([split2(dts), split2(tails)], axis=0)
    db = jnp.zeros((rows, STATE), F32)
    q3 = jnp.zeros((rows, LANES), F32)
    for quad in range(inner // QUAD):
        cols = slice(quad * QUAD, (quad + 1) * QUAD)
        wide = nn(factors, ex_ref[:, cols])
        red = red_ref[cols, :]
        dte, tle = wide[:rows], wide[rows:]
        xdt = (act_ref[0, :, cols].astype(F32) * dte).astype(BF16).astype(F32)
        ds_b = ds_ref[0, :, cols]
        dxc = tle * nn(bmat, ds_b)
        q3 = q3 + nn((xdt * dxc).astype(BF16), red)
        db = db + nt((xdt * tle).astype(BF16), ds_b)
        conv_back(g_ref[0, :, cols] + dte * dxc, cols)
    db_all = jnp.concatenate([db, jnp.zeros_like(db)], axis=1)
    cols = slice(inner, inner + QUAD)
    conv_back(g_ref[0, :, cols] + db_all, cols)

    step = q3 - q2_ref[0]
    row, col = iotas(rows, rows)
    prefix = exact((row > col).astype(F32), step) + carry_ref[0:1, :]
    carry_ref[...] = carry_ref[...] + jnp.sum(step, axis=0, keepdims=True)
    da = da_ref[0] + c4_ref[0, 0:1, :] + prefix
    rate = heads_ref[1:2, :]
    raw = raw_ref[0].astype(F32) + heads_ref[0:1, :]
    direct = (direct_ref[0] + q3) / jnp.maximum(dts, 1e-30)
    grad = (direct + rate * da) * sigmoid(raw) * heads_ref[3:4, :]
    gdt_ref[0] = grad.astype(BF16)
    heads_sum_ref[0:1, :] += jnp.sum(grad, axis=0, keepdims=True)
    heads_sum_ref[1:2, :] += jnp.sum(da * dts, axis=0, keepdims=True) * rate


def finish_call(
    grad, act, xbc, halo, raw, dts, dev, tot, ds_end, q2, direct, da, c4, taps, bias, heads, ex, red,
    rows,
):
    seqs, length, width = xbc.shape
    inner = ds_end.shape[2]
    whole = lambda s, c: (0, 0)
    row = lambda s, c: (s, c, 0)
    per_seq = lambda s, c: (s, 0, 0)
    lane_block = pl.BlockSpec((1, rows, LANES), row)
    wide_block = pl.BlockSpec((1, rows, width), row)
    return pl.pallas_call(
        finish_kernel,
        grid=(seqs, length // rows),
        in_specs=[
            wide_block,
            wide_block,
            wide_block,
            pl.BlockSpec((1, 16, width), lambda s, c: (s, jnp.maximum(c * (rows // 16) - 1, 0), 0)),
            pl.BlockSpec((1, 16, width), per_seq),
            lane_block,
            lane_block,
            lane_block,
            pl.BlockSpec((1, 8, LANES), per_seq),
            pl.BlockSpec((1, STATE, inner), per_seq),
            lane_block,
            lane_block,
            lane_block,
            pl.BlockSpec((1, 8, LANES), per_seq),
            pl.BlockSpec(taps.shape, whole),
            pl.BlockSpec(bias.shape, whole),
            pl.BlockSpec(heads.shape, whole),
            pl.BlockSpec(ex.shape, whole),
            pl.BlockSpec(red.shape, whole),
        ],
        out_specs=[
            wide_block,
            lane_block,
            pl.BlockSpec((8, width), whole),
            pl.BlockSpec((8, LANES), whole),
        ],
        out_shape=[
            jax.ShapeDtypeStruct((seqs, length, width), F32),
            jax.ShapeDtypeStruct((seqs, length, LANES), BF16),
            jax.ShapeDtypeStruct((8, width), F32),
            jax.ShapeDtypeStruct((8, LANES), F32),
        ],
        scratch_shapes=[
            pltpu.VMEM((width // LANES, rows + 8, LANES), F32),
            pltpu.VMEM((8, LANES), F32),
        ],
        compiler_params=pltpu.CompilerParams(vmem_limit_bytes=VMEM_LIMIT),
        cost_estimate=cost(seqs * length, 21),
        name="conv_backward",
    )(
        grad, act, xbc, xbc, halo, raw, dts, dev, tot, ds_end, q2, direct, da, c4, taps, bias, heads,
        ex, red,
    )


def taps_back_kernel(
    g_ref, next_ref, after_ref, gdt_ref, normed_ref, taps_ref,
    gx_ref, gw_ref,
    ext_ref,
):
    s, c = pl.program_id(0), pl.program_id(1)
    rows, width = g_ref.shape[1], g_ref.shape[2]

    @pl.when(jnp.logical_and(s == 0, c == 0))
    def _():
        gw_ref[...] = jnp.zeros_like(gw_ref)

    last = c == pl.num_programs(1) - 1
    for block in range(width // LANES):
        cols = slice(block * LANES, (block + 1) * LANES)
        ext_ref[block, 0:rows, :] = g_ref[0, :, cols]
        ext_ref[block, rows : rows + 8, :] = jnp.where(
            last, after_ref[0, :, cols], next_ref[0, :, cols]
        )
        total = taps_ref[3:4, cols] * g_ref[0, :, cols]
        for k in range(3):
            total = total + taps_ref[k : k + 1, cols] * ext_ref[block, pl.ds(3 - k, rows), :]
        gx_ref[0, :, cols] = total.astype(BF16)
    gx_ref[0, :, width:] = gdt_ref[0]
    gw_ref[...] += tn(normed_ref[0], gx_ref[0])


def taps_back_call(gconv, after, gdt, normed, taps, rows):
    seqs, length, width = gconv.shape
    depth = normed.shape[2]
    whole = lambda s, c: (0, 0)
    row = lambda s, c: (s, c, 0)
    last = length // 8 - 1
    return pl.pallas_call(
        taps_back_kernel,
        grid=(seqs, length // rows),
        in_specs=[
            pl.BlockSpec((1, rows, width), row),
            pl.BlockSpec(
                (1, 8, width), lambda s, c: (s, jnp.minimum((c + 1) * (rows // 8), last), 0)
            ),
            pl.BlockSpec((1, 8, width), lambda s, c: (s, 0, 0)),
            pl.BlockSpec((1, rows, LANES), row),
            pl.BlockSpec((1, rows, depth), row),
            pl.BlockSpec(taps.shape, whole),
        ],
        out_specs=[
            pl.BlockSpec((1, rows, width + LANES), row),
            pl.BlockSpec((depth, width + LANES), whole),
        ],
        out_shape=[
            jax.ShapeDtypeStruct((seqs, length, width + LANES), BF16),
            jax.ShapeDtypeStruct((depth, width + LANES), F32),
        ],
        scratch_shapes=[pltpu.VMEM((width // LANES, rows + 8, LANES), F32)],
        compiler_params=pltpu.CompilerParams(vmem_limit_bytes=VMEM_LIMIT),
        cost_estimate=cost(seqs * length, 9),
        name="taps_backward",
    )(gconv, gconv, after, gdt, normed, taps)


def input_kernel(dz_ref, gx_ref, wz_ref, wx_ref, u_ref, c_ref, gain_ref, out_ref, sum_ref):
    @pl.when(jnp.logical_and(pl.program_id(0) == 0, pl.program_id(1) == 0))
    def _():
        sum_ref[...] = jnp.zeros_like(sum_ref)

    grad = nt(dz_ref[0], wz_ref[...]) + nt(gx_ref[0], wx_ref[...])
    u = u_ref[0].astype(F32)
    scale = lax.rsqrt(jnp.mean(u * u, axis=1, keepdims=True) + EPS)
    us = u * scale
    sum_ref[0:1, :] += jnp.sum(grad * us, axis=0, keepdims=True)
    h = grad * gain_ref[0:1, :]
    back = scale * (h - us * jnp.mean(h * us, axis=1, keepdims=True))
    out_ref[0] = c_ref[0].astype(F32) + back


def input_call(dz, gx, w_z, w_x, u, cot, gain, rows):
    seqs, length, depth = u.shape
    whole = lambda s, c: (0, 0)
    row = lambda s, c: (s, c, 0)
    return pl.pallas_call(
        input_kernel,
        grid=(seqs, length // rows),
        in_specs=[
            pl.BlockSpec((1, rows, dz.shape[2]), row),
            pl.BlockSpec((1, rows, gx.shape[2]), row),
            pl.BlockSpec(w_z.shape, whole),
            pl.BlockSpec(w_x.shape, whole),
            pl.BlockSpec((1, rows, depth), row),
            pl.BlockSpec((1, rows, depth), row),
            pl.BlockSpec(gain.shape, whole),
        ],
        out_specs=[pl.BlockSpec((1, rows, depth), row), pl.BlockSpec((8, depth), whole)],
        out_shape=[
            jax.ShapeDtypeStruct((seqs, length, depth), F32),
            jax.ShapeDtypeStruct((8, depth), F32),
        ],
        compiler_params=pltpu.CompilerParams(vmem_limit_bytes=VMEM_LIMIT),
        cost_estimate=cost(seqs * length, 9),
        name="input_gradient",
    )(dz, gx, w_z, w_x, u, cot, gain)


def to_all(value, size, axes):
    copies = jnp.broadcast_to(value[None], (size,) + value.shape)
    return lax.all_to_all(copies, axes, split_axis=0, concat_axis=0, tiled=True)


def other_core(value, sizes):
    return lax.ppermute(value, "dp", [(i, i ^ 1) for i in range(sizes["dp"])])


def both_cores(value, sizes, axis):
    other = other_core(value, sizes)
    first = lax.axis_index("dp") % 2 == 0
    return jnp.where(first, jnp.stack([value, other], axis), jnp.stack([other, value], axis))


def core_half(shard):
    half = shard.shape[0] // 2
    return lax.dynamic_slice_in_dim(shard, (lax.axis_index("dp") % 2) * half, half, 0)


def gather_rows(shard, sizes):
    got = to_all(core_half(shard), sizes["seq"], "seq").reshape(sizes["seq"], -1, shard.shape[1])
    return both_cores(got, sizes, 1).reshape(sizes["seq"] * shard.shape[0], shard.shape[1])


def gather_later(shards, sizes):
    columns = max(shard.shape[1] for shard in shards)
    halves = [core_half(shard).reshape(-1, columns) for shard in shards]
    got = lax.all_gather(jnp.concatenate(halves, axis=0), "seq", axis=0)
    other = other_core(got, sizes)
    first = lax.axis_index("dp") % 2 == 0
    outs, at = [], 0
    for shard, half in zip(shards, halves):
        rows = slice(at, at + half.shape[0])
        at += half.shape[0]
        mine, away = got[:, rows], other[:, rows]
        pair = jnp.where(first, jnp.stack([mine, away], 1), jnp.stack([away, mine], 1))
        outs.append(pair.reshape(sizes["seq"] * shard.shape[0], shard.shape[1]))
    return outs


def scatter_rows(grads, sizes):
    size = sizes["seq"]
    core = lax.axis_index("dp") % 2
    columns = max(grad.shape[1] for grad in grads)
    halves = []
    for grad in grads:
        parts = grad.reshape(size, 2, -1, grad.shape[1])
        mine = lax.dynamic_index_in_dim(parts, core, 1, keepdims=False)
        away = lax.dynamic_index_in_dim(parts, 1 - core, 1, keepdims=False).astype(BF16)
        half = (mine + other_core(away, sizes).astype(F32)).astype(BF16)
        halves.append(half.reshape(size, -1, columns))
    return lax.all_to_all(
        jnp.concatenate(halves, axis=1), "seq", split_axis=0, concat_axis=0, tiled=True
    )


def add_up(got, sizes):
    total = got.astype(F32).sum(axis=0)
    step = 2
    while step < sizes["dp"]:
        sent = total.astype(BF16)
        away = lax.ppermute(sent, "dp", [(i, i ^ step) for i in range(sizes["dp"])])
        total = sent.astype(F32) + away.astype(F32)
        step *= 2
    return total


def swap_rows(total, shapes, sizes):
    pair = both_cores(total, sizes, 0)
    outs, at = [], 0
    for rows, columns in shapes:
        count = rows * columns // (2 * sizes["seq"] * total.shape[1])
        outs.append(pair[:, at : at + count].reshape(rows // sizes["seq"], columns))
        at += count
    return outs


def sum_small(values, sizes, beside):
    flat = jnp.concatenate([value.reshape(-1) for value in values])
    count = flat.shape[0]
    flat = jnp.pad(flat, (0, -count % 1024)).reshape(-1, LANES)
    step = 1
    while step < sizes["dp"]:
        flat = flat + lax.ppermute(flat, "dp", [(i, i ^ step) for i in range(sizes["dp"])])
        step *= 2
    flat, beside = lax.optimization_barrier((to_all(flat, sizes["seq"], "seq"), beside))
    flat = flat.reshape(sizes["seq"], -1).sum(axis=0)
    out, at = [], 0
    for value in values:
        out.append(flat[at : at + value.size].reshape(value.shape))
        at += value.size
    return out, beside


def shift_in(value, size, step):
    pairs = [(i, i + step) for i in range(size) if 0 <= i + step < size]
    return lax.ppermute(value, "seq", pairs)


def carry_over(states, decay, size, step, beside):
    seqs, depth, inner = states.shape
    piece = depth // size
    sent = states.astype(BF16).reshape(seqs, size, piece, inner)
    got = lax.all_to_all(sent, "seq", split_axis=1, concat_axis=1, tiled=True)
    got, beside = lax.optimization_barrier((got, beside))
    got = got.astype(F32)
    order = range(size) if step > 0 else range(size - 1, -1, -1)
    held = jnp.zeros((seqs, piece, inner), F32)
    into = [None] * size
    for i in order:
        into[i] = held
        held = held * decay[i][:, None, :] + got[:, i]
    back = jnp.stack(into, axis=1).astype(BF16)
    back = lax.all_to_all(back, "seq", split_axis=1, concat_axis=1, tiled=True)
    return back.reshape(seqs, depth, inner), beside


def rms_gain(values, gain):
    return values * lax.rsqrt(jnp.mean(values * values, axis=-1, keepdims=True) + EPS) * gain


def body(
    sizes, inputs, w_in, w_out, norm_gain, conv_weight, conv_bias, dt_bias, a_log, skip, gate_gain,
    cotangent,
):
    size = sizes["seq"]
    seqs, length, depth = inputs.shape
    inner = gate_gain.shape[0]
    width = conv_weight.shape[1]
    tokens = seqs * length
    rows = min(256, length)

    w_x = gather_rows(jnp.pad(w_in[:, inner:], ((0, 0), (0, LANES - HEADS))), sizes)
    w_z, full_out = gather_later([w_in[:, :inner], w_out], sizes)

    def pad_heads(values):
        return jnp.pad(values, (0, LANES - HEADS))

    rates = -jnp.exp(a_log)
    heads = jnp.stack([pad_heads(dt_bias), pad_heads(rates), pad_heads(skip), pad_heads(jnp.ones_like(skip))])
    heads = jnp.pad(heads, ((0, 4), (0, 0)))
    taps = jnp.pad(conv_weight, ((0, 4), (0, 0)))
    bias = jnp.pad(conv_bias[None, :], ((0, 7), (0, 0)))
    vecs = jnp.pad(jnp.stack([gate_gain, jnp.repeat(skip, HEADDIM)]), ((0, 6), (0, 0)))
    ex, red = head_matrices(inner)

    edge = shift_in(inputs[:, length - 16 :], size, 1).astype(F32)
    edge = rms_gain(edge, norm_gain).astype(BF16).reshape(seqs * 16, depth)
    normed = rms_gain(inputs.astype(F32), norm_gain).astype(BF16)
    flat = normed.reshape(tokens, depth)

    def project(left, matrix):
        return jnp.dot(left, matrix, preferred_element_type=F32).astype(BF16)

    halo = project(edge, w_x)[:, :width].reshape(seqs, 16, width)
    xbc = project(flat, w_x[:, :width]).reshape(seqs, length, width)
    raw = project(flat, w_x[:, width:]).reshape(seqs, length, LANES)

    total = (softplus(raw.astype(F32) + heads[0]) * heads[3]).sum(axis=1) * heads[1]
    decay = jnp.exp(to_all(total, size, "seq").reshape(size, seqs, LANES)[:, :, :HEADS])
    decay = jnp.repeat(decay, HEADDIM, axis=2)
    act, y, dts, cum, dev, states, final = scan_call(xbc, halo, raw, taps, bias, heads, ex, inner)
    final, decay = lax.optimization_barrier((final, decay))
    z = project(flat, w_z).reshape(seqs, length, inner)
    s_in, z = carry_over(final, decay, size, 1, z)

    mixed, dy, dz, normalized, row_sums, q2, gate_sums, ds_loc = gate_call(
        y, act, z, dev, s_in, inputs, cotangent, full_out, vecs, ex, red, rows
    )
    grad_out, grad_z = weights_call(normalized, cotangent, normed, dz, min(512, length))
    ds_end, weight_grads = carry_over(ds_loc, decay, size, -1, (grad_out, grad_z))
    got_zo = scatter_rows(weight_grads, sizes)

    grad, direct, da = back_call(act, dy, dts, cum, dev, states, s_in, row_sums, vecs, ex, red)

    both = (s_in.astype(F32) * ds_end.astype(F32)).sum(axis=1).reshape(seqs, HEADS, HEADDIM).sum(axis=2)
    both = jnp.pad(both, ((0, 0), (0, LANES - HEADS))) * jnp.exp(total)
    c4 = jnp.broadcast_to((both + q2.sum(axis=1))[:, None, :], (seqs, 8, LANES))
    tot = jnp.broadcast_to(total[:, None, :], (seqs, 8, LANES))
    gconv, gdt, taps_sum, heads_sum = finish_call(
        grad, act, xbc, halo, raw, dts, dev, tot, ds_end, q2, direct, da, c4, taps, bias, heads, ex,
        red, rows,
    )
    after = shift_in(gconv[:, :8], size, -1)
    gx, grad_x = taps_back_call(gconv, after, gdt, normed, taps, rows)
    gx, grad_x, got_zo = lax.optimization_barrier((gx, grad_x, got_zo))
    got_x = scatter_rows([grad_x], sizes)
    total_zo = add_up(got_zo, sizes)
    gain = jnp.pad(norm_gain[None, :], ((0, 7), (0, 0)))
    grad_inputs, gain_sum = input_call(dz, gx, w_z, w_x, inputs, cotangent, gain, rows)
    got_x, gain_sum, total_zo = lax.optimization_barrier((got_x, gain_sum, total_zo))
    rows_out, rows_z = swap_rows(total_zo, [grad_out.shape, grad_z.shape], sizes)
    total_x = add_up(got_x, sizes)
    sums, total_x = sum_small(
        (
            gain_sum[0],
            taps_sum[:4],
            taps_sum[4],
            heads_sum[0, :HEADS],
            heads_sum[1, :HEADS],
            gate_sums[1].reshape(HEADS, HEADDIM).sum(axis=1),
            gate_sums[0],
        ),
        sizes,
        total_x,
    )
    (rows_x,) = swap_rows(total_x, [grad_x.shape], sizes)

    rows_in = jnp.concatenate([rows_z, rows_x[:, : width + HEADS]], axis=1)
    return (mixed, grad_inputs, rows_in, rows_out, *sums)


def solution(mesh):
    placed = (
        P("dp", "seq", None),
        P("seq", None),
        P("seq", None),
        P(),
        P(),
        P(),
        P(),
        P(),
        P(),
        P(),
        P("dp", "seq", None),
    )
    return jax.shard_map(
        functools.partial(body, dict(mesh.shape)),
        mesh=mesh,
        in_specs=placed,
        out_specs=(
            P("dp", "seq", None),
            P("dp", "seq", None),
            P("seq", None),
            P("seq", None),
            P(),
            P(),
            P(),
            P(),
            P(),
            P(),
            P(),
        ),
        check_vma=False,
    )
```

```python
import functools

import jax
import jax.numpy as jnp
from jax import lax
from jax.experimental import pallas as pl
from jax.experimental.pallas import tpu as pltpu
from jax.sharding import PartitionSpec as P

HEADS = 24
HEADDIM = 64
STATE = 128
LANES = 128
Q = 128
SUB = 2
QUAD = 256
EPS = 1e-05
F32 = jnp.float32
BF16 = jnp.bfloat16
VMEM_LIMIT = 56 * 1024 * 1024


def cost(tokens, per_token_ns):
    seconds = tokens * per_token_ns * 1e-9
    return pl.CostEstimate(
        flops=int(seconds * 1e15), bytes_accessed=int(seconds * 3e12), transcendentals=0
    )


def dot(left, right, dims):
    return lax.dot_general(left, right, (dims, ((), ())), preferred_element_type=F32)


def nn(left, right):
    return dot(left, right, ((1,), (0,)))


def nt(left, right):
    return dot(left, right, ((1,), (1,)))


def tn(left, right):
    return dot(left, right, ((0,), (0,)))


def exact(left, right):
    return lax.dot_general(
        left, right, (((1,), (0,)), ((), ())), precision=lax.Precision.HIGHEST,
        preferred_element_type=F32,
    )


def split2(values):
    high = values.astype(BF16)
    rest = (values - high.astype(F32)).astype(BF16)
    return jnp.concatenate([high, rest], axis=1)


def sigmoid(values):
    return 0.5 + 0.5 * jnp.tanh(0.5 * values)


def softplus(values):
    return jnp.maximum(values, 0.0) + jnp.log1p(jnp.exp(-jnp.abs(values)))


def iotas(rows, cols):
    return (
        lax.broadcasted_iota(jnp.int32, (rows, cols), 0),
        lax.broadcasted_iota(jnp.int32, (rows, cols), 1),
    )


def head_matrices(inner):
    col_head = jnp.arange(inner) // HEADDIM
    expand = (jnp.arange(LANES)[:, None] == col_head[None, :]).astype(BF16)
    return jnp.concatenate([expand, expand], axis=0), expand.T


def block_pair(pair):
    low = lax.broadcasted_iota(jnp.int32, pair.shape, 1) < HEADDIM
    zero = jnp.zeros_like(pair)
    return jnp.concatenate([jnp.where(low, pair, zero), jnp.where(low, zero, pair)], axis=0)


def shifted(ext_ref, start, rows):
    block = start // LANES
    return [ext_ref[block, pl.ds(5 + k, rows), :] for k in range(4)]


def conv_columns(views, taps_ref, bias_ref, cols):
    total = bias_ref[0:1, cols] + taps_ref[0:1, cols] * views[0]
    for k in range(1, 4):
        total = total + taps_ref[k : k + 1, cols] * views[k]
    return total


def fill_ext(ext_ref, xbc_ref, prev_ref, halo_ref, first):
    rows = xbc_ref.shape[1]
    for block in range(ext_ref.shape[0]):
        cols = slice(block * LANES, (block + 1) * LANES)
        before = jnp.where(
            first, halo_ref[0, :, cols].astype(F32), prev_ref[0, :, cols].astype(F32)
        )
        ext_ref[block, 0:8, :] = before[8:16]
        ext_ref[block, pl.ds(8, rows), :] = xbc_ref[0, :, cols].astype(F32)


def scan_kernel(
    xbc_ref, prev_ref, halo_ref, raw_ref, taps_ref, bias_ref, heads_ref, ex_ref,
    act_ref, y_ref, dt_ref, cum_ref, dev_ref, st_ref, fin_ref,
    ext_ref, state_ref, carry_ref,
):
    c = pl.program_id(1)
    rows, width = xbc_ref.shape[1], xbc_ref.shape[2]
    inner = y_ref.shape[2]

    @pl.when(c == 0)
    def _():
        state_ref[...] = jnp.zeros_like(state_ref)
        carry_ref[...] = jnp.zeros_like(carry_ref)

    fill_ext(ext_ref, xbc_ref, prev_ref, halo_ref, c == 0)
    for start in range(0, width, LANES):
        cols = slice(start, start + LANES)
        half = 0.5 * conv_columns(shifted(ext_ref, start, rows), taps_ref, bias_ref, cols)
        act_ref[0, :, cols] = (half + half * jnp.tanh(half)).astype(BF16)

    row, col = iotas(Q, Q)
    lower = row >= col
    before = carry_ref[0:1, :]
    held, factors = [], []
    for sub in range(rows // Q):
        at = slice(sub * Q, (sub + 1) * Q)
        dts = softplus(raw_ref[0, at].astype(F32) + heads_ref[0:1, :]) * heads_ref[3:4, :]
        cum = exact(lower.astype(F32), dts * heads_ref[1:2, :])
        dt_ref[0, at] = dts
        cum_ref[0, at] = cum
        dev_ref[0, at] = cum + before
        before = before + cum[Q - 1 : Q, :]
        bmat = act_ref[0, at, inner : inner + STATE]
        cmat = act_ref[0, at, inner + STATE : inner + 2 * STATE]
        factors += [dts, jnp.exp(cum), jnp.exp(cum[Q - 1 : Q, :] - cum)]
        held.append((
            at, cum, cum.T, cmat, bmat.astype(F32).T.astype(BF16),
            jnp.where(lower, nt(cmat, bmat), 0.0),
        ))
    factors = jnp.concatenate([split2(factor) for factor in factors], axis=0)
    carry_ref[...] = jnp.broadcast_to(before, carry_ref.shape)

    for quad in range(inner // QUAD):
        cols = slice(quad * QUAD, (quad + 1) * QUAD)
        wide = nn(factors, ex_ref[:, cols])
        state = state_ref[:, cols]
        for sub, (at, cum, cum_t, cmat, bmat_t, scores) in enumerate(held):
            dte, ece, tle = (wide[(3 * sub + k) * Q : (3 * sub + k + 1) * Q] for k in range(3))
            xdt = act_ref[0, at, cols].astype(F32) * dte
            xdt_b = xdt.astype(BF16)
            xtail = (xdt * tle).astype(BF16)
            parts = []
            for pair in range(2):
                mats = []
                for h in (quad * 4 + pair * 2, quad * 4 + pair * 2 + 1):
                    diff = cum[:, h : h + 1] - cum_t[h : h + 1, :]
                    mats.append((scores * jnp.exp(jnp.minimum(diff, 0.0))).astype(BF16))
                mat = jnp.concatenate(mats, axis=1)
                parts.append(nn(mat, block_pair(xdt_b[:, pair * LANES : (pair + 1) * LANES])))
            state_b = state.astype(BF16)
            st_ref[0, sub, :, cols] = state_b
            y_ref[0, at, cols] = jnp.concatenate(parts, axis=1) + ece * nn(cmat, state_b)
            state = state * ece[Q - 1 : Q, :] + nn(bmat_t, xtail)
        state_ref[:, cols] = state
        fin_ref[0, :, cols] = state


def scan_call(xbc, halo, raw, taps, bias, heads, ex, inner):
    seqs, length, width = xbc.shape
    chunks = length // Q
    rows = SUB * Q
    whole = lambda s, c: (0, 0)
    row = lambda s, c: (s, c, 0)
    lanes = jax.ShapeDtypeStruct((seqs, length, LANES), F32)
    return pl.pallas_call(
        scan_kernel,
        grid=(seqs, length // rows),
        in_specs=[
            pl.BlockSpec((1, rows, width), row),
            pl.BlockSpec((1, 16, width), lambda s, c: (s, jnp.maximum(c * (rows // 16) - 1, 0), 0)),
            pl.BlockSpec((1, 16, width), lambda s, c: (s, 0, 0)),
            pl.BlockSpec((1, rows, LANES), row),
            pl.BlockSpec(taps.shape, whole),
            pl.BlockSpec(bias.shape, whole),
            pl.BlockSpec(heads.shape, whole),
            pl.BlockSpec(ex.shape, whole),
        ],
        out_specs=[
            pl.BlockSpec((1, rows, width), row),
            pl.BlockSpec((1, rows, inner), row),
            pl.BlockSpec((1, rows, LANES), row),
            pl.BlockSpec((1, rows, LANES), row),
            pl.BlockSpec((1, rows, LANES), row),
            pl.BlockSpec((1, SUB, STATE, inner), lambda s, c: (s, c, 0, 0)),
            pl.BlockSpec((1, STATE, inner), lambda s, c: (s, 0, 0)),
        ],
        out_shape=[
            jax.ShapeDtypeStruct((seqs, length, width), BF16),
            jax.ShapeDtypeStruct((seqs, length, inner), F32),
            lanes,
            lanes,
            lanes,
            jax.ShapeDtypeStruct((seqs, chunks, STATE, inner), BF16),
            jax.ShapeDtypeStruct((seqs, STATE, inner), F32),
        ],
        scratch_shapes=[
            pltpu.VMEM((width // LANES, rows + 8, LANES), F32),
            pltpu.VMEM((STATE, inner), F32),
            pltpu.VMEM((8, LANES), F32),
        ],
        compiler_params=pltpu.CompilerParams(vmem_limit_bytes=VMEM_LIMIT),
        cost_estimate=cost(seqs * length, 20),
        name="scan_forward",
    )(xbc, xbc, halo, raw, taps, bias, heads, ex)


def gate_kernel(
    y_ref, act_ref, z_ref, dev_ref, sin_ref, u_ref, c_ref, w_ref, vec_ref, ex_ref, red_ref,
    mixed_ref, dy_ref, dz_ref, norm_ref, rows_ref, q2_ref, sums_ref, ds_ref,
):
    s, i = pl.program_id(0), pl.program_id(1)
    inner = y_ref.shape[2]

    @pl.when(jnp.logical_and(s == 0, i == 0))
    def _():
        sums_ref[...] = jnp.zeros_like(sums_ref)

    @pl.when(i == 0)
    def _():
        ds_ref[...] = jnp.zeros_like(ds_ref)

    cmat = act_ref[0, :, inner + STATE : inner + 2 * STATE]
    ec2 = split2(jnp.exp(dev_ref[0]))
    ece = nn(ec2, ex_ref[...])
    x = act_ref[0, :, :inner].astype(F32)
    y_loc = y_ref[0]
    y_in = ece * nn(cmat, sin_ref[0])
    y = (y_loc + y_in + vec_ref[1:2, :] * x).astype(BF16).astype(F32)
    z = z_ref[0].astype(F32)
    sig = sigmoid(z)
    silu = z * sig
    g = y * silu
    scale = lax.rsqrt(jnp.mean(g * g, axis=1, keepdims=True) + EPS)
    gain = vec_ref[0:1, :]
    gs = g * scale
    normalized = (gs * gain).astype(BF16)
    norm_ref[0] = normalized
    mixed_ref[0] = (u_ref[0].astype(F32) + nn(normalized, w_ref[...])).astype(BF16)
    gn = nt(c_ref[0], w_ref[...])
    sums_ref[0:1, :] += jnp.sum(gn * gs, axis=0, keepdims=True)
    h = gn * gain
    dg = scale * (h - gs * jnp.mean(h * gs, axis=1, keepdims=True))
    dy_b = (dg * silu).astype(BF16)
    dy = dy_b.astype(F32)
    dy_ref[0] = dy_b
    dz_ref[0] = (dg * y * (sig + silu * (1.0 - sig))).astype(BF16)
    sums_ref[1:2, :] += jnp.sum(dy * x, axis=0, keepdims=True)
    rows = dy * y_loc
    high = rows.astype(BF16)
    rest = (rows - high.astype(F32)).astype(BF16)
    rows_ref[0] = nn(high, red_ref[...]) + nn(rest, red_ref[...])
    q2_ref[0] = nn((dy * y_in).astype(BF16), red_ref[...])
    ds_ref[0] += tn(cmat, (dy * ece).astype(BF16))


def gate_call(y, act, z, dev, s_in, u, cot, w_out, vecs, ex, red, rows):
    seqs, length, inner = y.shape
    width = act.shape[2]
    depth = u.shape[2]
    whole = lambda s, c: (0, 0)
    row = lambda s, c: (s, c, 0)
    per_seq = lambda s, c: (s, 0, 0)
    lanes = jax.ShapeDtypeStruct((seqs, length, LANES), F32)
    wide = jax.ShapeDtypeStruct((seqs, length, inner), BF16)
    return pl.pallas_call(
        gate_kernel,
        grid=(seqs, length // rows),
        in_specs=[
            pl.BlockSpec((1, rows, inner), row),
            pl.BlockSpec((1, rows, width), row),
            pl.BlockSpec((1, rows, inner), row),
            pl.BlockSpec((1, rows, LANES), row),
            pl.BlockSpec((1, STATE, inner), per_seq),
            pl.BlockSpec((1, rows, depth), row),
            pl.BlockSpec((1, rows, depth), row),
            pl.BlockSpec(w_out.shape, whole),
            pl.BlockSpec(vecs.shape, whole),
            pl.BlockSpec(ex.shape, whole),
            pl.BlockSpec(red.shape, whole),
        ],
        out_specs=[
            pl.BlockSpec((1, rows, depth), row),
            pl.BlockSpec((1, rows, inner), row),
            pl.BlockSpec((1, rows, inner), row),
            pl.BlockSpec((1, rows, inner), row),
            pl.BlockSpec((1, rows, LANES), row),
            pl.BlockSpec((1, rows, LANES), row),
            pl.BlockSpec((8, inner), whole),
            pl.BlockSpec((1, STATE, inner), per_seq),
        ],
        out_shape=[
            jax.ShapeDtypeStruct((seqs, length, depth), BF16),
            wide,
            wide,
            wide,
            lanes,
            lanes,
            jax.ShapeDtypeStruct((8, inner), F32),
            jax.ShapeDtypeStruct((seqs, STATE, inner), F32),
        ],
        compiler_params=pltpu.CompilerParams(vmem_limit_bytes=VMEM_LIMIT),
        cost_estimate=cost(seqs * length, 22),
        name="gate_and_output",
    )(y, act, z, dev, s_in, u, cot, w_out, vecs, ex, red)


def weights_kernel(norm_ref, c_ref, n_ref, dz_ref, gwo_ref, gwz_ref):
    @pl.when(jnp.logical_and(pl.program_id(0) == 0, pl.program_id(1) == 0))
    def _():
        gwo_ref[...] = jnp.zeros_like(gwo_ref)
        gwz_ref[...] = jnp.zeros_like(gwz_ref)

    gwo_ref[...] += tn(norm_ref[0], c_ref[0])
    gwz_ref[...] += tn(n_ref[0], dz_ref[0])


def weights_call(normalized, cot, normed, dz, rows):
    seqs, length, inner = dz.shape
    depth = cot.shape[2]
    whole = lambda s, c: (0, 0)
    row = lambda s, c: (s, c, 0)
    return pl.pallas_call(
        weights_kernel,
        grid=(seqs, length // rows),
        in_specs=[
            pl.BlockSpec((1, rows, inner), row),
            pl.BlockSpec((1, rows, depth), row),
            pl.BlockSpec((1, rows, depth), row),
            pl.BlockSpec((1, rows, inner), row),
        ],
        out_specs=[pl.BlockSpec((inner, depth), whole), pl.BlockSpec((depth, inner), whole)],
        out_shape=[
            jax.ShapeDtypeStruct((inner, depth), F32),
            jax.ShapeDtypeStruct((depth, inner), F32),
        ],
        compiler_params=pltpu.CompilerParams(vmem_limit_bytes=VMEM_LIMIT),
        cost_estimate=cost(seqs * length, 8),
        name="weight_gradients",
    )(normalized, cot, normed, dz)


def back_kernel(
    act_ref, dy_ref, dt_ref, cum_ref, dev_ref, st_ref, sin_ref, rows_ref, vec_ref, ex_ref, red_ref,
    g_ref, direct_ref, da_ref,
    ds_ref,
):
    inner = dy_ref.shape[2]

    @pl.when(pl.program_id(1) == 0)
    def _():
        ds_ref[...] = jnp.zeros_like(ds_ref)

    row, col = iotas(Q, Q)
    upper = row <= col
    subs = range(dy_ref.shape[1] // Q)
    held, sums, factors = [], [], []
    for sub in subs:
        at = slice(sub * Q, (sub + 1) * Q)
        bmat = act_ref[0, at, inner : inner + STATE]
        cmat = act_ref[0, at, inner + STATE : inner + 2 * STATE]
        cum = cum_ref[0, at]
        held.append((
            at, bmat, cmat.astype(F32).T.astype(BF16), jnp.where(upper, nt(bmat, cmat), 0.0), cum,
            cum.T,
        ))
        factors += [
            dt_ref[0, at], jnp.exp(cum), jnp.exp(cum[Q - 1 : Q, :] - cum),
            jnp.exp(dev_ref[0, sub * Q : sub * Q + 16, :] - cum[0:16, :]),
        ]
        square = jnp.zeros((Q, LANES), F32)
        sums.append([square] * 5 + [jnp.zeros((16, LANES), F32)])
    factors = jnp.concatenate([split2(factor) for factor in factors], axis=0)

    for quad in range(inner // QUAD):
        cols = slice(quad * QUAD, (quad + 1) * QUAD)
        wide = nn(factors, ex_ref[:, cols])
        red = red_ref[cols, :]
        ds = ds_ref[:, cols]
        for sub in reversed(subs):
            at, bmat, cmat_t, scores, cum, cum_t = held[sub]
            d_scores, db, dc, col_sums, w_loc, const = sums[sub]
            base = sub * (3 * Q + 16)
            dte, ece, tle = (wide[base + k * Q : base + (k + 1) * Q] for k in range(3))
            before = wide[base + 3 * Q : base + 3 * Q + 1]
            x = act_ref[0, at, cols].astype(F32)
            xdt_b = (x * dte).astype(BF16)
            xdt = xdt_b.astype(F32)
            dy_b = dy_ref[0, at, cols]
            dy = dy_b.astype(F32)
            parts = []
            for pair in range(2):
                lanes = slice(pair * LANES, (pair + 1) * LANES)
                stacked = block_pair(dy_b[:, lanes])
                d_mat = nt(xdt_b[:, lanes], stacked)
                mats = []
                for j in range(2):
                    h = quad * 4 + pair * 2 + j
                    decay = jnp.exp(jnp.minimum(cum_t[h : h + 1, :] - cum[:, h : h + 1], 0.0))
                    mats.append((scores * decay).astype(BF16))
                    d_scores = d_scores + d_mat[:, j * Q : (j + 1) * Q] * decay
                parts.append(nn(jnp.concatenate(mats, axis=1), stacked))
            ds_b = ds.astype(BF16)
            st = st_ref[0, sub, :, cols].astype(F32)
            state_b = (st + before * sin_ref[0, :, cols].astype(F32)).astype(BF16)
            dx_intra = jnp.concatenate(parts, axis=1)
            dx_inter = tle * nn(bmat, ds_b)
            dxp = dx_intra + dx_inter
            g_ref[0, at, cols] = dte * dxp + vec_ref[1:2, cols] * dy
            last = ece[Q - 1 : Q, :]
            both = jnp.sum(st * ds, axis=0, keepdims=True) * last
            stack = []
            for value in (xdt * dx_intra, jnp.broadcast_to(both, (16, QUAD))):
                high = value.astype(BF16)
                stack += [high, (value - high.astype(F32)).astype(BF16)]
            stack.append((xdt * dx_inter).astype(BF16))
            by_head = nn(jnp.concatenate(stack, axis=0), red)
            col_sums = col_sums + by_head[:Q] + by_head[Q : 2 * Q]
            const = const + by_head[2 * Q : 2 * Q + 16] + by_head[2 * Q + 16 : 2 * Q + 32]
            w_loc = w_loc + by_head[2 * Q + 32 :]
            db = db + nt((xdt * tle).astype(BF16), ds_b)
            dye = (dy * ece).astype(BF16)
            dc = dc + nt(dye, state_b)
            ds = ds * last + nn(cmat_t, dye)
            sums[sub] = [d_scores, db, dc, col_sums, w_loc, const]
        ds_ref[:, cols] = ds
    for sub in subs:
        at, bmat = held[sub][:2]
        cmat = act_ref[0, at, inner + STATE : inner + 2 * STATE]
        d_scores, db, dc, col_sums, w_loc, const = sums[sub]
        d_scores = jnp.where(upper, d_scores, 0.0)
        g_ref[0, at, inner : inner + STATE] = db + nn(d_scores.astype(BF16), cmat)
        g_ref[0, at, inner + STATE :] = dc + nn(d_scores.T.astype(BF16), bmat)
        direct_ref[0, at] = col_sums + w_loc
        da_ref[0, at] = (
            exact(upper.astype(F32), rows_ref[0, at] - col_sums)
            + exact((row > col).astype(F32), w_loc)
            + const[0:1, :]
        )


def back_call(act, dy, dts, cum, dev, states, s_in, rows, vecs, ex, red):
    seqs, length, width = act.shape
    inner = dy.shape[2]
    step = SUB * Q
    steps = length // step
    whole = lambda s, c: (0, 0)
    row = lambda s, c: (s, steps - 1 - c, 0)
    lanes = jax.ShapeDtypeStruct((seqs, length, LANES), F32)
    lane_block = pl.BlockSpec((1, step, LANES), row)
    return pl.pallas_call(
        back_kernel,
        grid=(seqs, steps),
        in_specs=[
            pl.BlockSpec((1, step, width), row),
            pl.BlockSpec((1, step, inner), row),
            lane_block,
            lane_block,
            lane_block,
            pl.BlockSpec((1, SUB, STATE, inner), lambda s, c: (s, steps - 1 - c, 0, 0)),
            pl.BlockSpec((1, STATE, inner), lambda s, c: (s, 0, 0)),
            lane_block,
            pl.BlockSpec(vecs.shape, whole),
            pl.BlockSpec(ex.shape, whole),
            pl.BlockSpec(red.shape, whole),
        ],
        out_specs=[pl.BlockSpec((1, step, width), row), lane_block, lane_block],
        out_shape=[jax.ShapeDtypeStruct((seqs, length, width), F32), lanes, lanes],
        scratch_shapes=[pltpu.VMEM((STATE, inner), F32)],
        compiler_params=pltpu.CompilerParams(vmem_limit_bytes=VMEM_LIMIT),
        cost_estimate=cost(seqs * length, 29),
        name="scan_backward",
    )(act, dy, dts, cum, dev, states, s_in, rows, vecs, ex, red)


def finish_kernel(
    g_ref, act_ref, xbc_ref, prev_ref, halo_ref, raw_ref, dt_ref, dev_ref, tot_ref, ds_ref, q2_ref,
    direct_ref, da_ref, c4_ref, taps_ref, bias_ref, heads_ref, ex_ref, red_ref,
    gconv_ref, gdt_ref, taps_sum_ref, heads_sum_ref,
    ext_ref, carry_ref,
):
    s, c = pl.program_id(0), pl.program_id(1)
    width = xbc_ref.shape[2]
    inner = ds_ref.shape[2]
    rows = xbc_ref.shape[1]

    @pl.when(jnp.logical_and(s == 0, c == 0))
    def _():
        taps_sum_ref[...] = jnp.zeros_like(taps_sum_ref)
        heads_sum_ref[...] = jnp.zeros_like(heads_sum_ref)

    @pl.when(c == 0)
    def _():
        carry_ref[...] = jnp.zeros_like(carry_ref)

    fill_ext(ext_ref, xbc_ref, prev_ref, halo_ref, c == 0)

    def conv_back(grads, quad_cols):
        for j in range(QUAD // LANES):
            start = quad_cols.start + j * LANES
            cols = slice(start, start + LANES)
            views = shifted(ext_ref, start, rows)
            conv = conv_columns(views, taps_ref, bias_ref, cols)
            sig = sigmoid(conv)
            out = grads[:, j * LANES : (j + 1) * LANES] * (sig + conv * sig * (1.0 - sig))
            gconv_ref[0, :, cols] = out
            for k in range(4):
                taps_sum_ref[k : k + 1, cols] += jnp.sum(out * views[k], axis=0, keepdims=True)
            taps_sum_ref[4:5, cols] += jnp.sum(out, axis=0, keepdims=True)

    bmat = act_ref[0, :, inner : inner + STATE]
    dts = dt_ref[0]
    tails = jnp.exp(tot_ref[0, 0:1, :] - dev_ref[0])
    factors = jnp.concatenate([split2(dts), split2(tails)], axis=0)
    db = jnp.zeros((rows, STATE), F32)
    q3 = jnp.zeros((rows, LANES), F32)
    for quad in range(inner // QUAD):
        cols = slice(quad * QUAD, (quad + 1) * QUAD)
        wide = nn(factors, ex_ref[:, cols])
        red = red_ref[cols, :]
        dte, tle = wide[:rows], wide[rows:]
        xdt = (act_ref[0, :, cols].astype(F32) * dte).astype(BF16).astype(F32)
        ds_b = ds_ref[0, :, cols]
        dxc = tle * nn(bmat, ds_b)
        q3 = q3 + nn((xdt * dxc).astype(BF16), red)
        db = db + nt((xdt * tle).astype(BF16), ds_b)
        conv_back(g_ref[0, :, cols] + dte * dxc, cols)
    db_all = jnp.concatenate([db, jnp.zeros_like(db)], axis=1)
    cols = slice(inner, inner + QUAD)
    conv_back(g_ref[0, :, cols] + db_all, cols)

    step = q3 - q2_ref[0]
    row, col = iotas(rows, rows)
    prefix = exact((row > col).astype(F32), step) + carry_ref[0:1, :]
    carry_ref[...] = carry_ref[...] + jnp.sum(step, axis=0, keepdims=True)
    da = da_ref[0] + c4_ref[0, 0:1, :] + prefix
    rate = heads_ref[1:2, :]
    raw = raw_ref[0].astype(F32) + heads_ref[0:1, :]
    direct = (direct_ref[0] + q3) / jnp.maximum(dts, 1e-30)
    grad = (direct + rate * da) * sigmoid(raw) * heads_ref[3:4, :]
    gdt_ref[0] = grad.astype(BF16)
    heads_sum_ref[0:1, :] += jnp.sum(grad, axis=0, keepdims=True)
    heads_sum_ref[1:2, :] += jnp.sum(da * dts, axis=0, keepdims=True) * rate


def finish_call(
    grad, act, xbc, halo, raw, dts, dev, tot, ds_end, q2, direct, da, c4, taps, bias, heads, ex, red,
    rows,
):
    seqs, length, width = xbc.shape
    inner = ds_end.shape[2]
    whole = lambda s, c: (0, 0)
    row = lambda s, c: (s, c, 0)
    per_seq = lambda s, c: (s, 0, 0)
    lane_block = pl.BlockSpec((1, rows, LANES), row)
    wide_block = pl.BlockSpec((1, rows, width), row)
    return pl.pallas_call(
        finish_kernel,
        grid=(seqs, length // rows),
        in_specs=[
            wide_block,
            wide_block,
            wide_block,
            pl.BlockSpec((1, 16, width), lambda s, c: (s, jnp.maximum(c * (rows // 16) - 1, 0), 0)),
            pl.BlockSpec((1, 16, width), per_seq),
            lane_block,
            lane_block,
            lane_block,
            pl.BlockSpec((1, 8, LANES), per_seq),
            pl.BlockSpec((1, STATE, inner), per_seq),
            lane_block,
            lane_block,
            lane_block,
            pl.BlockSpec((1, 8, LANES), per_seq),
            pl.BlockSpec(taps.shape, whole),
            pl.BlockSpec(bias.shape, whole),
            pl.BlockSpec(heads.shape, whole),
            pl.BlockSpec(ex.shape, whole),
            pl.BlockSpec(red.shape, whole),
        ],
        out_specs=[
            wide_block,
            lane_block,
            pl.BlockSpec((8, width), whole),
            pl.BlockSpec((8, LANES), whole),
        ],
        out_shape=[
            jax.ShapeDtypeStruct((seqs, length, width), F32),
            jax.ShapeDtypeStruct((seqs, length, LANES), BF16),
            jax.ShapeDtypeStruct((8, width), F32),
            jax.ShapeDtypeStruct((8, LANES), F32),
        ],
        scratch_shapes=[
            pltpu.VMEM((width // LANES, rows + 8, LANES), F32),
            pltpu.VMEM((8, LANES), F32),
        ],
        compiler_params=pltpu.CompilerParams(vmem_limit_bytes=VMEM_LIMIT),
        cost_estimate=cost(seqs * length, 21),
        name="conv_backward",
    )(
        grad, act, xbc, xbc, halo, raw, dts, dev, tot, ds_end, q2, direct, da, c4, taps, bias, heads,
        ex, red,
    )


def taps_back_kernel(
    g_ref, next_ref, after_ref, gdt_ref, normed_ref, taps_ref,
    gx_ref, gw_ref,
    ext_ref,
):
    s, c = pl.program_id(0), pl.program_id(1)
    rows, width = g_ref.shape[1], g_ref.shape[2]

    @pl.when(jnp.logical_and(s == 0, c == 0))
    def _():
        gw_ref[...] = jnp.zeros_like(gw_ref)

    last = c == pl.num_programs(1) - 1
    for block in range(width // LANES):
        cols = slice(block * LANES, (block + 1) * LANES)
        ext_ref[block, 0:rows, :] = g_ref[0, :, cols]
        ext_ref[block, rows : rows + 8, :] = jnp.where(
            last, after_ref[0, :, cols], next_ref[0, :, cols]
        )
        total = taps_ref[3:4, cols] * g_ref[0, :, cols]
        for k in range(3):
            total = total + taps_ref[k : k + 1, cols] * ext_ref[block, pl.ds(3 - k, rows), :]
        gx_ref[0, :, cols] = total.astype(BF16)
    gx_ref[0, :, width:] = gdt_ref[0]
    gw_ref[...] += tn(normed_ref[0], gx_ref[0])


def taps_back_call(gconv, after, gdt, normed, taps, rows):
    seqs, length, width = gconv.shape
    depth = normed.shape[2]
    whole = lambda s, c: (0, 0)
    row = lambda s, c: (s, c, 0)
    last = length // 8 - 1
    return pl.pallas_call(
        taps_back_kernel,
        grid=(seqs, length // rows),
        in_specs=[
            pl.BlockSpec((1, rows, width), row),
            pl.BlockSpec(
                (1, 8, width), lambda s, c: (s, jnp.minimum((c + 1) * (rows // 8), last), 0)
            ),
            pl.BlockSpec((1, 8, width), lambda s, c: (s, 0, 0)),
            pl.BlockSpec((1, rows, LANES), row),
            pl.BlockSpec((1, rows, depth), row),
            pl.BlockSpec(taps.shape, whole),
        ],
        out_specs=[
            pl.BlockSpec((1, rows, width + LANES), row),
            pl.BlockSpec((depth, width + LANES), whole),
        ],
        out_shape=[
            jax.ShapeDtypeStruct((seqs, length, width + LANES), BF16),
            jax.ShapeDtypeStruct((depth, width + LANES), F32),
        ],
        scratch_shapes=[pltpu.VMEM((width // LANES, rows + 8, LANES), F32)],
        compiler_params=pltpu.CompilerParams(vmem_limit_bytes=VMEM_LIMIT),
        cost_estimate=cost(seqs * length, 9),
        name="taps_backward",
    )(gconv, gconv, after, gdt, normed, taps)


def input_kernel(dz_ref, gx_ref, wz_ref, wx_ref, u_ref, c_ref, gain_ref, out_ref, sum_ref):
    @pl.when(jnp.logical_and(pl.program_id(0) == 0, pl.program_id(1) == 0))
    def _():
        sum_ref[...] = jnp.zeros_like(sum_ref)

    grad = nt(dz_ref[0], wz_ref[...]) + nt(gx_ref[0], wx_ref[...])
    u = u_ref[0].astype(F32)
    scale = lax.rsqrt(jnp.mean(u * u, axis=1, keepdims=True) + EPS)
    us = u * scale
    sum_ref[0:1, :] += jnp.sum(grad * us, axis=0, keepdims=True)
    h = grad * gain_ref[0:1, :]
    back = scale * (h - us * jnp.mean(h * us, axis=1, keepdims=True))
    out_ref[0] = c_ref[0].astype(F32) + back


def input_call(dz, gx, w_z, w_x, u, cot, gain, rows):
    seqs, length, depth = u.shape
    whole = lambda s, c: (0, 0)
    row = lambda s, c: (s, c, 0)
    return pl.pallas_call(
        input_kernel,
        grid=(seqs, length // rows),
        in_specs=[
            pl.BlockSpec((1, rows, dz.shape[2]), row),
            pl.BlockSpec((1, rows, gx.shape[2]), row),
            pl.BlockSpec(w_z.shape, whole),
            pl.BlockSpec(w_x.shape, whole),
            pl.BlockSpec((1, rows, depth), row),
            pl.BlockSpec((1, rows, depth), row),
            pl.BlockSpec(gain.shape, whole),
        ],
        out_specs=[pl.BlockSpec((1, rows, depth), row), pl.BlockSpec((8, depth), whole)],
        out_shape=[
            jax.ShapeDtypeStruct((seqs, length, depth), F32),
            jax.ShapeDtypeStruct((8, depth), F32),
        ],
        compiler_params=pltpu.CompilerParams(vmem_limit_bytes=VMEM_LIMIT),
        cost_estimate=cost(seqs * length, 9),
        name="input_gradient",
    )(dz, gx, w_z, w_x, u, cot, gain)


def to_all(value, size, axes):
    copies = jnp.broadcast_to(value[None], (size,) + value.shape)
    return lax.all_to_all(copies, axes, split_axis=0, concat_axis=0, tiled=True)


def other_core(value, sizes):
    return lax.ppermute(value, "dp", [(i, i ^ 1) for i in range(sizes["dp"])])


def both_cores(value, sizes, axis):
    other = other_core(value, sizes)
    first = lax.axis_index("dp") % 2 == 0
    return jnp.where(first, jnp.stack([value, other], axis), jnp.stack([other, value], axis))


def core_half(shard):
    half = shard.shape[0] // 2
    return lax.dynamic_slice_in_dim(shard, (lax.axis_index("dp") % 2) * half, half, 0)


def gather_rows(shard, sizes):
    got = to_all(core_half(shard), sizes["seq"], "seq").reshape(sizes["seq"], -1, shard.shape[1])
    return both_cores(got, sizes, 1).reshape(sizes["seq"] * shard.shape[0], shard.shape[1])


def gather_later(shards, sizes):
    columns = max(shard.shape[1] for shard in shards)
    halves = [core_half(shard).reshape(-1, columns) for shard in shards]
    got = lax.all_gather(jnp.concatenate(halves, axis=0), "seq", axis=0)
    other = other_core(got, sizes)
    first = lax.axis_index("dp") % 2 == 0
    outs, at = [], 0
    for shard, half in zip(shards, halves):
        rows = slice(at, at + half.shape[0])
        at += half.shape[0]
        mine, away = got[:, rows], other[:, rows]
        pair = jnp.where(first, jnp.stack([mine, away], 1), jnp.stack([away, mine], 1))
        outs.append(pair.reshape(sizes["seq"] * shard.shape[0], shard.shape[1]))
    return outs


def scatter_rows(grads, sizes):
    size = sizes["seq"]
    core = lax.axis_index("dp") % 2
    columns = max(grad.shape[1] for grad in grads)
    halves = []
    for grad in grads:
        parts = grad.reshape(size, 2, -1, grad.shape[1])
        mine = lax.dynamic_index_in_dim(parts, core, 1, keepdims=False)
        away = lax.dynamic_index_in_dim(parts, 1 - core, 1, keepdims=False).astype(BF16)
        half = (mine + other_core(away, sizes).astype(F32)).astype(BF16)
        halves.append(half.reshape(size, -1, columns))
    return lax.all_to_all(
        jnp.concatenate(halves, axis=1), "seq", split_axis=0, concat_axis=0, tiled=True
    )


def add_up(got, sizes):
    total = got.astype(F32).sum(axis=0)
    step = 2
    while step < sizes["dp"]:
        sent = total.astype(BF16)
        away = lax.ppermute(sent, "dp", [(i, i ^ step) for i in range(sizes["dp"])])
        total = sent.astype(F32) + away.astype(F32)
        step *= 2
    return total


def swap_rows(total, shapes, sizes):
    pair = both_cores(total, sizes, 0)
    outs, at = [], 0
    for rows, columns in shapes:
        count = rows * columns // (2 * sizes["seq"] * total.shape[1])
        outs.append(pair[:, at : at + count].reshape(rows // sizes["seq"], columns))
        at += count
    return outs


def sum_small(values, sizes, beside):
    flat = jnp.concatenate([value.reshape(-1) for value in values])
    count = flat.shape[0]
    flat = jnp.pad(flat, (0, -count % 1024)).reshape(-1, LANES)
    step = 1
    while step < sizes["dp"]:
        flat = flat + lax.ppermute(flat, "dp", [(i, i ^ step) for i in range(sizes["dp"])])
        step *= 2
    flat, beside = lax.optimization_barrier((to_all(flat, sizes["seq"], "seq"), beside))
    flat = flat.reshape(sizes["seq"], -1).sum(axis=0)
    out, at = [], 0
    for value in values:
        out.append(flat[at : at + value.size].reshape(value.shape))
        at += value.size
    return out, beside


def shift_in(value, size, step):
    pairs = [(i, i + step) for i in range(size) if 0 <= i + step < size]
    return lax.ppermute(value, "seq", pairs)


def prefix_kernel(step, got_ref, decay_ref, out_ref):
    size = got_ref.shape[1]
    held = jnp.zeros(got_ref.shape[2:], F32)
    for i in range(size) if step > 0 else range(size - 1, -1, -1):
        out_ref[0, i] = held.astype(BF16)
        held = held * decay_ref[0, i : i + 1, :] + got_ref[0, i].astype(F32)


def prefix_call(got, decay, step):
    seqs, size, piece, inner = got.shape
    block = pl.BlockSpec((1, size, piece, inner), lambda s: (s, 0, 0, 0))
    return pl.pallas_call(
        functools.partial(prefix_kernel, step),
        grid=(seqs,),
        in_specs=[block, pl.BlockSpec((1, size, inner), lambda s: (s, 0, 0))],
        out_specs=block,
        out_shape=jax.ShapeDtypeStruct(got.shape, BF16),
        compiler_params=pltpu.CompilerParams(vmem_limit_bytes=VMEM_LIMIT),
        name="state_prefix",
    )(got, decay)


def carry_over(states, decay, size, step, beside):
    seqs, depth, inner = states.shape
    piece = depth // size
    sent = states.astype(BF16).reshape(seqs, size, piece, inner)
    got = lax.all_to_all(sent, "seq", split_axis=1, concat_axis=1, tiled=True)
    got, beside = lax.optimization_barrier((got, beside))
    back = prefix_call(got, jnp.swapaxes(decay, 0, 1), step)
    back = lax.all_to_all(back, "seq", split_axis=1, concat_axis=1, tiled=True)
    return back.reshape(seqs, depth, inner), beside


def rms_gain(values, gain):
    return values * lax.rsqrt(jnp.mean(values * values, axis=-1, keepdims=True) + EPS) * gain


def body(
    sizes, inputs, w_in, w_out, norm_gain, conv_weight, conv_bias, dt_bias, a_log, skip, gate_gain,
    cotangent,
):
    size = sizes["seq"]
    seqs, length, depth = inputs.shape
    inner = gate_gain.shape[0]
    width = conv_weight.shape[1]
    tokens = seqs * length
    rows = min(256, length)

    w_x = gather_rows(jnp.pad(w_in[:, inner:], ((0, 0), (0, LANES - HEADS))), sizes)
    w_z, full_out = gather_later([w_in[:, :inner], w_out], sizes)

    def pad_heads(values):
        return jnp.pad(values, (0, LANES - HEADS))

    rates = -jnp.exp(a_log)
    heads = jnp.stack([pad_heads(dt_bias), pad_heads(rates), pad_heads(skip), pad_heads(jnp.ones_like(skip))])
    heads = jnp.pad(heads, ((0, 4), (0, 0)))
    taps = jnp.pad(conv_weight, ((0, 4), (0, 0)))
    bias = jnp.pad(conv_bias[None, :], ((0, 7), (0, 0)))
    vecs = jnp.pad(jnp.stack([gate_gain, jnp.repeat(skip, HEADDIM)]), ((0, 6), (0, 0)))
    ex, red = head_matrices(inner)

    edge = shift_in(inputs[:, length - 16 :], size, 1).astype(F32)
    edge = rms_gain(edge, norm_gain).astype(BF16).reshape(seqs * 16, depth)
    normed = rms_gain(inputs.astype(F32), norm_gain).astype(BF16)
    flat = normed.reshape(tokens, depth)

    def project(left, matrix):
        return jnp.dot(left, matrix, preferred_element_type=F32).astype(BF16)

    halo = project(edge, w_x)[:, :width].reshape(seqs, 16, width)
    xbc = project(flat, w_x[:, :width]).reshape(seqs, length, width)
    raw = project(flat, w_x[:, width:]).reshape(seqs, length, LANES)

    total = (softplus(raw.astype(F32) + heads[0]) * heads[3]).sum(axis=1) * heads[1]
    decay = jnp.exp(to_all(total, size, "seq").reshape(size, seqs, LANES)[:, :, :HEADS])
    decay = jnp.repeat(decay, HEADDIM, axis=2)
    act, y, dts, cum, dev, states, final = scan_call(xbc, halo, raw, taps, bias, heads, ex, inner)
    final, decay = lax.optimization_barrier((final, decay))
    z = project(flat, w_z).reshape(seqs, length, inner)
    s_in, z = carry_over(final, decay, size, 1, z)

    mixed, dy, dz, normalized, row_sums, q2, gate_sums, ds_loc = gate_call(
        y, act, z, dev, s_in, inputs, cotangent, full_out, vecs, ex, red, rows
    )
    grad_out, grad_z = weights_call(normalized, cotangent, normed, dz, min(512, length))
    ds_end, weight_grads = carry_over(ds_loc, decay, size, -1, (grad_out, grad_z))
    got_zo = scatter_rows(weight_grads, sizes)

    grad, direct, da = back_call(act, dy, dts, cum, dev, states, s_in, row_sums, vecs, ex, red)

    both = (s_in.astype(F32) * ds_end.astype(F32)).sum(axis=1).reshape(seqs, HEADS, HEADDIM).sum(axis=2)
    both = jnp.pad(both, ((0, 0), (0, LANES - HEADS))) * jnp.exp(total)
    c4 = jnp.broadcast_to((both + q2.sum(axis=1))[:, None, :], (seqs, 8, LANES))
    tot = jnp.broadcast_to(total[:, None, :], (seqs, 8, LANES))
    gconv, gdt, taps_sum, heads_sum = finish_call(
        grad, act, xbc, halo, raw, dts, dev, tot, ds_end, q2, direct, da, c4, taps, bias, heads, ex,
        red, rows,
    )
    after = shift_in(gconv[:, :8], size, -1)
    gx, grad_x = taps_back_call(gconv, after, gdt, normed, taps, rows)
    gx, grad_x, got_zo = lax.optimization_barrier((gx, grad_x, got_zo))
    got_x = scatter_rows([grad_x], sizes)
    total_zo = add_up(got_zo, sizes)
    gain = jnp.pad(norm_gain[None, :], ((0, 7), (0, 0)))
    grad_inputs, gain_sum = input_call(dz, gx, w_z, w_x, inputs, cotangent, gain, rows)
    got_x, gain_sum, total_zo = lax.optimization_barrier((got_x, gain_sum, total_zo))
    rows_out, rows_z = swap_rows(total_zo, [grad_out.shape, grad_z.shape], sizes)
    total_x = add_up(got_x, sizes)
    sums, total_x = sum_small(
        (
            gain_sum[0],
            taps_sum[:4],
            taps_sum[4],
            heads_sum[0, :HEADS],
            heads_sum[1, :HEADS],
            gate_sums[1].reshape(HEADS, HEADDIM).sum(axis=1),
            gate_sums[0],
        ),
        sizes,
        total_x,
    )
    (rows_x,) = swap_rows(total_x, [grad_x.shape], sizes)

    rows_in = jnp.concatenate([rows_z, rows_x[:, : width + HEADS]], axis=1)
    return (mixed, grad_inputs, rows_in, rows_out, *sums)


def solution(mesh):
    placed = (
        P("dp", "seq", None),
        P("seq", None),
        P("seq", None),
        P(),
        P(),
        P(),
        P(),
        P(),
        P(),
        P(),
        P("dp", "seq", None),
    )
    return jax.shard_map(
        functools.partial(body, dict(mesh.shape)),
        mesh=mesh,
        in_specs=placed,
        out_specs=(
            P("dp", "seq", None),
            P("dp", "seq", None),
            P("seq", None),
            P("seq", None),
            P(),
            P(),
            P(),
            P(),
            P(),
            P(),
            P(),
        ),
        check_vma=False,
    )
```
